256 devices in a mesh: groups: 64 (over z, y, core), rays: 4 (over x).
Axes of the slice: x: 4, y: 4, z: 8, core: 2. Of those that a mesh axis runs over, the one named last changes fastest.
Arguments:
- excitation: bfloat16 [3, 64, 32768], P(None, None, ('groups', 'rays')), may hold values from -6 to 6
- cycle: bfloat16 [8, 64, 32768], P(None, None, ('groups', 'rays')), may hold values from -6 to 6
- near_blocks: bfloat16 [64, 5, 8, 512, 512], P('groups', None, None, 'rays'), may hold values from -0.0390625 to 0.0390625
- near_list: int32 [64, 5], P('groups'), may hold values from 0 to 4, as said below
- near_count: int32 [64], P('groups'), may hold values from 1 to 5, as said below
- newest: int32 [8], replicated, may hold values from 0 to 7, each once
- inverse: bfloat16 [512, 32768], P(None, ('groups', 'rays')), may hold values from -0.25 to 0.25
- radiate: bfloat16 [1024, 32768], P(None, ('groups', 'rays')), may hold values from -0.25 to 0.25
- translate: float32 [64, 64, 1024], P('groups', None, 'rays'), may hold values from -0.75 to 0.75
- receive: bfloat16 [1024, 32768], P('rays', 'groups'), may hold values from -0.1875 to 0.1875
Outputs:
- currents: bfloat16 [3, 64, 32768], P(None, None, ('groups', 'rays'))
The draws below stay inside these ranges and needn't reach their ends.
Inputs may be any that keep to these rules, and one draw needn't show every extreme that they name: `near_list`: each row holds every number 0 to 4 once; its first near_count entries name the near groups, always include 2 (the group itself) and never a group outside the range. `near_count`: some group lists all 5 entries. `newest`: holds each slot once.
All inputs are finite; a program needn't handle non-finite values.
Results may differ from the reference program's by a relative error of at most 0.018.
Values may be sent and summed in bfloat16 or wider, within the bound.
A program may use at most 64 MiB of HBM per device.

```python
import jax
import jax.numpy as jnp
from jax import lax

GROUP_SIZE = 512
WAVES = 64
RAYS = 1024
SLOTS = 8
REACH = 2
STEPS = 3
MAX_NEAR = 5
GROUP_COUNT = 64
UNKNOWNS = 32768


def near_choice(key):
    flips = jax.random.randint(key, (GROUP_COUNT, 2 * REACH + 1), 0, 2)
    offsets = jnp.arange(2 * REACH + 1, dtype=jnp.int32) - REACH
    places = jnp.arange(GROUP_COUNT, dtype=jnp.int32)[:, None] + offsets[None, :]
    inside = (places >= 0) & (places < GROUP_COUNT)
    filled = jnp.arange(GROUP_COUNT, dtype=jnp.int32)[:, None] == GROUP_COUNT // 2
    chosen = ((flips == 1) | (offsets[None, :] == 0) | filled) & inside
    return chosen.astype(jnp.int32)


def draw_near_list(key, part):
    chosen = near_choice(key)
    scores = (1 - chosen) * (4 * REACH + 4) + jnp.arange(2 * REACH + 1, dtype=jnp.int32)[None, :]
    return jnp.argsort(scores, axis=1).astype(jnp.int32)


def draw_near_count(key, part):
    chosen = near_choice(key)
    return jnp.sum(chosen, axis=1).astype(jnp.int32)


def steps_of(rng, shape, cuts, low, top_value):
    gain, own = 1.0, jax.random.fold_in(rng, 6)
    for position, blocks in cuts:
        draws = jnp.exp(jax.random.uniform(jax.random.fold_in(own, position), (blocks,), jnp.float32, low / len(cuts), top_value / len(cuts)))
        gain = gain * jnp.repeat(draws, shape[position] // blocks).reshape([-1 if axis == position else 1 for axis in range(len(shape))])
    return gain


def noise(key, dims, deviation, limit, split=(), kind=jnp.bfloat16):
    result = deviation * jax.random.normal(key, dims, jnp.float32)
    if split:
        result = result * steps_of(key, dims, split, -0.22, 0.18)
    return jnp.clip(result, -limit, limit).astype(kind)


def setup_inputs(seed: int = 0) -> dict:
    seeds = jax.random.split(jax.random.key(seed), 11)
    excitation = noise(seeds[0], (STEPS, WAVES, UNKNOWNS), 1.0, 6.0, ((2, 256),))
    cycle = noise(seeds[1], (SLOTS, WAVES, UNKNOWNS), 1.0, 6.0, ((2, 256),))
    near_blocks = noise(seeds[2], (GROUP_COUNT, MAX_NEAR, SLOTS, GROUP_SIZE, GROUP_SIZE), (MAX_NEAR * SLOTS * GROUP_SIZE) ** -0.5, 0.0390625, ((0, 64), (3, 4)))
    near_list = draw_near_list(jax.random.fold_in(seeds[10], 71), 0)
    near_count = draw_near_count(jax.random.fold_in(seeds[10], 71), 0)
    newest = jax.random.permutation(seeds[5], SLOTS).astype(jnp.int32)
    inverse = noise(seeds[6], (GROUP_SIZE, UNKNOWNS), GROUP_SIZE ** -0.5, 0.25, ((1, 256),))
    radiate = noise(seeds[7], (RAYS, UNKNOWNS), GROUP_SIZE ** -0.5, 0.25, ((1, 256),))
    translate = noise(seeds[8], (GROUP_COUNT, GROUP_COUNT, RAYS), GROUP_COUNT ** -0.5, 0.75, ((0, 64), (2, 4)), jnp.float32)
    receive = noise(seeds[9], (RAYS, UNKNOWNS), RAYS ** -0.5, 0.1875, ((0, 4), (1, 64)))
    return {"excitation": excitation, "cycle": cycle, "near_blocks": near_blocks, "near_list": near_list, "near_count": near_count, "newest": newest, "inverse": inverse, "radiate": radiate, "translate": translate, "receive": receive}


def reference(excitation, cycle, near_blocks, near_list, near_count, newest, inverse, radiate, translate, receive):
    every = jnp.arange(GROUP_COUNT, dtype=jnp.int32)
    entries = jnp.arange(MAX_NEAR, dtype=jnp.int32)
    sources = every[:, None] + near_list - REACH
    valid = (entries[None, :] < near_count[:, None]) & (sources >= 0) & (sources < GROUP_COUNT)
    marked = jnp.any(valid[:, :, None] & (sources[:, :, None] == every[None, None, :]), axis=1)
    weights = translate * jnp.where(marked, 0.0, 1.0).astype(jnp.float32)[:, :, None]
    radiate_groups = radiate.reshape(RAYS, GROUP_COUNT, GROUP_SIZE).transpose(1, 0, 2)
    history = cycle
    outputs = []
    for step in range(STEPS):
        slot_now = (newest[0] + step) % SLOTS
        lag_slots = ((slot_now - jnp.arange(SLOTS, dtype=jnp.int32)) % SLOTS).astype(jnp.int32)
        lagged = history[lag_slots]
        latest = lagged[0].reshape(WAVES, GROUP_COUNT, GROUP_SIZE).transpose(1, 0, 2)

        def make_slab(pair):
            return jnp.dot(pair[0], pair[1].T, preferred_element_type=jnp.float32).astype(jnp.bfloat16)

        slabs = lax.map(make_slab, (latest, radiate_groups)).astype(jnp.float32)

        def one_group(group):
            start = (group * GROUP_SIZE).astype(jnp.int32)
            field = jnp.einsum("hr,hwr->wr", weights[group], slabs, precision=lax.Precision.HIGHEST).astype(jnp.bfloat16)
            recv = lax.dynamic_slice_in_dim(receive, start, GROUP_SIZE, 1)
            far = jnp.dot(field, recv, preferred_element_type=jnp.float32)
            near = jnp.zeros((WAVES, GROUP_SIZE), jnp.float32)
            for entry in range(MAX_NEAR):
                source = jnp.clip(sources[group, entry], 0, GROUP_COUNT - 1).astype(jnp.int32)
                picked = lax.dynamic_slice_in_dim(lagged, (source * GROUP_SIZE).astype(jnp.int32), GROUP_SIZE, 2)
                picked = jnp.where(valid[group, entry], picked, jnp.zeros_like(picked))
                rows = picked.transpose(1, 0, 2).reshape(WAVES, SLOTS * GROUP_SIZE)
                block = near_blocks[group, entry].reshape(SLOTS * GROUP_SIZE, GROUP_SIZE)
                near = near + jnp.dot(rows, block, preferred_element_type=jnp.float32)
            incident = lax.dynamic_slice_in_dim(excitation[step], start, GROUP_SIZE, 1).astype(jnp.float32)
            drive = (incident - near - far).astype(jnp.bfloat16)
            solve = lax.dynamic_slice_in_dim(inverse, start, GROUP_SIZE, 1)
            return jnp.dot(drive, solve, preferred_element_type=jnp.float32).astype(jnp.bfloat16)

        blocks = lax.map(one_group, every)
        current = blocks.transpose(1, 0, 2).reshape(WAVES, UNKNOWNS)
        history = lax.dynamic_update_index_in_dim(history, current, ((slot_now + 1) % SLOTS).astype(jnp.int32), 0)
        outputs.append(current)
    return jnp.stack(outputs)
```

```python
import functools

import jax
import jax.numpy as jnp
from jax import lax
from jax.experimental import pallas as pl
from jax.experimental.pallas import tpu as pltpu
from jax.sharding import PartitionSpec as P

REACH = 2
NEAR_SHIFTS = (-2, -1, 1, 2)
MESH = pl.DeviceIdType.MESH
F32 = jnp.float32
BF16 = jnp.bfloat16


def kernel(
    n,
    inner,
    copies_of_fold,
    m,
    exc_hbm,
    cyc_hbm,
    blocks_hbm,
    list_hbm,
    count_hbm,
    newest_hbm,
    inv_hbm,
    rad_hbm,
    tr_hbm,
    rec_hbm,
    out_ref,
    list_ref,
    count_ref,
    newest_ref,
    exc,
    cyc,
    blocks,
    tr,
    rad,
    inv,
    rs_send,
    rs_recv,
    rad_full,
    inv_full,
    slab_of_drive,
    rec_full,
    nearby,
    fresh_first,
    fresh_second,
    w_send,
    w_recv,
    w_both,
    turn_s,
    turn_f,
    s_send,
    s_recv,
    f_send,
    f_recv,
    base,
    p_send,
    p_recv,
    own,
    row_sem,
    load_sems,
    x_send,
    x_recv,
    w_sems,
    s_sems,
    f_sems,
    near_send,
    near_recv,
    p_sems,
):
    steps, waves, width = exc.shape
    slots = cyc.shape[0]
    entries = list_ref.shape[1]
    size = m * width
    rays = tr.shape[1]
    outer = n // inner
    chunks = n // copies_of_fold
    rows = rays // (2 * chunks)
    g = lax.axis_index("groups")
    r = lax.axis_index("rays")
    go = g // inner
    gi = g - go * inner
    pair = go // 2
    plane = go - 2 * pair
    chunk = plane * inner + gi
    first_target = g - chunk
    mine = pl.ds(pl.multiple_of(r * width, width), width)
    dims = (((1,), (1,)), ((), ()))
    fresh_of = (fresh_first, fresh_second)
    ray_order = sorted(range(1, m), key=lambda d: -min(d, m - d))
    inner_order = sorted(range(inner), key=lambda d: -min(d, inner - d))

    def wrap(x, limit):
        return jnp.where(x >= limit, x - limit, x)

    inner_place = [wrap(gi + d, inner) for d in range(inner)]
    ray_place = [wrap(r + d, m) for d in range(m)]

    def near_group(d):
        return wrap(g + d + n, n) if d < 0 else wrap(g + d, n)

    def other_ray(d):
        return ray_place[d]

    def remote(src, dst, send_sem, recv_sem, group, ray):
        return pltpu.make_async_remote_copy(
            src_ref=src,
            dst_ref=dst,
            send_sem=send_sem,
            recv_sem=recv_sem,
            device_id=(group, ray),
            device_id_type=MESH,
        )

    def each_peer(act):
        def body(k, carry):
            shift, change = carry
            place = wrap(go + shift, outer)
            other = place * inner
            bit = place - 2 * (place // 2)
            for d in inner_order:
                act(other + inner_place[d], bit * inner + inner_place[d])
            return shift + change, jnp.where(change < 0, 1 - change, -1 - change)

        lax.fori_loop(0, outer - 1, body, (jnp.int32(outer // 2), jnp.int32(-1)))
        for d in inner_order:
            if d:
                act(go * inner + inner_place[d], plane * inner + inner_place[d])

    def each_target(act, with_self):
        for d in inner_order:
            act((1 - plane) * inner + inner_place[d])
        for d in inner_order:
            if d or with_self:
                act(plane * inner + inner_place[d])

    def wait_blocks(like, sem, count=None):
        part = like.at[pl.ds(0, like.shape[0] - 1 if count is None else count)]
        pltpu.make_async_copy(part, part, sem).wait()

    def near_copies(src, dst, index):
        return [
            remote(
                src,
                dst.at[REACH - shift],
                near_send.at[index, k],
                near_recv.at[index, k],
                near_group(shift),
                r,
            )
            for k, shift in enumerate(NEAR_SHIFTS)
        ]

    def ray_copies(src_of, dst, index):
        return [
            remote(
                src_of(d), dst, x_send.at[index, d - 1], x_recv.at[index, d - 1], g, other_ray(d)
            )
            for d in ray_order
        ]

    barrier = pltpu.get_barrier_semaphore()
    greeted = [(g, other_ray(d)) for d in ray_order]
    greeted += [(go * inner + inner_place[d], r) for d in inner_order if d]
    row_peers = [(wrap(go + d, outer) * inner + gi, r) for d in range(1, outer)]
    greeted += row_peers
    greeted += [(near_group(d), r) for d in NEAR_SHIFTS]
    for device in greeted:
        pl.semaphore_signal(barrier, inc=1, device_id=device, device_id_type=MESH)

    rows_here = pl.ds(pl.multiple_of(r * rays, rays), rays)
    pairs = (
        (newest_hbm, newest_ref),
        (cyc_hbm, cyc),
        (rad_hbm, rad),
        (list_hbm, list_ref),
        (count_hbm, count_ref),
        (tr_hbm.at[0], tr),
        (rad_hbm.at[rows_here, :], rad_full.at[:, mine]),
        (blocks_hbm.at[0], blocks),
        (inv_hbm, inv_full.at[:, mine]),
        (inv_hbm, inv),
        (cyc_hbm, nearby.at[REACH]),
        (rec_hbm, rec_full.at[rows_here, :]),
        (exc_hbm, exc),
    )
    loads = [
        pltpu.make_async_copy(src, dst, load_sems.at[i]) for i, (src, dst) in enumerate(pairs)
    ]
    for load in loads:
        load.start()
    (
        load_newest,
        load_cyc,
        load_all_rad,
        load_list,
        load_count,
        load_tr,
        load_rad,
        load_blocks,
        load_inv,
        load_own_inv,
        load_self,
        load_rec,
        load_exc,
    ) = loads

    pl.semaphore_wait(barrier, len(greeted))

    for device in row_peers:
        pl.semaphore_signal(row_sem, inc=1, device_id=device, device_id_type=MESH)
    load_newest.wait()
    load_cyc.wait()
    start_slot = newest_ref[0]
    newest_value = cyc[start_slot]
    load_all_rad.wait()
    partial_slab = lax.dot_general(rad[...], newest_value, dims, preferred_element_type=F32)
    for k in range(m):
        top, middle = k * rays, k * rays + rays // 2
        rs_send[k] = jnp.concatenate(
            [partial_slab[top:middle], partial_slab[middle : top + rays]], axis=1
        ).astype(BF16)
    slab_copies = ray_copies(lambda d: rs_send.at[other_ray(d)], rs_recv.at[r], 0)
    for copy in slab_copies:
        copy.start()
    rs_recv[r] = rs_send[r]
    cycle_copies = near_copies(cyc_hbm, nearby, 0)
    for copy in cycle_copies:
        copy.start()
    near_all = list(cycle_copies)

    load_list.wait()
    load_count.wait()
    near_shift = []
    near_valid = []
    for b in range(entries):
        shift = list_ref[0, b]
        source = g + shift - REACH
        near_shift.append(shift)
        near_valid.append((b < count_ref[0]) & (source >= 0) & (source < n))
    load_tr.wait()
    every = lax.broadcasted_iota(jnp.int32, (n, rays), 0)
    weights = tr[...]
    for b in range(entries):
        hit = near_valid[b] & (every == g + near_shift[b] - REACH)
        weights = jnp.where(hit, 0.0, weights)
    turned = weights.T
    w_rows = jnp.concatenate([turned[: rays // 2], turned[rays // 2 :]], axis=1)
    w_send[...] = w_rows.reshape(w_send.shape)

    pl.semaphore_wait(row_sem, len(row_peers))

    def send_weights(k):
        remote(
            w_send.at[k], w_recv.at[chunk], w_sems.at[0], w_sems.at[1], first_target + k, r
        ).start()

    each_target(send_weights, False)
    w_recv[chunk] = w_send[chunk]
    rad_copies = ray_copies(
        lambda d: rad_hbm.at[pl.ds(pl.multiple_of(other_ray(d) * rays, rays), rays), :],
        rad_full.at[:, mine],
        1,
    )
    inv_copies = ray_copies(lambda d: inv_hbm, inv_full.at[:, mine], 2)
    for copy in rad_copies + inv_copies:
        copy.start()
    rec_copies = ray_copies(lambda d: rec_hbm, rec_full.at[rows_here, :], 3)
    p_copies = []

    def send_slab(step, wide):
        for k in range(chunks):
            s_send[step, k] = wide[k * rows : (k + 1) * rows].astype(BF16)

        def send(group, k):
            remote(
                s_send.at[step, k],
                s_recv.at[step, g],
                s_sems.at[step, 0],
                s_sems.at[step, 1],
                group,
                r,
            ).start()

        each_peer(send)
        s_recv[step, g] = s_send[step, chunk]

    def fold(step):
        wait_blocks(s_recv.at[step], s_sems.at[step, 1])
        for h in range(n):
            turn_s[h * rows : (h + 1) * rows] = s_recv[step, h].astype(F32)
        lane = lax.broadcasted_iota(jnp.int32, (n, 2 * waves), 1)
        for i in range(rows):
            slab = turn_s[pl.ds(i, n, stride=rows), :]
            wide = jnp.concatenate(
                [jnp.where(lane < waves, slab, 0.0), jnp.where(lane < waves, 0.0, slab)], axis=0
            ).astype(BF16)
            both = jnp.dot(w_both[i], wide, preferred_element_type=F32)
            turn_f[i * chunks : (i + 1) * chunks] = both[:chunks] + both[chunks:]
        for k in range(chunks):
            f_send[step, k] = turn_f[pl.ds(k, rows, stride=chunks), :].astype(BF16)
        place = r * chunks + chunk

        def send(k, ray):
            remote(
                f_send.at[step, k],
                f_recv.at[step, place],
                f_sems.at[step, 0],
                f_sems.at[step, 1],
                first_target + k,
                ray,
            ).start()

        if step:
            for d in ray_order:
                each_target(lambda k, ray=other_ray(d): send(k, ray), True)
        each_target(lambda k: send(k, r), False)
        f_recv[step, place] = f_send[step, chunk]

    def send_partial(step, part):
        p_send[step] = part
        copies = [
            remote(
                p_send.at[step],
                p_recv.at[step, r],
                p_sems.at[step, 0, d - 1],
                p_sems.at[step, 1, d - 1],
                g,
                other_ray(d),
            )
            for d in ray_order
        ]
        for copy in copies:
            copy.start()
        p_copies.append(copies)
        p_recv[step, r] = part

    for copy in slab_copies:
        copy.wait_recv()
    first_slab = rs_recv[0].astype(F32)
    for k in range(1, m):
        first_slab = first_slab + rs_recv[k].astype(F32)
    send_slab(0, first_slab)

    load_self.wait()
    load_blocks.wait()
    load_exc.wait()
    for copy in cycle_copies:
        copy.wait_recv()
    base[...] = jnp.zeros_like(base)
    for step in range(steps):
        base[step, :, mine] = exc[step].astype(F32)

    def add_cycle(b, carry):
        shift = list_ref[0, b]
        source = g + shift - REACH
        valid = (b < count_ref[0]) & (source >= 0) & (source < n)
        past = [nearby[shift, lax.rem(start_slot - i + slots, slots)] for i in range(slots)]
        past = [jnp.where(valid, x, jnp.zeros_like(x)) for x in past]
        blank = jnp.zeros_like(past[0])
        lagged = jnp.concatenate(
            [
                jnp.concatenate([blank] * step + past[: slots - step], axis=1)
                for step in range(steps)
            ],
            axis=0,
        )
        near = jnp.dot(
            lagged, blocks[b].reshape(slots * width, size), preferred_element_type=F32
        )
        for step in range(steps):
            base[step] = base[step] - near[step * waves : (step + 1) * waves]
        return carry

    lax.fori_loop(0, entries, add_cycle, 0)

    wait_blocks(w_recv, w_sems.at[1])
    for i in range(rows):
        w_all = w_recv[:, i, :]
        w_high = w_all.astype(BF16)
        w_both[i, :chunks] = w_high
        w_both[i, chunks:] = (w_all - w_high.astype(F32)).astype(BF16)
    fold(0)

    load_rad.wait()
    load_inv.wait()
    load_own_inv.wait()
    for copy in rad_copies + inv_copies:
        copy.wait_recv()
    slab_of_drive[...] = lax.dot_general(
        rad_full[...], inv_full[...], dims, preferred_element_type=F32
    ).astype(BF16)

    def gathered_sum(step):
        for copy in p_copies[step]:
            copy.wait_recv()
        total = p_recv[step, 0].astype(F32)
        for d in range(1, m):
            total = total + p_recv[step, d].astype(F32)
        return total

    def turn_field(pieces):
        turned = jnp.concatenate([x.astype(F32) for x in pieces], axis=0).T.astype(BF16)
        span = rays // 2
        return jnp.concatenate(
            [
                turned[p * waves : (p + 1) * waves, k * span : (k + 1) * span]
                for k in range(len(pieces) // chunks)
                for p in range(2)
            ],
            axis=1,
        )

    for step in range(steps):
        if step == 0:
            load_rec.wait()
            wait_blocks(f_recv.at[0], f_sems.at[0, 1], chunks - 1)
            field = turn_field([f_recv[0, r * chunks + k] for k in range(chunks)])
            far = jnp.dot(field, rec_full[rows_here, :], preferred_element_type=F32)
            send_partial(0, (base[0] - far).astype(BF16))
            for copy in rec_copies:
                copy.start()
            drive = gathered_sum(0).astype(BF16)
        else:
            total = gathered_sum(step)
            if step == 1:
                for copy in rec_copies:
                    copy.wait_recv()
            wait_blocks(f_recv.at[step], f_sems.at[step, 1])
            field = turn_field([f_recv[step, k] for k in range(m * chunks)])
            far = jnp.dot(field, rec_full[...], preferred_element_type=F32)
            drive = (total - far).astype(BF16)
        if step + 1 < steps:
            slab = lax.dot_general(slab_of_drive[...], drive, dims, preferred_element_type=F32)
            send_slab(
                step + 1, jnp.concatenate([slab[: rays // 2], slab[rays // 2 :]], axis=1)
            )
        own[step] = jnp.dot(drive, inv[...], preferred_element_type=F32).astype(BF16)
        out_ref[step] = own[step]
        if step + 1 < steps:
            fresh = fresh_of[step]
            copies = near_copies(own.at[step], fresh, step + 1)
            for copy in copies:
                copy.start()
            near_all.extend(copies)
            fresh[REACH] = own[step]
            for copy in copies:
                copy.wait_recv()

            def add_near(later):
                latest = [fresh[near_shift[b]] for b in range(entries)]
                latest = [
                    jnp.where(near_valid[b], x, jnp.zeros_like(x)) for b, x in enumerate(latest)
                ]
                base[later] = base[later] - jnp.dot(
                    jnp.concatenate(latest, axis=1),
                    blocks[:, later - step - 1].reshape(entries * width, size),
                    preferred_element_type=F32,
                )

            add_near(step + 1)
            send_partial(step + 1, base[step + 1].astype(BF16))
            fold(step + 1)
            for later in range(step + 2, steps):
                add_near(later)

    for copy in slab_copies + rad_copies + inv_copies + rec_copies + near_all + sum(p_copies, []):
        copy.wait_send()
    wait_blocks(w_send, w_sems.at[0])
    for step in range(steps):
        wait_blocks(s_recv.at[step], s_sems.at[step, 0])
        wait_blocks(f_recv.at[step], f_sems.at[step, 0], None if step else chunks - 1)


def layout_of(n):
    inner = 1
    while inner * inner < n:
        inner *= 2
    return inner, max(n // (2 * inner), 1)


def solution(mesh):
    n = mesh.shape["groups"]
    m = mesh.shape["rays"]
    inner, copies_of_fold = layout_of(n)
    chunks = n // copies_of_fold

    def local(
        excitation,
        cycle,
        near_blocks,
        near_list,
        near_count,
        newest,
        inverse,
        radiate,
        translate,
        receive,
    ):
        steps, waves, width = excitation.shape
        slots = cycle.shape[0]
        entries = near_list.shape[1]
        size = m * width
        rays = receive.shape[0]
        rows = rays // (2 * chunks)
        spread = 2 * REACH + 1
        anywhere = pl.BlockSpec(memory_space=pl.ANY)
        dma = pltpu.SemaphoreType.DMA
        vmem = pltpu.VMEM
        smem = pltpu.SMEM
        return pl.pallas_call(
            functools.partial(kernel, n, inner, copies_of_fold, m),
            out_shape=jax.ShapeDtypeStruct(excitation.shape, BF16),
            in_specs=[anywhere] * 10,
            out_specs=pl.BlockSpec(memory_space=vmem),
            scratch_shapes=[
                smem(near_list.shape, jnp.int32),
                smem(near_count.shape, jnp.int32),
                smem(newest.shape, jnp.int32),
                vmem(excitation.shape, BF16),
                vmem(cycle.shape, BF16),
                vmem((entries, slots, width, size), BF16),
                vmem((n, rays), F32),
                vmem(radiate.shape, BF16),
                vmem(inverse.shape, BF16),
                vmem((m, rays // 2, 2 * waves), BF16),
                vmem((m, rays // 2, 2 * waves), BF16),
                vmem((rays, size), BF16),
                vmem((size, size), BF16),
                vmem((rays, size), BF16),
                vmem((m * rays, size), BF16),
                vmem((spread, slots, waves, width), BF16),
                vmem((spread, waves, width), BF16),
                vmem((spread, waves, width), BF16),
                vmem((chunks, rows, 2 * n), F32),
                vmem((chunks, rows, 2 * n), F32),
                vmem((rows, 2 * chunks, 2 * n), BF16),
                vmem((n * rows, 2 * waves), F32),
                vmem((chunks * rows, 2 * waves), F32),
                vmem((steps, chunks, rows, 2 * waves), BF16),
                vmem((steps, n, rows, 2 * waves), BF16),
                vmem((steps, chunks, rows, 2 * waves), BF16),
                vmem((steps, m * chunks, rows, 2 * waves), BF16),
                vmem((steps, waves, size), F32),
                vmem((steps, waves, size), BF16),
                vmem((steps, m, waves, size), BF16),
                vmem((steps, waves, width), BF16),
                pltpu.SemaphoreType.REGULAR,
                dma((13,)),
                dma((4, m - 1)),
                dma((4, m - 1)),
                dma((2,)),
                dma((steps, 2)),
                dma((steps, 2)),
                dma((steps, 4)),
                dma((steps, 4)),
                dma((steps, 2, m - 1)),
            ],
            compiler_params=pltpu.CompilerParams(
                collective_id=0, has_side_effects=True, vmem_limit_bytes=56 * 1024 * 1024
            ),
        )(
            excitation,
            cycle,
            near_blocks,
            near_list,
            near_count,
            newest,
            inverse,
            radiate,
            translate,
            receive,
        )

    placed = (
        P(None, None, ("groups", "rays")),
        P(None, None, ("groups", "rays")),
        P("groups", None, None, "rays", None),
        P("groups", None),
        P("groups"),
        P(),
        P(None, ("groups", "rays")),
        P(None, ("groups", "rays")),
        P("groups", None, "rays"),
        P("rays", "groups"),
    )
    return jax.shard_map(
        local,
        mesh=mesh,
        in_specs=placed,
        out_specs=P(None, None, ("groups", "rays")),
        check_vma=False,
    )
```

```python
import functools

import jax
import jax.numpy as jnp
from jax import lax
from jax.experimental import pallas as pl
from jax.experimental.pallas import tpu as pltpu
from jax.sharding import PartitionSpec as P

REACH = 2
NEAR_SHIFTS = (-2, -1, 1, 2)
MESH = pl.DeviceIdType.MESH
F32 = jnp.float32
BF16 = jnp.bfloat16


def kernel(
    n,
    inner,
    copies_of_fold,
    m,
    exc_hbm,
    cyc_hbm,
    blocks_hbm,
    list_hbm,
    count_hbm,
    newest_hbm,
    inv_hbm,
    rad_hbm,
    tr_hbm,
    rec_hbm,
    out_ref,
    list_ref,
    count_ref,
    newest_ref,
    exc,
    cyc,
    blocks,
    tr,
    rad,
    inv,
    rs_send,
    rs_recv,
    rad_full,
    inv_full,
    slab_of_drive,
    rec_full,
    nearby,
    fresh_first,
    fresh_second,
    w_send,
    w_recv,
    w_both,
    turn_s,
    turn_f,
    s_send,
    s_recv,
    f_send,
    f_recv,
    base,
    p_send,
    p_recv,
    own,
    row_sem,
    load_sems,
    x_send,
    x_recv,
    w_sems,
    s_sems,
    f_sems,
    near_send,
    near_recv,
    p_sems,
):
    steps, waves, width = exc.shape
    slots = cyc.shape[0]
    entries = list_ref.shape[1]
    size = m * width
    rays = tr.shape[1]
    outer = n // inner
    chunks = n // copies_of_fold
    rows = rays // (2 * chunks)
    g = lax.axis_index("groups")
    r = lax.axis_index("rays")
    go = g // inner
    gi = g - go * inner
    pair = go // 2
    plane = go - 2 * pair
    chunk = plane * inner + gi
    first_target = g - chunk
    mine = pl.ds(pl.multiple_of(r * width, width), width)
    dims = (((1,), (1,)), ((), ()))
    fresh_of = (fresh_first, fresh_second)
    ray_order = sorted(range(1, m), key=lambda d: -min(d, m - d))
    inner_order = sorted(range(inner), key=lambda d: -min(d, inner - d))

    def wrap(x, limit):
        return jnp.where(x >= limit, x - limit, x)

    inner_place = [wrap(gi + d, inner) for d in range(inner)]
    ray_place = [wrap(r + d, m) for d in range(m)]

    def near_group(d):
        return wrap(g + d + n, n) if d < 0 else wrap(g + d, n)

    def other_ray(d):
        return ray_place[d]

    def remote(src, dst, send_sem, recv_sem, group, ray):
        return pltpu.make_async_remote_copy(
            src_ref=src,
            dst_ref=dst,
            send_sem=send_sem,
            recv_sem=recv_sem,
            device_id=(group, ray),
            device_id_type=MESH,
        )

    def each_peer(act):
        def body(k, carry):
            shift, change = carry
            place = wrap(go + shift, outer)
            other = place * inner
            bit = place - 2 * (place // 2)
            for d in inner_order:
                act(other + inner_place[d], bit * inner + inner_place[d])
            return shift + change, jnp.where(change < 0, 1 - change, -1 - change)

        lax.fori_loop(0, outer - 1, body, (jnp.int32(outer // 2), jnp.int32(-1)))
        for d in inner_order:
            if d:
                act(go * inner + inner_place[d], plane * inner + inner_place[d])

    def each_target(act, with_self):
        for d in inner_order:
            act((1 - plane) * inner + inner_place[d])
        for d in inner_order:
            if d or with_self:
                act(plane * inner + inner_place[d])

    def wait_blocks(like, sem, count=None):
        part = like.at[pl.ds(0, like.shape[0] - 1 if count is None else count)]
        pltpu.make_async_copy(part, part, sem).wait()

    def near_copies(src, dst, index):
        return [
            remote(
                src,
                dst.at[REACH - shift],
                near_send.at[index, k],
                near_recv.at[index, k],
                near_group(shift),
                r,
            )
            for k, shift in enumerate(NEAR_SHIFTS)
        ]

    def ray_copies(src_of, dst, index):
        return [
            remote(
                src_of(d), dst, x_send.at[index, d - 1], x_recv.at[index, d - 1], g, other_ray(d)
            )
            for d in ray_order
        ]

    barrier = pltpu.get_barrier_semaphore()
    greeted = [(g, other_ray(d)) for d in ray_order]
    greeted += [(go * inner + inner_place[d], r) for d in inner_order if d]
    row_peers = [(wrap(go + d, outer) * inner + gi, r) for d in range(1, outer)]
    greeted += row_peers
    greeted += [(near_group(d), r) for d in NEAR_SHIFTS]
    for device in greeted:
        pl.semaphore_signal(barrier, inc=1, device_id=device, device_id_type=MESH)

    rows_here = pl.ds(pl.multiple_of(r * rays, rays), rays)
    pairs = (
        (newest_hbm, newest_ref),
        (cyc_hbm, cyc),
        (rad_hbm, rad),
        (list_hbm, list_ref),
        (count_hbm, count_ref),
        (tr_hbm.at[0], tr),
        (rad_hbm.at[rows_here, :], rad_full.at[:, mine]),
        (blocks_hbm.at[0], blocks),
        (inv_hbm, inv_full.at[:, mine]),
        (inv_hbm, inv),
        (cyc_hbm, nearby.at[REACH]),
        (rec_hbm, rec_full.at[rows_here, :]),
        (exc_hbm, exc),
    )
    loads = [
        pltpu.make_async_copy(src, dst, load_sems.at[i]) for i, (src, dst) in enumerate(pairs)
    ]
    for load in loads:
        load.start()
    (
        load_newest,
        load_cyc,
        load_all_rad,
        load_list,
        load_count,
        load_tr,
        load_rad,
        load_blocks,
        load_inv,
        load_own_inv,
        load_self,
        load_rec,
        load_exc,
    ) = loads

    pl.semaphore_wait(barrier, len(greeted))

    for device in row_peers:
        pl.semaphore_signal(row_sem, inc=1, device_id=device, device_id_type=MESH)
    load_newest.wait()
    load_cyc.wait()
    start_slot = newest_ref[0]
    newest_value = cyc[start_slot]
    load_all_rad.wait()
    partial_slab = lax.dot_general(rad[...], newest_value, dims, preferred_element_type=F32)
    for k in range(m):
        top, middle = k * rays, k * rays + rays // 2
        rs_send[k] = jnp.concatenate(
            [partial_slab[top:middle], partial_slab[middle : top + rays]], axis=1
        ).astype(BF16)
    slab_copies = ray_copies(lambda d: rs_send.at[other_ray(d)], rs_recv.at[r], 0)
    for copy in slab_copies:
        copy.start()
    rs_recv[r] = rs_send[r]
    cycle_copies = near_copies(cyc_hbm, nearby, 0)
    for copy in cycle_copies:
        copy.start()
    near_all = list(cycle_copies)

    load_list.wait()
    load_count.wait()
    near_shift = []
    near_valid = []
    for b in range(entries):
        shift = list_ref[0, b]
        source = g + shift - REACH
        near_shift.append(shift)
        near_valid.append((b < count_ref[0]) & (source >= 0) & (source < n))
    load_tr.wait()
    every = lax.broadcasted_iota(jnp.int32, (n, rays), 0)
    weights = tr[...]
    for b in range(entries):
        hit = near_valid[b] & (every == g + near_shift[b] - REACH)
        weights = jnp.where(hit, 0.0, weights)
    turned = weights.T
    w_rows = jnp.concatenate([turned[: rays // 2], turned[rays // 2 :]], axis=1)
    w_send[...] = w_rows.reshape(w_send.shape)

    pl.semaphore_wait(row_sem, len(row_peers))

    def send_weights(k):
        remote(
            w_send.at[k], w_recv.at[chunk], w_sems.at[0], w_sems.at[1], first_target + k, r
        ).start()

    each_target(send_weights, False)
    w_recv[chunk] = w_send[chunk]
    rad_copies = ray_copies(
        lambda d: rad_hbm.at[pl.ds(pl.multiple_of(other_ray(d) * rays, rays), rays), :],
        rad_full.at[:, mine],
        1,
    )
    for copy in rad_copies:
        copy.start()

    near_rays = sorted({1 % m, m - 1} - {0})

    def columns_of(ray):
        return pl.ds(pl.multiple_of(ray * width, width), width)

    def rows_of(ray, half):
        start = ray * rays + half * (rays // 2)
        return pl.ds(pl.multiple_of(start, rays // 2), rays // 2)

    def neighbour_copies(src, dst, index):
        return [
            remote(src, dst, x_send.at[index, d - 1], x_recv.at[index, d - 1], g, other_ray(d))
            for d in near_rays
        ]

    def pass_copies(part_of, index):
        if m != 4:
            return []
        return [
            remote(
                part_of(other_ray(m - d), k),
                part_of(other_ray(m - d), k),
                x_send.at[index, d - 1],
                x_recv.at[index, d - 1],
                g,
                other_ray(d),
            )
            for k, d in enumerate(near_rays)
        ]

    inv_copies = neighbour_copies(inv_hbm, inv_full.at[:, mine], 2)
    rec_copies = neighbour_copies(rec_hbm, rec_full.at[rows_here, :], 3)
    inv_passed = pass_copies(
        lambda ray, k: inv_full.at[pl.ds(k * (size // 2), size // 2), columns_of(ray)], 4
    )
    rec_passed = pass_copies(lambda ray, k: rec_full.at[rows_of(ray, k), :], 5)
    for copy in inv_copies:
        copy.start()
    p_copies = []

    def send_slab(step, wide):
        for k in range(chunks):
            s_send[step, k] = wide[k * rows : (k + 1) * rows].astype(BF16)

        def send(group, k):
            remote(
                s_send.at[step, k],
                s_recv.at[step, g],
                s_sems.at[step, 0],
                s_sems.at[step, 1],
                group,
                r,
            ).start()

        each_peer(send)
        s_recv[step, g] = s_send[step, chunk]

    def fold(step):
        wait_blocks(s_recv.at[step], s_sems.at[step, 1])
        for h in range(n):
            turn_s[h * rows : (h + 1) * rows] = s_recv[step, h].astype(F32)
        lane = lax.broadcasted_iota(jnp.int32, (n, 2 * waves), 1)
        for i in range(rows):
            slab = turn_s[pl.ds(i, n, stride=rows), :]
            wide = jnp.concatenate(
                [jnp.where(lane < waves, slab, 0.0), jnp.where(lane < waves, 0.0, slab)], axis=0
            ).astype(BF16)
            both = jnp.dot(w_both[i], wide, preferred_element_type=F32)
            turn_f[i * chunks : (i + 1) * chunks] = both[:chunks] + both[chunks:]
        for k in range(chunks):
            f_send[step, k] = turn_f[pl.ds(k, rows, stride=chunks), :].astype(BF16)
        place = r * chunks + chunk

        def send(k, ray):
            remote(
                f_send.at[step, k],
                f_recv.at[step, place],
                f_sems.at[step, 0],
                f_sems.at[step, 1],
                first_target + k,
                ray,
            ).start()

        if step:
            for d in ray_order:
                each_target(lambda k, ray=other_ray(d): send(k, ray), True)
        each_target(lambda k: send(k, r), False)
        f_recv[step, place] = f_send[step, chunk]

    def send_partial(step, part):
        p_send[step] = part
        copies = [
            remote(
                p_send.at[step],
                p_recv.at[step, r],
                p_sems.at[step, 0, d - 1],
                p_sems.at[step, 1, d - 1],
                g,
                other_ray(d),
            )
            for d in ray_order
        ]
        for copy in copies:
            copy.start()
        p_copies.append(copies)
        p_recv[step, r] = part

    for copy in slab_copies:
        copy.wait_recv()
    first_slab = rs_recv[0].astype(F32)
    for k in range(1, m):
        first_slab = first_slab + rs_recv[k].astype(F32)
    send_slab(0, first_slab)

    load_self.wait()
    load_blocks.wait()
    load_exc.wait()
    for copy in cycle_copies:
        copy.wait_recv()
    base[...] = jnp.zeros_like(base)
    for step in range(steps):
        base[step, :, mine] = exc[step].astype(F32)

    def add_cycle(b, carry):
        shift = list_ref[0, b]
        source = g + shift - REACH
        valid = (b < count_ref[0]) & (source >= 0) & (source < n)
        past = [nearby[shift, lax.rem(start_slot - i + slots, slots)] for i in range(slots)]
        past = [jnp.where(valid, x, jnp.zeros_like(x)) for x in past]
        blank = jnp.zeros_like(past[0])
        lagged = jnp.concatenate(
            [
                jnp.concatenate([blank] * step + past[: slots - step], axis=1)
                for step in range(steps)
            ],
            axis=0,
        )
        near = jnp.dot(
            lagged, blocks[b].reshape(slots * width, size), preferred_element_type=F32
        )
        for step in range(steps):
            base[step] = base[step] - near[step * waves : (step + 1) * waves]
        return carry

    lax.fori_loop(0, entries, add_cycle, 0)
    for copy in rec_copies:
        copy.start()
    for copy in inv_copies:
        copy.wait_recv()
    for copy in inv_passed:
        copy.start()

    wait_blocks(w_recv, w_sems.at[1])
    for i in range(rows):
        w_all = w_recv[:, i, :]
        w_high = w_all.astype(BF16)
        w_both[i, :chunks] = w_high
        w_both[i, chunks:] = (w_all - w_high.astype(F32)).astype(BF16)
    fold(0)

    load_rad.wait()
    load_inv.wait()
    load_own_inv.wait()
    for copy in rad_copies + inv_passed:
        copy.wait_recv()
    slab_of_drive[...] = lax.dot_general(
        rad_full[...], inv_full[...], dims, preferred_element_type=F32
    ).astype(BF16)

    def gathered_sum(step):
        for copy in p_copies[step]:
            copy.wait_recv()
        total = p_recv[step, 0].astype(F32)
        for d in range(1, m):
            total = total + p_recv[step, d].astype(F32)
        return total

    def turn_field(pieces):
        turned = jnp.concatenate([x.astype(F32) for x in pieces], axis=0).T.astype(BF16)
        span = rays // 2
        return jnp.concatenate(
            [
                turned[p * waves : (p + 1) * waves, k * span : (k + 1) * span]
                for k in range(len(pieces) // chunks)
                for p in range(2)
            ],
            axis=1,
        )

    for step in range(steps):
        if step == 0:
            load_rec.wait()
            wait_blocks(f_recv.at[0], f_sems.at[0, 1], chunks - 1)
            field = turn_field([f_recv[0, r * chunks + k] for k in range(chunks)])
            far = jnp.dot(field, rec_full[rows_here, :], preferred_element_type=F32)
            send_partial(0, (base[0] - far).astype(BF16))
            for copy in rec_copies:
                copy.wait_recv()
            for copy in rec_passed:
                copy.start()
            drive = gathered_sum(0).astype(BF16)
        else:
            total = gathered_sum(step)
            if step == 1:
                for copy in rec_passed:
                    copy.wait_recv()
            wait_blocks(f_recv.at[step], f_sems.at[step, 1])
            field = turn_field([f_recv[step, k] for k in range(m * chunks)])
            far = jnp.dot(field, rec_full[...], preferred_element_type=F32)
            drive = (total - far).astype(BF16)
        if step + 1 < steps:
            slab = lax.dot_general(slab_of_drive[...], drive, dims, preferred_element_type=F32)
            send_slab(
                step + 1, jnp.concatenate([slab[: rays // 2], slab[rays // 2 :]], axis=1)
            )
        own[step] = jnp.dot(drive, inv[...], preferred_element_type=F32).astype(BF16)
        out_ref[step] = own[step]
        if step + 1 < steps:
            fresh = fresh_of[step]
            copies = near_copies(own.at[step], fresh, step + 1)
            for copy in copies:
                copy.start()
            near_all.extend(copies)
            fresh[REACH] = own[step]
            for copy in copies:
                copy.wait_recv()

            def add_near(later):
                latest = [fresh[near_shift[b]] for b in range(entries)]
                latest = [
                    jnp.where(near_valid[b], x, jnp.zeros_like(x)) for b, x in enumerate(latest)
                ]
                base[later] = base[later] - jnp.dot(
                    jnp.concatenate(latest, axis=1),
                    blocks[:, later - step - 1].reshape(entries * width, size),
                    preferred_element_type=F32,
                )

            add_near(step + 1)
            send_partial(step + 1, base[step + 1].astype(BF16))
            fold(step + 1)
            for later in range(step + 2, steps):
                add_near(later)

    gathers = inv_copies + rec_copies + inv_passed + rec_passed
    for copy in slab_copies + rad_copies + gathers + near_all + sum(p_copies, []):
        copy.wait_send()
    wait_blocks(w_send, w_sems.at[0])
    for step in range(steps):
        wait_blocks(s_recv.at[step], s_sems.at[step, 0])
        wait_blocks(f_recv.at[step], f_sems.at[step, 0], None if step else chunks - 1)


def layout_of(n):
    inner = 1
    while inner * inner < n:
        inner *= 2
    return inner, max(n // (2 * inner), 1)


def solution(mesh):
    n = mesh.shape["groups"]
    m = mesh.shape["rays"]
    inner, copies_of_fold = layout_of(n)
    chunks = n // copies_of_fold

    def local(
        excitation,
        cycle,
        near_blocks,
        near_list,
        near_count,
        newest,
        inverse,
        radiate,
        translate,
        receive,
    ):
        steps, waves, width = excitation.shape
        slots = cycle.shape[0]
        entries = near_list.shape[1]
        size = m * width
        rays = receive.shape[0]
        rows = rays // (2 * chunks)
        spread = 2 * REACH + 1
        anywhere = pl.BlockSpec(memory_space=pl.ANY)
        dma = pltpu.SemaphoreType.DMA
        vmem = pltpu.VMEM
        smem = pltpu.SMEM
        return pl.pallas_call(
            functools.partial(kernel, n, inner, copies_of_fold, m),
            out_shape=jax.ShapeDtypeStruct(excitation.shape, BF16),
            in_specs=[anywhere] * 10,
            out_specs=pl.BlockSpec(memory_space=vmem),
            scratch_shapes=[
                smem(near_list.shape, jnp.int32),
                smem(near_count.shape, jnp.int32),
                smem(newest.shape, jnp.int32),
                vmem(excitation.shape, BF16),
                vmem(cycle.shape, BF16),
                vmem((entries, slots, width, size), BF16),
                vmem((n, rays), F32),
                vmem(radiate.shape, BF16),
                vmem(inverse.shape, BF16),
                vmem((m, rays // 2, 2 * waves), BF16),
                vmem((m, rays // 2, 2 * waves), BF16),
                vmem((rays, size), BF16),
                vmem((size, size), BF16),
                vmem((rays, size), BF16),
                vmem((m * rays, size), BF16),
                vmem((spread, slots, waves, width), BF16),
                vmem((spread, waves, width), BF16),
                vmem((spread, waves, width), BF16),
                vmem((chunks, rows, 2 * n), F32),
                vmem((chunks, rows, 2 * n), F32),
                vmem((rows, 2 * chunks, 2 * n), BF16),
                vmem((n * rows, 2 * waves), F32),
                vmem((chunks * rows, 2 * waves), F32),
                vmem((steps, chunks, rows, 2 * waves), BF16),
                vmem((steps, n, rows, 2 * waves), BF16),
                vmem((steps, chunks, rows, 2 * waves), BF16),
                vmem((steps, m * chunks, rows, 2 * waves), BF16),
                vmem((steps, waves, size), F32),
                vmem((steps, waves, size), BF16),
                vmem((steps, m, waves, size), BF16),
                vmem((steps, waves, width), BF16),
                pltpu.SemaphoreType.REGULAR,
                dma((13,)),
                dma((6, m - 1)),
                dma((6, m - 1)),
                dma((2,)),
                dma((steps, 2)),
                dma((steps, 2)),
                dma((steps, 4)),
                dma((steps, 4)),
                dma((steps, 2, m - 1)),
            ],
            compiler_params=pltpu.CompilerParams(
                collective_id=0, has_side_effects=True, vmem_limit_bytes=56 * 1024 * 1024
            ),
        )(
            excitation,
            cycle,
            near_blocks,
            near_list,
            near_count,
            newest,
            inverse,
            radiate,
            translate,
            receive,
        )

    placed = (
        P(None, None, ("groups", "rays")),
        P(None, None, ("groups", "rays")),
        P("groups", None, None, "rays", None),
        P("groups", None),
        P("groups"),
        P(),
        P(None, ("groups", "rays")),
        P(None, ("groups", "rays")),
        P("groups", None, "rays"),
        P("rays", "groups"),
    )
    return jax.shard_map(
        local,
        mesh=mesh,
        in_specs=placed,
        out_specs=P(None, None, ("groups", "rays")),
        check_vma=False,
    )
```

```python
import functools

import jax
import jax.numpy as jnp
from jax import lax
from jax.experimental import pallas as pl
from jax.experimental.pallas import tpu as pltpu
from jax.sharding import PartitionSpec as P

REACH = 2
NEAR_SHIFTS = (-2, -1, 1, 2)
MESH = pl.DeviceIdType.MESH
F32 = jnp.float32
BF16 = jnp.bfloat16


def kernel(
    n,
    inner,
    copies_of_fold,
    m,
    exc_hbm,
    cyc_hbm,
    blocks_hbm,
    list_hbm,
    count_hbm,
    newest_hbm,
    inv_hbm,
    rad_hbm,
    tr_hbm,
    rec_hbm,
    out_ref,
    list_ref,
    count_ref,
    newest_ref,
    exc,
    cyc,
    blocks,
    tr,
    rad,
    inv,
    rs_send,
    rs_recv,
    rad_full,
    inv_full,
    slab_of_drive,
    rec_full,
    nearby,
    fresh_first,
    fresh_second,
    w_send,
    w_recv,
    w_both,
    turn_s,
    turn_f,
    s_send,
    s_recv,
    f_send,
    f_recv,
    base,
    p_send,
    p_recv,
    own,
    row_sem,
    load_sems,
    x_send,
    x_recv,
    w_sems,
    s_sems,
    f_sems,
    near_send,
    near_recv,
    p_sems,
):
    steps, waves, width = exc.shape
    slots = cyc.shape[0]
    entries = list_ref.shape[1]
    size = m * width
    rays = tr.shape[1]
    outer = n // inner
    chunks = n // copies_of_fold
    rows = rays // (2 * chunks)
    g = lax.axis_index("groups")
    r = lax.axis_index("rays")
    go = g // inner
    gi = g - go * inner
    pair = go // 2
    plane = go - 2 * pair
    chunk = plane * inner + gi
    first_target = g - chunk
    mine = pl.ds(pl.multiple_of(r * width, width), width)
    dims = (((1,), (1,)), ((), ()))
    fresh_of = (fresh_first, fresh_second)
    ray_order = sorted(range(1, m), key=lambda d: -min(d, m - d))
    inner_order = sorted(range(inner), key=lambda d: -min(d, inner - d))

    def wrap(x, limit):
        return jnp.where(x >= limit, x - limit, x)

    inner_place = [wrap(gi + d, inner) for d in range(inner)]
    ray_place = [wrap(r + d, m) for d in range(m)]

    def near_group(d):
        return wrap(g + d + n, n) if d < 0 else wrap(g + d, n)

    def other_ray(d):
        return ray_place[d]

    def remote(src, dst, send_sem, recv_sem, group, ray):
        return pltpu.make_async_remote_copy(
            src_ref=src,
            dst_ref=dst,
            send_sem=send_sem,
            recv_sem=recv_sem,
            device_id=(group, ray),
            device_id_type=MESH,
        )

    def each_peer(act):
        def body(k, carry):
            shift, change = carry
            place = wrap(go + shift, outer)
            other = place * inner
            bit = place - 2 * (place // 2)
            for d in inner_order:
                act(other + inner_place[d], bit * inner + inner_place[d])
            return shift + change, jnp.where(change < 0, 1 - change, -1 - change)

        lax.fori_loop(0, outer - 1, body, (jnp.int32(outer // 2), jnp.int32(-1)))
        for d in inner_order:
            if d:
                act(go * inner + inner_place[d], plane * inner + inner_place[d])

    def each_target(act, with_self):
        for d in inner_order:
            act((1 - plane) * inner + inner_place[d])
        for d in inner_order:
            if d or with_self:
                act(plane * inner + inner_place[d])

    def wait_blocks(like, sem, count=None):
        part = like.at[pl.ds(0, like.shape[0] - 1 if count is None else count)]
        pltpu.make_async_copy(part, part, sem).wait()

    def near_copies(src, dst, index):
        return [
            remote(
                src,
                dst.at[REACH - shift],
                near_send.at[index, k],
                near_recv.at[index, k],
                near_group(shift),
                r,
            )
            for k, shift in enumerate(NEAR_SHIFTS)
        ]

    def ray_copies(src_of, dst, index):
        return [
            remote(
                src_of(d), dst, x_send.at[index, d - 1], x_recv.at[index, d - 1], g, other_ray(d)
            )
            for d in ray_order
        ]

    rows_here = pl.ds(pl.multiple_of(r * rays, rays), rays)
    pairs = (
        (newest_hbm, newest_ref),
        (cyc_hbm, cyc),
        (rad_hbm, rad),
        (list_hbm, list_ref),
        (count_hbm, count_ref),
        (tr_hbm.at[0], tr),
        (rad_hbm.at[rows_here, :], rad_full.at[:, mine]),
        (blocks_hbm.at[0], blocks),
        (inv_hbm, inv_full.at[:, mine]),
        (inv_hbm, inv),
        (cyc_hbm, nearby.at[REACH]),
        (rec_hbm, rec_full.at[rows_here, :]),
        (exc_hbm, exc),
    )
    loads = [
        pltpu.make_async_copy(src, dst, load_sems.at[i]) for i, (src, dst) in enumerate(pairs)
    ]
    for load in loads[:3]:
        load.start()

    barrier = pltpu.get_barrier_semaphore()
    greeted = [(g, other_ray(d)) for d in ray_order]
    greeted += [(go * inner + inner_place[d], r) for d in inner_order if d]
    row_peers = [(wrap(go + d, outer) * inner + gi, r) for d in range(1, outer)]
    greeted += row_peers
    greeted += [(near_group(d), r) for d in NEAR_SHIFTS]
    for device in greeted:
        pl.semaphore_signal(barrier, inc=1, device_id=device, device_id_type=MESH)

    for load in loads[3:]:
        load.start()
    (
        load_newest,
        load_cyc,
        load_all_rad,
        load_list,
        load_count,
        load_tr,
        load_rad,
        load_blocks,
        load_inv,
        load_own_inv,
        load_self,
        load_rec,
        load_exc,
    ) = loads

    pl.semaphore_wait(barrier, len(greeted))

    for device in row_peers:
        pl.semaphore_signal(row_sem, inc=1, device_id=device, device_id_type=MESH)
    load_newest.wait()
    load_cyc.wait()
    start_slot = newest_ref[0]
    newest_value = cyc[start_slot]
    load_all_rad.wait()
    partial_slab = lax.dot_general(rad[...], newest_value, dims, preferred_element_type=F32)
    for k in range(m):
        top, middle = k * rays, k * rays + rays // 2
        rs_send[k] = jnp.concatenate(
            [partial_slab[top:middle], partial_slab[middle : top + rays]], axis=1
        ).astype(BF16)
    slab_copies = ray_copies(lambda d: rs_send.at[other_ray(d)], rs_recv.at[r], 0)
    for copy in slab_copies:
        copy.start()
    rs_recv[r] = rs_send[r]
    cycle_copies = near_copies(cyc_hbm, nearby, 0)
    for copy in cycle_copies:
        copy.start()
    near_all = list(cycle_copies)

    load_list.wait()
    load_count.wait()
    near_shift = []
    near_valid = []
    for b in range(entries):
        shift = list_ref[0, b]
        source = g + shift - REACH
        near_shift.append(shift)
        near_valid.append((b < count_ref[0]) & (source >= 0) & (source < n))
    load_tr.wait()
    every = lax.broadcasted_iota(jnp.int32, (n, rays), 0)
    weights = tr[...]
    for b in range(entries):
        hit = near_valid[b] & (every == g + near_shift[b] - REACH)
        weights = jnp.where(hit, 0.0, weights)
    turned = weights.T
    w_rows = jnp.concatenate([turned[: rays // 2], turned[rays // 2 :]], axis=1)
    w_send[...] = w_rows.reshape(w_send.shape)

    pl.semaphore_wait(row_sem, len(row_peers))

    def send_weights(k):
        remote(
            w_send.at[k], w_recv.at[chunk], w_sems.at[0], w_sems.at[1], first_target + k, r
        ).start()

    each_target(send_weights, False)
    w_recv[chunk] = w_send[chunk]
    rad_copies = ray_copies(
        lambda d: rad_hbm.at[pl.ds(pl.multiple_of(other_ray(d) * rays, rays), rays), :],
        rad_full.at[:, mine],
        1,
    )
    inv_copies = ray_copies(lambda d: inv_hbm, inv_full.at[:, mine], 2)
    for copy in rad_copies + inv_copies:
        copy.start()
    rec_copies = ray_copies(lambda d: rec_hbm, rec_full.at[rows_here, :], 3)
    p_copies = []

    def send_slab(step, wide):
        for k in range(chunks):
            s_send[step, k] = wide[k * rows : (k + 1) * rows].astype(BF16)

        def send(group, k):
            remote(
                s_send.at[step, k],
                s_recv.at[step, g],
                s_sems.at[step, 0],
                s_sems.at[step, 1],
                group,
                r,
            ).start()

        each_peer(send)
        s_recv[step, g] = s_send[step, chunk]

    def fold(step):
        wait_blocks(s_recv.at[step], s_sems.at[step, 1])
        for h in range(n):
            turn_s[h * rows : (h + 1) * rows] = s_recv[step, h].astype(F32)
        lane = lax.broadcasted_iota(jnp.int32, (n, 2 * waves), 1)
        for i in range(rows):
            slab = turn_s[pl.ds(i, n, stride=rows), :]
            wide = jnp.concatenate(
                [jnp.where(lane < waves, slab, 0.0), jnp.where(lane < waves, 0.0, slab)], axis=0
            ).astype(BF16)
            both = jnp.dot(w_both[i], wide, preferred_element_type=F32)
            turn_f[i * chunks : (i + 1) * chunks] = both[:chunks] + both[chunks:]
        for k in range(chunks):
            f_send[step, k] = turn_f[pl.ds(k, rows, stride=chunks), :].astype(BF16)
        place = r * chunks + chunk

        def send(k, ray):
            remote(
                f_send.at[step, k],
                f_recv.at[step, place],
                f_sems.at[step, 0],
                f_sems.at[step, 1],
                first_target + k,
                ray,
            ).start()

        if step:
            for d in ray_order:
                each_target(lambda k, ray=other_ray(d): send(k, ray), True)
        each_target(lambda k: send(k, r), False)
        f_recv[step, place] = f_send[step, chunk]

    def send_partial(step, part):
        p_send[step] = part
        copies = [
            remote(
                p_send.at[step],
                p_recv.at[step, r],
                p_sems.at[step, 0, d - 1],
                p_sems.at[step, 1, d - 1],
                g,
                other_ray(d),
            )
            for d in ray_order
        ]
        for copy in copies:
            copy.start()
        p_copies.append(copies)
        p_recv[step, r] = part

    for copy in slab_copies:
        copy.wait_recv()
    first_slab = rs_recv[0].astype(F32)
    for k in range(1, m):
        first_slab = first_slab + rs_recv[k].astype(F32)
    send_slab(0, first_slab)

    load_self.wait()
    load_blocks.wait()
    load_exc.wait()
    for copy in cycle_copies:
        copy.wait_recv()
    base[...] = jnp.zeros_like(base)
    for step in range(steps):
        base[step, :, mine] = exc[step].astype(F32)

    def add_cycle(b, carry):
        shift = list_ref[0, b]
        source = g + shift - REACH
        valid = (b < count_ref[0]) & (source >= 0) & (source < n)
        past = [nearby[shift, lax.rem(start_slot - i + slots, slots)] for i in range(slots)]
        past = [jnp.where(valid, x, jnp.zeros_like(x)) for x in past]
        blank = jnp.zeros_like(past[0])
        lagged = jnp.concatenate(
            [
                jnp.concatenate([blank] * step + past[: slots - step], axis=1)
                for step in range(steps)
            ],
            axis=0,
        )
        near = jnp.dot(
            lagged, blocks[b].reshape(slots * width, size), preferred_element_type=F32
        )
        for step in range(steps):
            base[step] = base[step] - near[step * waves : (step + 1) * waves]
        return carry

    early = (entries + 1) // 2
    lax.fori_loop(0, early, add_cycle, 0)

    wait_blocks(w_recv, w_sems.at[1])
    for i in range(rows):
        w_all = w_recv[:, i, :]
        w_high = w_all.astype(BF16)
        w_both[i, :chunks] = w_high
        w_both[i, chunks:] = (w_all - w_high.astype(F32)).astype(BF16)
    fold(0)

    lax.fori_loop(early, entries, add_cycle, 0)

    def gathered_sum(step):
        for copy in p_copies[step]:
            copy.wait_recv()
        total = p_recv[step, 0].astype(F32)
        for d in range(1, m):
            total = total + p_recv[step, d].astype(F32)
        return total

    def turn_field(pieces):
        turned = jnp.concatenate([x.astype(F32) for x in pieces], axis=0).T.astype(BF16)
        span = rays // 2
        return jnp.concatenate(
            [
                turned[p * waves : (p + 1) * waves, k * span : (k + 1) * span]
                for k in range(len(pieces) // chunks)
                for p in range(2)
            ],
            axis=1,
        )

    for step in range(steps):
        if step == 0:
            load_rec.wait()
            wait_blocks(f_recv.at[0], f_sems.at[0, 1], chunks - 1)
            field = turn_field([f_recv[0, r * chunks + k] for k in range(chunks)])
            far = jnp.dot(field, rec_full[rows_here, :], preferred_element_type=F32)
            send_partial(0, (base[0] - far).astype(BF16))
            for copy in rec_copies:
                copy.start()
            load_rad.wait()
            load_inv.wait()
            load_own_inv.wait()
            for copy in rad_copies + inv_copies:
                copy.wait_recv()
            slab_of_drive[...] = lax.dot_general(
                rad_full[...], inv_full[...], dims, preferred_element_type=F32
            ).astype(BF16)
            drive = gathered_sum(0).astype(BF16)
        else:
            total = gathered_sum(step)
            if step == 1:
                for copy in rec_copies:
                    copy.wait_recv()
            wait_blocks(f_recv.at[step], f_sems.at[step, 1])
            field = turn_field([f_recv[step, k] for k in range(m * chunks)])
            far = jnp.dot(field, rec_full[...], preferred_element_type=F32)
            drive = (total - far).astype(BF16)
        current = jnp.dot(drive, inv[...], preferred_element_type=F32).astype(BF16)
        if step + 1 < steps:
            slab = lax.dot_general(slab_of_drive[...], drive, dims, preferred_element_type=F32)
            wide = jnp.concatenate([slab[: rays // 2], slab[rays // 2 :]], axis=1)
        own[step] = current
        if step + 1 < steps:
            fresh = fresh_of[step]
            copies = near_copies(own.at[step], fresh, step + 1)
            for copy in copies:
                copy.start()
            near_all.extend(copies)
            send_slab(step + 1, wide)
            fresh[REACH] = current
        out_ref[step] = current
        if step + 1 < steps:
            for copy in copies:
                copy.wait_recv()

            def add_near(later):
                latest = [fresh[near_shift[b]] for b in range(entries)]
                latest = [
                    jnp.where(near_valid[b], x, jnp.zeros_like(x)) for b, x in enumerate(latest)
                ]
                base[later] = base[later] - jnp.dot(
                    jnp.concatenate(latest, axis=1),
                    blocks[:, later - step - 1].reshape(entries * width, size),
                    preferred_element_type=F32,
                )

            add_near(step + 1)
            send_partial(step + 1, base[step + 1].astype(BF16))
            fold(step + 1)
            for later in range(step + 2, steps):
                add_near(later)

    for copy in slab_copies + rad_copies + inv_copies + rec_copies + near_all + sum(p_copies, []):
        copy.wait_send()
    wait_blocks(w_send, w_sems.at[0])
    for step in range(steps):
        wait_blocks(s_recv.at[step], s_sems.at[step, 0])
        wait_blocks(f_recv.at[step], f_sems.at[step, 0], None if step else chunks - 1)


def layout_of(n):
    inner = 1
    while inner * inner < n:
        inner *= 2
    return inner, max(n // (2 * inner), 1)


def solution(mesh):
    n = mesh.shape["groups"]
    m = mesh.shape["rays"]
    inner, copies_of_fold = layout_of(n)
    chunks = n // copies_of_fold

    def local(
        excitation,
        cycle,
        near_blocks,
        near_list,
        near_count,
        newest,
        inverse,
        radiate,
        translate,
        receive,
    ):
        steps, waves, width = excitation.shape
        slots = cycle.shape[0]
        entries = near_list.shape[1]
        size = m * width
        rays = receive.shape[0]
        rows = rays // (2 * chunks)
        spread = 2 * REACH + 1
        anywhere = pl.BlockSpec(memory_space=pl.ANY)
        dma = pltpu.SemaphoreType.DMA
        vmem = pltpu.VMEM
        smem = pltpu.SMEM
        return pl.pallas_call(
            functools.partial(kernel, n, inner, copies_of_fold, m),
            out_shape=pltpu.VMEM(excitation.shape, BF16),
            in_specs=[anywhere] * 10,
            out_specs=pl.BlockSpec(memory_space=vmem),
            scratch_shapes=[
                smem(near_list.shape, jnp.int32),
                smem(near_count.shape, jnp.int32),
                smem(newest.shape, jnp.int32),
                vmem(excitation.shape, BF16),
                vmem(cycle.shape, BF16),
                vmem((entries, slots, width, size), BF16),
                vmem((n, rays), F32),
                vmem(radiate.shape, BF16),
                vmem(inverse.shape, BF16),
                vmem((m, rays // 2, 2 * waves), BF16),
                vmem((m, rays // 2, 2 * waves), BF16),
                vmem((rays, size), BF16),
                vmem((size, size), BF16),
                vmem((rays, size), BF16),
                vmem((m * rays, size), BF16),
                vmem((spread, slots, waves, width), BF16),
                vmem((spread, waves, width), BF16),
                vmem((spread, waves, width), BF16),
                vmem((chunks, rows, 2 * n), F32),
                vmem((chunks, rows, 2 * n), F32),
                vmem((rows, 2 * chunks, 2 * n), BF16),
                vmem((n * rows, 2 * waves), F32),
                vmem((chunks * rows, 2 * waves), F32),
                vmem((steps, chunks, rows, 2 * waves), BF16),
                vmem((steps, n, rows, 2 * waves), BF16),
                vmem((steps, chunks, rows, 2 * waves), BF16),
                vmem((steps, m * chunks, rows, 2 * waves), BF16),
                vmem((steps, waves, size), F32),
                vmem((steps, waves, size), BF16),
                vmem((steps, m, waves, size), BF16),
                vmem((steps, waves, width), BF16),
                pltpu.SemaphoreType.REGULAR,
                dma((13,)),
                dma((4, m - 1)),
                dma((4, m - 1)),
                dma((2,)),
                dma((steps, 2)),
                dma((steps, 2)),
                dma((steps, 4)),
                dma((steps, 4)),
                dma((steps, 2, m - 1)),
            ],
            compiler_params=pltpu.CompilerParams(
                collective_id=0, has_side_effects=True, vmem_limit_bytes=56 * 1024 * 1024
            ),
        )(
            excitation,
            cycle,
            near_blocks,
            near_list,
            near_count,
            newest,
            inverse,
            radiate,
            translate,
            receive,
        )

    placed = (
        P(None, None, ("groups", "rays")),
        P(None, None, ("groups", "rays")),
        P("groups", None, None, "rays", None),
        P("groups", None),
        P("groups"),
        P(),
        P(None, ("groups", "rays")),
        P(None, ("groups", "rays")),
        P("groups", None, "rays"),
        P("rays", "groups"),
    )
    return jax.shard_map(
        local,
        mesh=mesh,
        in_specs=placed,
        out_specs=P(None, None, ("groups", "rays")),
        check_vma=False,
    )
```

```python
import functools

import jax
import jax.numpy as jnp
from jax import lax
from jax.experimental import pallas as pl
from jax.experimental.pallas import tpu as pltpu
from jax.sharding import PartitionSpec as P

REACH = 2
NEAR_SHIFTS = (-2, -1, 1, 2)
MESH = pl.DeviceIdType.MESH
F32 = jnp.float32
BF16 = jnp.bfloat16


def kernel(
    n,
    inner,
    copies_of_fold,
    m,
    exc_hbm,
    cyc_hbm,
    blocks_hbm,
    list_hbm,
    count_hbm,
    newest_hbm,
    inv_hbm,
    rad_hbm,
    tr_hbm,
    rec_hbm,
    out_ref,
    list_ref,
    count_ref,
    newest_ref,
    exc,
    cyc,
    blocks,
    tr,
    rad,
    inv,
    rs_send,
    rs_recv,
    rad_full,
    inv_full,
    slab_of_drive,
    rec_full,
    nearby,
    fresh_first,
    fresh_second,
    w_send,
    w_recv,
    w_both,
    turn_s,
    turn_f,
    s_send,
    s_recv,
    f_send,
    f_recv,
    base,
    p_send,
    p_recv,
    own,
    row_sem,
    load_sems,
    x_send,
    x_recv,
    w_sems,
    s_sems,
    f_sems,
    near_send,
    near_recv,
    p_sems,
):
    steps, waves, width = exc.shape
    slots = cyc.shape[0]
    entries = list_ref.shape[1]
    size = m * width
    rays = tr.shape[1]
    outer = n // inner
    chunks = n // copies_of_fold
    rows = rays // (2 * chunks)
    g = lax.axis_index("groups")
    r = lax.axis_index("rays")
    go = g // inner
    gi = g - go * inner
    pair = go // 2
    plane = go - 2 * pair
    chunk = plane * inner + gi
    first_target = g - chunk
    mine = pl.ds(pl.multiple_of(r * width, width), width)
    dims = (((1,), (1,)), ((), ()))
    fresh_of = (fresh_first, fresh_second)
    ray_order = sorted(range(1, m), key=lambda d: -min(d, m - d))
    inner_order = sorted(range(inner), key=lambda d: -min(d, inner - d))

    def wrap(x, limit):
        return jnp.where(x >= limit, x - limit, x)

    inner_place = [wrap(gi + d, inner) for d in range(inner)]
    ray_place = [wrap(r + d, m) for d in range(m)]

    def near_group(d):
        return wrap(g + d + n, n) if d < 0 else wrap(g + d, n)

    def other_ray(d):
        return ray_place[d]

    def remote(src, dst, send_sem, recv_sem, group, ray):
        return pltpu.make_async_remote_copy(
            src_ref=src,
            dst_ref=dst,
            send_sem=send_sem,
            recv_sem=recv_sem,
            device_id=(group, ray),
            device_id_type=MESH,
        )

    def each_peer(act):
        def body(k, carry):
            shift, change = carry
            place = wrap(go + shift, outer)
            other = place * inner
            bit = place - 2 * (place // 2)
            for d in inner_order:
                act(other + inner_place[d], bit * inner + inner_place[d])
            return shift + change, jnp.where(change < 0, 1 - change, -1 - change)

        lax.fori_loop(0, outer - 1, body, (jnp.int32(outer // 2), jnp.int32(-1)))
        for d in inner_order:
            if d:
                act(go * inner + inner_place[d], plane * inner + inner_place[d])

    def each_target(act, with_self):
        for d in inner_order:
            act((1 - plane) * inner + inner_place[d])
        for d in inner_order:
            if d or with_self:
                act(plane * inner + inner_place[d])

    def wait_blocks(like, sem, count=None):
        part = like.at[pl.ds(0, like.shape[0] - 1 if count is None else count)]
        pltpu.make_async_copy(part, part, sem).wait()

    def near_copies(src, dst, index):
        return [
            remote(
                src,
                dst.at[REACH - shift],
                near_send.at[index, k],
                near_recv.at[index, k],
                near_group(shift),
                r,
            )
            for k, shift in enumerate(NEAR_SHIFTS)
        ]

    def ray_copies(src_of, dst, index):
        return [
            remote(
                src_of(d), dst, x_send.at[index, d - 1], x_recv.at[index, d - 1], g, other_ray(d)
            )
            for d in ray_order
        ]

    rows_here = pl.ds(pl.multiple_of(r * rays, rays), rays)
    pairs = (
        (newest_hbm, newest_ref),
        (cyc_hbm, cyc),
        (rad_hbm, rad),
        (list_hbm, list_ref),
        (count_hbm, count_ref),
        (tr_hbm.at[0], tr),
        (rad_hbm.at[rows_here, :], rad_full.at[:, mine]),
        (blocks_hbm.at[0], blocks),
        (inv_hbm, inv_full.at[:, mine]),
        (inv_hbm, inv),
        (cyc_hbm, nearby.at[REACH]),
        (rec_hbm, rec_full.at[rows_here, :]),
        (exc_hbm, exc),
    )
    loads = [
        pltpu.make_async_copy(src, dst, load_sems.at[i]) for i, (src, dst) in enumerate(pairs)
    ]
    for load in loads[:3]:
        load.start()

    barrier = pltpu.get_barrier_semaphore()
    greeted = [(g, other_ray(d)) for d in ray_order]
    greeted += [(go * inner + inner_place[d], r) for d in inner_order if d]
    row_peers = [(wrap(go + d, outer) * inner + gi, r) for d in range(1, outer)]
    greeted += row_peers
    greeted += [(near_group(d), r) for d in NEAR_SHIFTS]
    for device in greeted:
        pl.semaphore_signal(barrier, inc=1, device_id=device, device_id_type=MESH)

    for load in loads[3:]:
        load.start(priority=1)
    (
        load_newest,
        load_cyc,
        load_all_rad,
        load_list,
        load_count,
        load_tr,
        load_rad,
        load_blocks,
        load_inv,
        load_own_inv,
        load_self,
        load_rec,
        load_exc,
    ) = loads

    pl.semaphore_wait(barrier, len(greeted))

    for device in row_peers:
        pl.semaphore_signal(row_sem, inc=1, device_id=device, device_id_type=MESH)
    load_newest.wait()
    load_cyc.wait()
    start_slot = newest_ref[0]
    newest_value = cyc[start_slot]
    load_all_rad.wait()
    partial_slab = lax.dot_general(rad[...], newest_value, dims, preferred_element_type=F32)
    for k in range(m):
        top, middle = k * rays, k * rays + rays // 2
        rs_send[k] = jnp.concatenate(
            [partial_slab[top:middle], partial_slab[middle : top + rays]], axis=1
        ).astype(BF16)
    slab_copies = ray_copies(lambda d: rs_send.at[other_ray(d)], rs_recv.at[r], 0)
    for copy in slab_copies:
        copy.start()
    rs_recv[r] = rs_send[r]
    cycle_copies = near_copies(cyc_hbm, nearby, 0)
    near_all = list(cycle_copies)

    load_list.wait()
    load_count.wait()
    near_shift = []
    near_valid = []
    for b in range(entries):
        shift = list_ref[0, b]
        source = g + shift - REACH
        near_shift.append(shift)
        near_valid.append((b < count_ref[0]) & (source >= 0) & (source < n))
    load_tr.wait()
    every = lax.broadcasted_iota(jnp.int32, (n, rays), 0)
    weights = tr[...]
    for b in range(entries):
        hit = near_valid[b] & (every == g + near_shift[b] - REACH)
        weights = jnp.where(hit, 0.0, weights)
    turned = weights.T
    w_rows = jnp.concatenate([turned[: rays // 2], turned[rays // 2 :]], axis=1)
    w_send[...] = w_rows.reshape(w_send.shape)

    pl.semaphore_wait(row_sem, len(row_peers))

    def send_weights(k):
        remote(
            w_send.at[k], w_recv.at[chunk], w_sems.at[0], w_sems.at[1], first_target + k, r
        ).start()

    each_target(send_weights, False)
    w_recv[chunk] = w_send[chunk]
    rad_copies = ray_copies(
        lambda d: rad_hbm.at[pl.ds(pl.multiple_of(other_ray(d) * rays, rays), rays), :],
        rad_full.at[:, mine],
        1,
    )
    inv_copies = ray_copies(lambda d: inv_hbm, inv_full.at[:, mine], 2)
    half = rays // 2
    rec_copies = []
    for k in range(2):
        there = pl.ds(pl.multiple_of(r * rays + k * half, half), half)
        rec_copies.append(
            ray_copies(
                lambda d, k=k: rec_hbm.at[pl.ds(k * half, half), :], rec_full.at[there, :], 3 + k
            )
        )
    p_copies = []

    def send_slab(step, wide):
        for k in range(chunks):
            s_send[step, k] = wide[k * rows : (k + 1) * rows].astype(BF16)

        def send(group, k):
            remote(
                s_send.at[step, k],
                s_recv.at[step, g],
                s_sems.at[step, 0],
                s_sems.at[step, 1],
                group,
                r,
            ).start()

        each_peer(send)
        s_recv[step, g] = s_send[step, chunk]

    def fold(step):
        wait_blocks(s_recv.at[step], s_sems.at[step, 1])
        for h in range(n):
            turn_s[h * rows : (h + 1) * rows] = s_recv[step, h].astype(F32)
        lane = lax.broadcasted_iota(jnp.int32, (n, 2 * waves), 1)
        for i in range(rows):
            slab = turn_s[pl.ds(i, n, stride=rows), :]
            wide = jnp.concatenate(
                [jnp.where(lane < waves, slab, 0.0), jnp.where(lane < waves, 0.0, slab)], axis=0
            ).astype(BF16)
            both = jnp.dot(w_both[i], wide, preferred_element_type=F32)
            turn_f[i * chunks : (i + 1) * chunks] = both[:chunks] + both[chunks:]
        for k in range(chunks):
            f_send[step, k] = turn_f[pl.ds(k, rows, stride=chunks), :].astype(BF16)
        place = r * chunks + chunk

        def send(k, ray):
            remote(
                f_send.at[step, k],
                f_recv.at[step, place],
                f_sems.at[step, 0],
                f_sems.at[step, 1],
                first_target + k,
                ray,
            ).start()

        if step:
            for d in ray_order:
                each_target(lambda k, ray=other_ray(d): send(k, ray), True)
        each_target(lambda k: send(k, r), False)
        f_recv[step, place] = f_send[step, chunk]

    def send_partial(step, part):
        p_send[step] = part
        copies = [
            remote(
                p_send.at[step],
                p_recv.at[step, r],
                p_sems.at[step, 0, d - 1],
                p_sems.at[step, 1, d - 1],
                g,
                other_ray(d),
            )
            for d in ray_order
        ]
        for copy in copies:
            copy.start()
        p_copies.append(copies)
        p_recv[step, r] = part

    for copy in slab_copies:
        copy.wait_recv()
    first_slab = rs_recv[0].astype(F32)
    for k in range(1, m):
        first_slab = first_slab + rs_recv[k].astype(F32)
    send_slab(0, first_slab)
    for copy in cycle_copies + rad_copies + inv_copies:
        copy.start()

    wait_blocks(w_recv, w_sems.at[1])
    for i in range(rows):
        w_all = w_recv[:, i, :]
        w_high = w_all.astype(BF16)
        w_both[i, :chunks] = w_high
        w_both[i, chunks:] = (w_all - w_high.astype(F32)).astype(BF16)
    fold(0)

    load_self.wait()
    load_blocks.wait()
    load_exc.wait()
    for copy in cycle_copies:
        copy.wait_recv()
    base[...] = jnp.zeros_like(base)
    for step in range(steps):
        base[step, :, mine] = exc[step].astype(F32)

    def add_cycle(b, carry):
        shift = list_ref[0, b]
        source = g + shift - REACH
        valid = (b < count_ref[0]) & (source >= 0) & (source < n)
        past = [nearby[shift, lax.rem(start_slot - i + slots, slots)] for i in range(slots)]
        past = [jnp.where(valid, x, jnp.zeros_like(x)) for x in past]
        blank = jnp.zeros_like(past[0])
        lagged = jnp.concatenate(
            [
                jnp.concatenate([blank] * step + past[: slots - step], axis=1)
                for step in range(steps)
            ],
            axis=0,
        )
        near = jnp.dot(
            lagged, blocks[b].reshape(slots * width, size), preferred_element_type=F32
        )
        for step in range(steps):
            base[step] = base[step] - near[step * waves : (step + 1) * waves]
        return carry


    lax.fori_loop(0, entries, add_cycle, 0)

    def gathered_sum(step):
        for copy in p_copies[step]:
            copy.wait_recv()
        total = p_recv[step, 0].astype(F32)
        for d in range(1, m):
            total = total + p_recv[step, d].astype(F32)
        return total

    def turn_field(pieces):
        turned = jnp.concatenate([x.astype(F32) for x in pieces], axis=0).T.astype(BF16)
        span = rays // 2
        return jnp.concatenate(
            [
                turned[p * waves : (p + 1) * waves, k * span : (k + 1) * span]
                for k in range(len(pieces) // chunks)
                for p in range(2)
            ],
            axis=1,
        )

    for step in range(steps):
        if step == 0:
            load_rec.wait()
            wait_blocks(f_recv.at[0], f_sems.at[0, 1], chunks - 1)
            field = turn_field([f_recv[0, r * chunks + k] for k in range(chunks)])
            far = jnp.dot(field, rec_full[rows_here, :], preferred_element_type=F32)
            send_partial(0, (base[0] - far).astype(BF16))
            for copy in rec_copies[0]:
                copy.start()
            load_rad.wait()
            load_inv.wait()
            load_own_inv.wait()
            for copy in rad_copies + inv_copies:
                copy.wait_recv()
            slab_of_drive[...] = lax.dot_general(
                rad_full[...], inv_full[...], dims, preferred_element_type=F32
            ).astype(BF16)
            drive = gathered_sum(0).astype(BF16)
        else:
            total = gathered_sum(step)
            if step == 1:
                for copy in rec_copies[0] + rec_copies[1]:
                    copy.wait_recv()
            wait_blocks(f_recv.at[step], f_sems.at[step, 1])
            field = turn_field([f_recv[step, k] for k in range(m * chunks)])
            far = jnp.dot(field, rec_full[...], preferred_element_type=F32)
            drive = (total - far).astype(BF16)
        current = jnp.dot(drive, inv[...], preferred_element_type=F32).astype(BF16)
        if step + 1 < steps:
            slab = lax.dot_general(slab_of_drive[...], drive, dims, preferred_element_type=F32)
            wide = jnp.concatenate([slab[: rays // 2], slab[rays // 2 :]], axis=1)
        own[step] = current
        if step + 1 < steps:
            fresh = fresh_of[step]
            copies = near_copies(own.at[step], fresh, step + 1)
            for copy in copies:
                copy.start()
            near_all.extend(copies)
            send_slab(step + 1, wide)
            if step == 0:
                for copy in rec_copies[1]:
                    copy.start()
            fresh[REACH] = current
        out_ref[step] = current
        if step + 1 < steps:
            for copy in copies:
                copy.wait_recv()

            def add_near(later):
                latest = [fresh[near_shift[b]] for b in range(entries)]
                latest = [
                    jnp.where(near_valid[b], x, jnp.zeros_like(x)) for b, x in enumerate(latest)
                ]
                base[later] = base[later] - jnp.dot(
                    jnp.concatenate(latest, axis=1),
                    blocks[:, later - step - 1].reshape(entries * width, size),
                    preferred_element_type=F32,
                )

            add_near(step + 1)
            send_partial(step + 1, base[step + 1].astype(BF16))
            fold(step + 1)
            for later in range(step + 2, steps):
                add_near(later)

    for copy in slab_copies + rad_copies + inv_copies + sum(rec_copies, []) + near_all + sum(p_copies, []):
        copy.wait_send()
    wait_blocks(w_send, w_sems.at[0])
    for step in range(steps):
        wait_blocks(s_recv.at[step], s_sems.at[step, 0])
        wait_blocks(f_recv.at[step], f_sems.at[step, 0], None if step else chunks - 1)


def layout_of(n):
    inner = 1
    while inner * inner < n:
        inner *= 2
    return inner, max(n // (2 * inner), 1)


def solution(mesh):
    n = mesh.shape["groups"]
    m = mesh.shape["rays"]
    inner, copies_of_fold = layout_of(n)
    chunks = n // copies_of_fold

    def local(
        excitation,
        cycle,
        near_blocks,
        near_list,
        near_count,
        newest,
        inverse,
        radiate,
        translate,
        receive,
    ):
        steps, waves, width = excitation.shape
        slots = cycle.shape[0]
        entries = near_list.shape[1]
        size = m * width
        rays = receive.shape[0]
        rows = rays // (2 * chunks)
        spread = 2 * REACH + 1
        anywhere = pl.BlockSpec(memory_space=pl.ANY)
        dma = pltpu.SemaphoreType.DMA
        vmem = pltpu.VMEM
        smem = pltpu.SMEM
        return pl.pallas_call(
            functools.partial(kernel, n, inner, copies_of_fold, m),
            out_shape=pltpu.VMEM(excitation.shape, BF16),
            in_specs=[anywhere] * 10,
            out_specs=pl.BlockSpec(memory_space=vmem),
            scratch_shapes=[
                smem(near_list.shape, jnp.int32),
                smem(near_count.shape, jnp.int32),
                smem(newest.shape, jnp.int32),
                vmem(excitation.shape, BF16),
                vmem(cycle.shape, BF16),
                vmem((entries, slots, width, size), BF16),
                vmem((n, rays), F32),
                vmem(radiate.shape, BF16),
                vmem(inverse.shape, BF16),
                vmem((m, rays // 2, 2 * waves), BF16),
                vmem((m, rays // 2, 2 * waves), BF16),
                vmem((rays, size), BF16),
                vmem((size, size), BF16),
                vmem((rays, size), BF16),
                vmem((m * rays, size), BF16),
                vmem((spread, slots, waves, width), BF16),
                vmem((spread, waves, width), BF16),
                vmem((spread, waves, width), BF16),
                vmem((chunks, rows, 2 * n), F32),
                vmem((chunks, rows, 2 * n), F32),
                vmem((rows, 2 * chunks, 2 * n), BF16),
                vmem((n * rows, 2 * waves), F32),
                vmem((chunks * rows, 2 * waves), F32),
                vmem((steps, chunks, rows, 2 * waves), BF16),
                vmem((steps, n, rows, 2 * waves), BF16),
                vmem((steps, chunks, rows, 2 * waves), BF16),
                vmem((steps, m * chunks, rows, 2 * waves), BF16),
                vmem((steps, waves, size), F32),
                vmem((steps, waves, size), BF16),
                vmem((steps, m, waves, size), BF16),
                vmem((steps, waves, width), BF16),
                pltpu.SemaphoreType.REGULAR,
                dma((13,)),
                dma((5, m - 1)),
                dma((5, m - 1)),
                dma((2,)),
                dma((steps, 2)),
                dma((steps, 2)),
                dma((steps, 4)),
                dma((steps, 4)),
                dma((steps, 2, m - 1)),
            ],
            compiler_params=pltpu.CompilerParams(
                collective_id=0, has_side_effects=True, vmem_limit_bytes=56 * 1024 * 1024
            ),
        )(
            excitation,
            cycle,
            near_blocks,
            near_list,
            near_count,
            newest,
            inverse,
            radiate,
            translate,
            receive,
        )

    placed = (
        P(None, None, ("groups", "rays")),
        P(None, None, ("groups", "rays")),
        P("groups", None, None, "rays", None),
        P("groups", None),
        P("groups"),
        P(),
        P(None, ("groups", "rays")),
        P(None, ("groups", "rays")),
        P("groups", None, "rays"),
        P("rays", "groups"),
    )
    return jax.shard_map(
        local,
        mesh=mesh,
        in_specs=placed,
        out_specs=P(None, None, ("groups", "rays")),
        check_vma=False,
    )
```

```python
import functools

import jax
import jax.numpy as jnp
from jax import lax
from jax.experimental import pallas as pl
from jax.experimental.pallas import tpu as pltpu
from jax.sharding import PartitionSpec as P

REACH = 2
NEAR_SHIFTS = (-2, -1, 1, 2)
MESH = pl.DeviceIdType.MESH
F32 = jnp.float32
BF16 = jnp.bfloat16


def kernel(
    n,
    inner,
    copies_of_fold,
    m,
    exc_hbm,
    cyc_hbm,
    blocks_hbm,
    list_hbm,
    count_hbm,
    newest_hbm,
    inv_hbm,
    rad_hbm,
    tr_hbm,
    rec_hbm,
    out_ref,
    list_ref,
    count_ref,
    newest_ref,
    exc,
    cyc,
    blocks,
    tr,
    rad,
    inv,
    rs_send,
    rs_recv,
    rad_full,
    inv_full,
    slab_of_drive,
    rec_full,
    nearby,
    fresh_first,
    fresh_second,
    w_send,
    w_recv,
    w_both,
    turn_s,
    turn_f,
    s_send,
    s_recv,
    f_send,
    f_recv,
    base,
    p_send,
    p_recv,
    own,
    row_sem,
    load_sems,
    x_send,
    x_recv,
    w_sems,
    s_sems,
    f_sems,
    near_send,
    near_recv,
    p_sems,
):
    steps, waves, width = exc.shape
    slots = cyc.shape[0]
    entries = list_ref.shape[1]
    size = m * width
    rays = tr.shape[1]
    outer = n // inner
    chunks = n // copies_of_fold
    rows = rays // (2 * chunks)
    g = lax.axis_index("groups")
    r = lax.axis_index("rays")
    go = g // inner
    gi = g - go * inner
    pair = go // 2
    plane = go - 2 * pair
    chunk = plane * inner + gi
    first_target = g - chunk
    mine = pl.ds(pl.multiple_of(r * width, width), width)
    dims = (((1,), (1,)), ((), ()))
    fresh_of = (fresh_first, fresh_second)
    ray_order = sorted(range(1, m), key=lambda d: -min(d, m - d))
    inner_order = sorted(range(inner), key=lambda d: -min(d, inner - d))

    def wrap(x, limit):
        return jnp.where(x >= limit, x - limit, x)

    inner_place = [wrap(gi + d, inner) for d in range(inner)]
    ray_place = [wrap(r + d, m) for d in range(m)]

    def near_group(d):
        return wrap(g + d + n, n) if d < 0 else wrap(g + d, n)

    def other_ray(d):
        return ray_place[d]

    def remote(src, dst, send_sem, recv_sem, group, ray):
        return pltpu.make_async_remote_copy(
            src_ref=src,
            dst_ref=dst,
            send_sem=send_sem,
            recv_sem=recv_sem,
            device_id=(group, ray),
            device_id_type=MESH,
        )

    def each_peer(act):
        def body(k, carry):
            shift, change = carry
            place = wrap(go + shift, outer)
            other = place * inner
            bit = place - 2 * (place // 2)
            for d in inner_order:
                act(other + inner_place[d], bit * inner + inner_place[d])
            return shift + change, jnp.where(change < 0, 1 - change, -1 - change)

        lax.fori_loop(0, outer - 1, body, (jnp.int32(outer // 2), jnp.int32(-1)))
        for d in inner_order:
            if d:
                act(go * inner + inner_place[d], plane * inner + inner_place[d])

    def each_target(act, with_self):
        for d in inner_order:
            act((1 - plane) * inner + inner_place[d])
        for d in inner_order:
            if d or with_self:
                act(plane * inner + inner_place[d])

    def wait_blocks(like, sem, count=None):
        part = like.at[pl.ds(0, like.shape[0] - 1 if count is None else count)]
        pltpu.make_async_copy(part, part, sem).wait()

    def near_copies(src, dst, index):
        return [
            remote(
                src,
                dst.at[REACH - shift],
                near_send.at[index, k],
                near_recv.at[index, k],
                near_group(shift),
                r,
            )
            for k, shift in enumerate(NEAR_SHIFTS)
        ]

    def ray_copies(src_of, dst, index):
        return [
            remote(
                src_of(d), dst, x_send.at[index, d - 1], x_recv.at[index, d - 1], g, other_ray(d)
            )
            for d in ray_order
        ]

    rows_here = pl.ds(pl.multiple_of(r * rays, rays), rays)
    pairs = (
        (newest_hbm, newest_ref),
        (cyc_hbm, cyc),
        (rad_hbm, rad),
        (list_hbm, list_ref),
        (count_hbm, count_ref),
        (tr_hbm.at[0], tr),
        (rad_hbm.at[rows_here, :], rad_full.at[:, mine]),
        (blocks_hbm.at[0], blocks),
        (inv_hbm, inv_full.at[:, mine]),
        (inv_hbm, inv),
        (cyc_hbm, nearby.at[REACH]),
        (rec_hbm, rec_full.at[rows_here, :]),
        (exc_hbm, exc),
    )
    loads = [
        pltpu.make_async_copy(src, dst, load_sems.at[i]) for i, (src, dst) in enumerate(pairs)
    ]
    for load in loads[:3]:
        load.start()

    barrier = pltpu.get_barrier_semaphore()
    greeted = [(g, other_ray(d)) for d in ray_order]
    greeted += [(go * inner + inner_place[d], r) for d in inner_order if d]
    row_peers = [(wrap(go + d, outer) * inner + gi, r) for d in range(1, outer)]
    greeted += row_peers
    greeted += [(near_group(d), r) for d in NEAR_SHIFTS]
    for device in greeted:
        pl.semaphore_signal(barrier, inc=1, device_id=device, device_id_type=MESH)

    for load in loads[3:]:
        load.start(priority=1)
    (
        load_newest,
        load_cyc,
        load_all_rad,
        load_list,
        load_count,
        load_tr,
        load_rad,
        load_blocks,
        load_inv,
        load_own_inv,
        load_self,
        load_rec,
        load_exc,
    ) = loads

    pl.semaphore_wait(barrier, len(greeted))

    for device in row_peers:
        pl.semaphore_signal(row_sem, inc=1, device_id=device, device_id_type=MESH)
    load_newest.wait()
    load_cyc.wait()
    start_slot = newest_ref[0]
    newest_value = cyc[start_slot]
    load_all_rad.wait()
    partial_slab = lax.dot_general(rad[...], newest_value, dims, preferred_element_type=F32)
    for k in range(m):
        top, middle = k * rays, k * rays + rays // 2
        rs_send[k] = jnp.concatenate(
            [partial_slab[top:middle], partial_slab[middle : top + rays]], axis=1
        ).astype(BF16)
    slab_copies = ray_copies(lambda d: rs_send.at[other_ray(d)], rs_recv.at[r], 0)
    for copy in slab_copies:
        copy.start()
    rs_recv[r] = rs_send[r]
    cycle_copies = near_copies(cyc_hbm, nearby, 0)
    near_all = list(cycle_copies)

    load_list.wait()
    load_count.wait()
    near_shift = []
    near_valid = []
    for b in range(entries):
        shift = list_ref[0, b]
        source = g + shift - REACH
        near_shift.append(shift)
        near_valid.append((b < count_ref[0]) & (source >= 0) & (source < n))
    load_tr.wait()
    every = lax.broadcasted_iota(jnp.int32, (n, rays), 0)
    weights = tr[...]
    for b in range(entries):
        hit = near_valid[b] & (every == g + near_shift[b] - REACH)
        weights = jnp.where(hit, 0.0, weights)
    turned = weights.T
    w_rows = jnp.concatenate([turned[: rays // 2], turned[rays // 2 :]], axis=1)
    w_send[...] = w_rows.reshape(w_send.shape)

    pl.semaphore_wait(row_sem, len(row_peers))

    def send_weights(k):
        remote(
            w_send.at[k], w_recv.at[chunk], w_sems.at[0], w_sems.at[1], first_target + k, r
        ).start()

    each_target(send_weights, False)
    w_recv[chunk] = w_send[chunk]
    rad_copies = ray_copies(
        lambda d: rad_hbm.at[pl.ds(pl.multiple_of(other_ray(d) * rays, rays), rays), :],
        rad_full.at[:, mine],
        1,
    )
    near_rays = sorted({1 % m, m - 1} - {0})
    half = rays // 2

    def columns_of(ray):
        return pl.ds(pl.multiple_of(ray * width, width), width)

    def rows_of(ray, k):
        return pl.ds(pl.multiple_of(ray * rays + k * half, half), half)

    def ring_copies(part_of, index):
        copies = []
        for k, d in enumerate(near_rays):
            src, dst = part_of(d, k)
            copies.append(
                remote(src, dst, x_send.at[index, d - 1], x_recv.at[index, d - 1], g, other_ray(d))
            )
        return copies

    def inv_part(d, k):
        part = inv_full.at[pl.ds(k * (size // 2), size // 2), columns_of(other_ray(m - d))]
        return part, part

    def rec_part(d, k):
        part = rec_full.at[rows_of(other_ray(m - d), k), :]
        return part, part

    inv_copies = ring_copies(lambda d, k: (inv_hbm, inv_full.at[:, mine]), 2)
    inv_passed = ring_copies(inv_part, 3) if m == 4 else []
    rec_copies = [
        ring_copies(
            lambda d, k: (rec_hbm.at[pl.ds(k * half, half), :], rec_full.at[rows_of(r, k), :]), 4
        ),
        ring_copies(
            lambda d, k: (
                rec_hbm.at[pl.ds((1 - k) * half, half), :],
                rec_full.at[rows_of(r, 1 - k), :],
            ),
            5,
        ),
    ]
    rec_passed = ring_copies(rec_part, 6) if m == 4 else []
    p_copies = []

    def send_slab(step, wide):
        for k in range(chunks):
            s_send[step, k] = wide[k * rows : (k + 1) * rows].astype(BF16)

        def send(group, k):
            remote(
                s_send.at[step, k],
                s_recv.at[step, g],
                s_sems.at[step, 0],
                s_sems.at[step, 1],
                group,
                r,
            ).start()

        each_peer(send)
        s_recv[step, g] = s_send[step, chunk]

    def fold(step):
        wait_blocks(s_recv.at[step], s_sems.at[step, 1])
        for h in range(n):
            turn_s[h * rows : (h + 1) * rows] = s_recv[step, h].astype(F32)
        lane = lax.broadcasted_iota(jnp.int32, (n, 2 * waves), 1)
        for i in range(rows):
            slab = turn_s[pl.ds(i, n, stride=rows), :]
            wide = jnp.concatenate(
                [jnp.where(lane < waves, slab, 0.0), jnp.where(lane < waves, 0.0, slab)], axis=0
            ).astype(BF16)
            both = jnp.dot(w_both[i], wide, preferred_element_type=F32)
            turn_f[i * chunks : (i + 1) * chunks] = both[:chunks] + both[chunks:]
        for k in range(chunks):
            f_send[step, k] = turn_f[pl.ds(k, rows, stride=chunks), :].astype(BF16)
        place = r * chunks + chunk

        def send(k, ray):
            remote(
                f_send.at[step, k],
                f_recv.at[step, place],
                f_sems.at[step, 0],
                f_sems.at[step, 1],
                first_target + k,
                ray,
            ).start()

        if step:
            for d in ray_order:
                each_target(lambda k, ray=other_ray(d): send(k, ray), True)
        each_target(lambda k: send(k, r), False)
        f_recv[step, place] = f_send[step, chunk]

    def send_partial(step, part):
        p_send[step] = part
        copies = [
            remote(
                p_send.at[step],
                p_recv.at[step, r],
                p_sems.at[step, 0, d - 1],
                p_sems.at[step, 1, d - 1],
                g,
                other_ray(d),
            )
            for d in ray_order
        ]
        for copy in copies:
            copy.start()
        p_copies.append(copies)
        p_recv[step, r] = part

    for copy in slab_copies:
        copy.wait_recv()
    first_slab = rs_recv[0].astype(F32)
    for k in range(1, m):
        first_slab = first_slab + rs_recv[k].astype(F32)
    send_slab(0, first_slab)
    for copy in cycle_copies + inv_copies + rad_copies:
        copy.start()

    wait_blocks(w_recv, w_sems.at[1])
    for i in range(rows):
        w_all = w_recv[:, i, :]
        w_high = w_all.astype(BF16)
        w_both[i, :chunks] = w_high
        w_both[i, chunks:] = (w_all - w_high.astype(F32)).astype(BF16)
    fold(0)
    for copy in inv_copies:
        copy.wait_recv()
    for copy in inv_passed:
        copy.start()

    load_self.wait()
    load_blocks.wait()
    load_exc.wait()
    for copy in cycle_copies:
        copy.wait_recv()
    base[...] = jnp.zeros_like(base)
    for step in range(steps):
        base[step, :, mine] = exc[step].astype(F32)

    def add_cycle(b, carry):
        shift = list_ref[0, b]
        source = g + shift - REACH
        valid = (b < count_ref[0]) & (source >= 0) & (source < n)
        past = [nearby[shift, lax.rem(start_slot - i + slots, slots)] for i in range(slots)]
        past = [jnp.where(valid, x, jnp.zeros_like(x)) for x in past]
        blank = jnp.zeros_like(past[0])
        lagged = jnp.concatenate(
            [
                jnp.concatenate([blank] * step + past[: slots - step], axis=1)
                for step in range(steps)
            ],
            axis=0,
        )
        near = jnp.dot(
            lagged, blocks[b].reshape(slots * width, size), preferred_element_type=F32
        )
        for step in range(steps):
            base[step] = base[step] - near[step * waves : (step + 1) * waves]
        return carry


    lax.fori_loop(0, entries, add_cycle, 0)

    def gathered_sum(step):
        for copy in p_copies[step]:
            copy.wait_recv()
        total = p_recv[step, 0].astype(F32)
        for d in range(1, m):
            total = total + p_recv[step, d].astype(F32)
        return total

    def turn_field(pieces):
        turned = jnp.concatenate([x.astype(F32) for x in pieces], axis=0).T.astype(BF16)
        span = rays // 2
        return jnp.concatenate(
            [
                turned[p * waves : (p + 1) * waves, k * span : (k + 1) * span]
                for k in range(len(pieces) // chunks)
                for p in range(2)
            ],
            axis=1,
        )

    for step in range(steps):
        if step == 0:
            load_rec.wait()
            wait_blocks(f_recv.at[0], f_sems.at[0, 1], chunks - 1)
            field = turn_field([f_recv[0, r * chunks + k] for k in range(chunks)])
            far = jnp.dot(field, rec_full[rows_here, :], preferred_element_type=F32)
            send_partial(0, (base[0] - far).astype(BF16))
            for copy in rec_copies[0]:
                copy.start()
            load_rad.wait()
            load_inv.wait()
            load_own_inv.wait()
            for copy in rad_copies + inv_passed:
                copy.wait_recv()
            slab_of_drive[...] = lax.dot_general(
                rad_full[...], inv_full[...], dims, preferred_element_type=F32
            ).astype(BF16)
            drive = gathered_sum(0).astype(BF16)
        else:
            total = gathered_sum(step)
            if step == 1:
                for copy in rec_copies[1] + rec_passed:
                    copy.wait_recv()
            wait_blocks(f_recv.at[step], f_sems.at[step, 1])
            field = turn_field([f_recv[step, k] for k in range(m * chunks)])
            far = jnp.dot(field, rec_full[...], preferred_element_type=F32)
            drive = (total - far).astype(BF16)
        current = jnp.dot(drive, inv[...], preferred_element_type=F32).astype(BF16)
        if step + 1 < steps:
            slab = lax.dot_general(slab_of_drive[...], drive, dims, preferred_element_type=F32)
            wide = jnp.concatenate([slab[: rays // 2], slab[rays // 2 :]], axis=1)
        own[step] = current
        if step + 1 < steps:
            fresh = fresh_of[step]
            copies = near_copies(own.at[step], fresh, step + 1)
            for copy in copies:
                copy.start()
            near_all.extend(copies)
            send_slab(step + 1, wide)
            if step == 0:
                for copy in rec_copies[0]:
                    copy.wait_recv()
                for copy in rec_passed + rec_copies[1]:
                    copy.start()
            fresh[REACH] = current
        out_ref[step] = current
        if step + 1 < steps:
            for copy in copies:
                copy.wait_recv()

            def add_near(later):
                latest = [fresh[near_shift[b]] for b in range(entries)]
                latest = [
                    jnp.where(near_valid[b], x, jnp.zeros_like(x)) for b, x in enumerate(latest)
                ]
                base[later] = base[later] - jnp.dot(
                    jnp.concatenate(latest, axis=1),
                    blocks[:, later - step - 1].reshape(entries * width, size),
                    preferred_element_type=F32,
                )

            add_near(step + 1)
            send_partial(step + 1, base[step + 1].astype(BF16))
            fold(step + 1)
            for later in range(step + 2, steps):
                add_near(later)

    ringed = inv_copies + inv_passed + sum(rec_copies, rec_passed)
    for copy in slab_copies + rad_copies + ringed + near_all + sum(p_copies, []):
        copy.wait_send()
    wait_blocks(w_send, w_sems.at[0])
    for step in range(steps):
        wait_blocks(s_recv.at[step], s_sems.at[step, 0])
        wait_blocks(f_recv.at[step], f_sems.at[step, 0], None if step else chunks - 1)


def layout_of(n):
    inner = 1
    while inner * inner < n:
        inner *= 2
    return inner, max(n // (2 * inner), 1)


def solution(mesh):
    n = mesh.shape["groups"]
    m = mesh.shape["rays"]
    inner, copies_of_fold = layout_of(n)
    chunks = n // copies_of_fold

    def local(
        excitation,
        cycle,
        near_blocks,
        near_list,
        near_count,
        newest,
        inverse,
        radiate,
        translate,
        receive,
    ):
        steps, waves, width = excitation.shape
        slots = cycle.shape[0]
        entries = near_list.shape[1]
        size = m * width
        rays = receive.shape[0]
        rows = rays // (2 * chunks)
        spread = 2 * REACH + 1
        anywhere = pl.BlockSpec(memory_space=pl.ANY)
        dma = pltpu.SemaphoreType.DMA
        vmem = pltpu.VMEM
        smem = pltpu.SMEM
        return pl.pallas_call(
            functools.partial(kernel, n, inner, copies_of_fold, m),
            out_shape=pltpu.VMEM(excitation.shape, BF16),
            in_specs=[anywhere] * 10,
            out_specs=pl.BlockSpec(memory_space=vmem),
            scratch_shapes=[
                smem(near_list.shape, jnp.int32),
                smem(near_count.shape, jnp.int32),
                smem(newest.shape, jnp.int32),
                vmem(excitation.shape, BF16),
                vmem(cycle.shape, BF16),
                vmem((entries, slots, width, size), BF16),
                vmem((n, rays), F32),
                vmem(radiate.shape, BF16),
                vmem(inverse.shape, BF16),
                vmem((m, rays // 2, 2 * waves), BF16),
                vmem((m, rays // 2, 2 * waves), BF16),
                vmem((rays, size), BF16),
                vmem((size, size), BF16),
                vmem((rays, size), BF16),
                vmem((m * rays, size), BF16),
                vmem((spread, slots, waves, width), BF16),
                vmem((spread, waves, width), BF16),
                vmem((spread, waves, width), BF16),
                vmem((chunks, rows, 2 * n), F32),
                vmem((chunks, rows, 2 * n), F32),
                vmem((rows, 2 * chunks, 2 * n), BF16),
                vmem((n * rows, 2 * waves), F32),
                vmem((chunks * rows, 2 * waves), F32),
                vmem((steps, chunks, rows, 2 * waves), BF16),
                vmem((steps, n, rows, 2 * waves), BF16),
                vmem((steps, chunks, rows, 2 * waves), BF16),
                vmem((steps, m * chunks, rows, 2 * waves), BF16),
                vmem((steps, waves, size), F32),
                vmem((steps, waves, size), BF16),
                vmem((steps, m, waves, size), BF16),
                vmem((steps, waves, width), BF16),
                pltpu.SemaphoreType.REGULAR,
                dma((13,)),
                dma((7, m - 1)),
                dma((7, m - 1)),
                dma((2,)),
                dma((steps, 2)),
                dma((steps, 2)),
                dma((steps, 4)),
                dma((steps, 4)),
                dma((steps, 2, m - 1)),
            ],
            compiler_params=pltpu.CompilerParams(
                collective_id=0, has_side_effects=True, vmem_limit_bytes=56 * 1024 * 1024
            ),
        )(
            excitation,
            cycle,
            near_blocks,
            near_list,
            near_count,
            newest,
            inverse,
            radiate,
            translate,
            receive,
        )

    placed = (
        P(None, None, ("groups", "rays")),
        P(None, None, ("groups", "rays")),
        P("groups", None, None, "rays", None),
        P("groups", None),
        P("groups"),
        P(),
        P(None, ("groups", "rays")),
        P(None, ("groups", "rays")),
        P("groups", None, "rays"),
        P("rays", "groups"),
    )
    return jax.shard_map(
        local,
        mesh=mesh,
        in_specs=placed,
        out_specs=P(None, None, ("groups", "rays")),
        check_vma=False,
    )
```

```python
import functools

import jax
import jax.numpy as jnp
from jax import lax
from jax.experimental import pallas as pl
from jax.experimental.pallas import tpu as pltpu
from jax.sharding import PartitionSpec as P

REACH = 2
NEAR_SHIFTS = (-2, -1, 1, 2)
MESH = pl.DeviceIdType.MESH
F32 = jnp.float32
BF16 = jnp.bfloat16


def kernel(
    n,
    inner,
    copies_of_fold,
    m,
    exc_hbm,
    cyc_hbm,
    blocks_hbm,
    list_hbm,
    count_hbm,
    newest_hbm,
    inv_hbm,
    rad_hbm,
    tr_hbm,
    rec_hbm,
    out_ref,
    list_ref,
    count_ref,
    newest_ref,
    exc,
    cyc,
    blocks,
    tr,
    rad,
    inv,
    rs_send,
    rs_recv,
    rad_full,
    inv_full,
    slab_of_drive,
    rec_full,
    nearby,
    fresh_first,
    fresh_second,
    w_send,
    w_recv,
    w_both,
    turn_s,
    turn_f,
    s_send,
    s_recv,
    f_send,
    f_recv,
    base,
    p_send,
    p_recv,
    own,
    row_sem,
    load_sems,
    x_send,
    x_recv,
    w_sems,
    s_sems,
    f_sems,
    near_send,
    near_recv,
    p_sems,
):
    steps, waves, width = exc.shape
    slots = cyc.shape[0]
    entries = list_ref.shape[1]
    size = m * width
    rays = tr.shape[1]
    outer = n // inner
    chunks = n // copies_of_fold
    rows = rays // (2 * chunks)
    g = lax.axis_index("groups")
    r = lax.axis_index("rays")
    go = g // inner
    gi = g - go * inner
    pair = go // 2
    plane = go - 2 * pair
    chunk = plane * inner + gi
    first_target = g - chunk
    mine = pl.ds(pl.multiple_of(r * width, width), width)
    dims = (((1,), (1,)), ((), ()))
    fresh_of = (fresh_first, fresh_second)
    ray_order = sorted(range(1, m), key=lambda d: -min(d, m - d))
    inner_order = sorted(range(inner), key=lambda d: -min(d, inner - d))

    def wrap(x, limit):
        return jnp.where(x >= limit, x - limit, x)

    inner_place = [wrap(gi + d, inner) for d in range(inner)]
    ray_place = [wrap(r + d, m) for d in range(m)]

    def near_group(d):
        return wrap(g + d + n, n) if d < 0 else wrap(g + d, n)

    def other_ray(d):
        return ray_place[d]

    def remote(src, dst, send_sem, recv_sem, group, ray):
        return pltpu.make_async_remote_copy(
            src_ref=src,
            dst_ref=dst,
            send_sem=send_sem,
            recv_sem=recv_sem,
            device_id=(group, ray),
            device_id_type=MESH,
        )

    def each_peer(act):
        def body(k, carry):
            shift, change = carry
            place = wrap(go + shift, outer)
            other = place * inner
            bit = place - 2 * (place // 2)
            for d in inner_order:
                act(other + inner_place[d], bit * inner + inner_place[d])
            return shift + change, jnp.where(change < 0, 1 - change, -1 - change)

        lax.fori_loop(0, outer - 1, body, (jnp.int32(outer // 2), jnp.int32(-1)))
        for d in inner_order:
            if d:
                act(go * inner + inner_place[d], plane * inner + inner_place[d])

    def each_target(act, with_self):
        for d in inner_order:
            act((1 - plane) * inner + inner_place[d])
        for d in inner_order:
            if d or with_self:
                act(plane * inner + inner_place[d])

    def wait_blocks(like, sem, count=None):
        part = like.at[pl.ds(0, like.shape[0] - 1 if count is None else count)]
        pltpu.make_async_copy(part, part, sem).wait()

    def near_copies(src, dst, index):
        return [
            remote(
                src,
                dst.at[REACH - shift],
                near_send.at[index, k],
                near_recv.at[index, k],
                near_group(shift),
                r,
            )
            for k, shift in enumerate(NEAR_SHIFTS)
        ]

    def ray_copies(src_of, dst, index):
        return [
            remote(
                src_of(d), dst, x_send.at[index, d - 1], x_recv.at[index, d - 1], g, other_ray(d)
            )
            for d in ray_order
        ]

    rows_here = pl.ds(pl.multiple_of(r * rays, rays), rays)
    pairs = (
        (newest_hbm, newest_ref),
        (cyc_hbm, cyc),
        (rad_hbm, rad),
        (list_hbm, list_ref),
        (count_hbm, count_ref),
        (tr_hbm.at[0], tr),
        (rad_hbm.at[rows_here, :], rad_full.at[:, mine]),
        (blocks_hbm.at[0], blocks),
        (inv_hbm, inv_full.at[:, mine]),
        (inv_hbm, inv),
        (cyc_hbm, nearby.at[REACH]),
        (rec_hbm, rec_full.at[rows_here, :]),
        (exc_hbm, exc),
    )
    loads = [
        pltpu.make_async_copy(src, dst, load_sems.at[i]) for i, (src, dst) in enumerate(pairs)
    ]
    for load in loads[:3]:
        load.start()

    barrier = pltpu.get_barrier_semaphore()
    greeted = [(g, other_ray(d)) for d in ray_order]
    greeted += [(go * inner + inner_place[d], r) for d in inner_order if d]
    row_peers = [(wrap(go + d, outer) * inner + gi, r) for d in range(1, outer)]
    greeted += row_peers
    greeted += [(near_group(d), r) for d in NEAR_SHIFTS]
    for device in greeted:
        pl.semaphore_signal(barrier, inc=1, device_id=device, device_id_type=MESH)

    for load in loads[3:]:
        load.start(priority=1)
    (
        load_newest,
        load_cyc,
        load_all_rad,
        load_list,
        load_count,
        load_tr,
        load_rad,
        load_blocks,
        load_inv,
        load_own_inv,
        load_self,
        load_rec,
        load_exc,
    ) = loads

    pl.semaphore_wait(barrier, len(greeted))

    for device in row_peers:
        pl.semaphore_signal(row_sem, inc=1, device_id=device, device_id_type=MESH)
    load_newest.wait()
    load_cyc.wait()
    start_slot = newest_ref[0]
    newest_value = cyc[start_slot]
    load_all_rad.wait()
    partial_slab = lax.dot_general(rad[...], newest_value, dims, preferred_element_type=F32)
    for k in range(m):
        top, middle = k * rays, k * rays + rays // 2
        rs_send[k] = jnp.concatenate(
            [partial_slab[top:middle], partial_slab[middle : top + rays]], axis=1
        ).astype(BF16)
    slab_copies = ray_copies(lambda d: rs_send.at[other_ray(d)], rs_recv.at[r], 0)
    for copy in slab_copies:
        copy.start()
    rs_recv[r] = rs_send[r]
    cycle_copies = near_copies(cyc_hbm, nearby, 0)
    near_all = list(cycle_copies)

    load_list.wait()
    load_count.wait()
    near_shift = []
    near_valid = []
    for b in range(entries):
        shift = list_ref[0, b]
        source = g + shift - REACH
        near_shift.append(shift)
        near_valid.append((b < count_ref[0]) & (source >= 0) & (source < n))
    load_tr.wait()
    every = lax.broadcasted_iota(jnp.int32, (n, rays), 0)
    weights = tr[...]
    for b in range(entries):
        hit = near_valid[b] & (every == g + near_shift[b] - REACH)
        weights = jnp.where(hit, 0.0, weights)
    turned = weights.T
    w_rows = jnp.concatenate([turned[: rays // 2], turned[rays // 2 :]], axis=1)
    w_send[...] = w_rows.reshape(w_send.shape)

    pl.semaphore_wait(row_sem, len(row_peers))

    def send_weights(k):
        remote(
            w_send.at[k], w_recv.at[chunk], w_sems.at[0], w_sems.at[1], first_target + k, r
        ).start()

    each_target(send_weights, False)
    w_recv[chunk] = w_send[chunk]
    rad_copies = ray_copies(
        lambda d: rad_hbm.at[pl.ds(pl.multiple_of(other_ray(d) * rays, rays), rays), :],
        rad_full.at[:, mine],
        1,
    )
    near_rays = sorted({1 % m, m - 1} - {0})
    half = rays // 2

    def columns_of(ray):
        return pl.ds(pl.multiple_of(ray * width, width), width)

    def rows_of(ray, k):
        return pl.ds(pl.multiple_of(ray * rays + k * half, half), half)

    def ring_copies(part_of, index):
        copies = []
        for k, d in enumerate(near_rays):
            src, dst = part_of(d, k)
            copies.append(
                remote(src, dst, x_send.at[index, d - 1], x_recv.at[index, d - 1], g, other_ray(d))
            )
        return copies

    def inv_part(d, k):
        part = inv_full.at[pl.ds(k * (size // 2), size // 2), columns_of(other_ray(m - d))]
        return part, part

    def rec_part(d, k):
        part = rec_full.at[rows_of(other_ray(m - d), k), :]
        return part, part

    inv_copies = ring_copies(lambda d, k: (inv_hbm, inv_full.at[:, mine]), 2)
    inv_passed = ring_copies(inv_part, 3) if m == 4 else []
    rec_copies = [
        ring_copies(
            lambda d, k: (rec_hbm.at[pl.ds(k * half, half), :], rec_full.at[rows_of(r, k), :]), 4
        ),
        ring_copies(
            lambda d, k: (
                rec_hbm.at[pl.ds((1 - k) * half, half), :],
                rec_full.at[rows_of(r, 1 - k), :],
            ),
            5,
        ),
    ]
    rec_passed = ring_copies(rec_part, 6) if m == 4 else []
    p_copies = []

    def send_slab(step, wide):
        for k in range(chunks):
            s_send[step, k] = wide[k * rows : (k + 1) * rows].astype(BF16)

        def send(group, k):
            remote(
                s_send.at[step, k],
                s_recv.at[step, g],
                s_sems.at[step, 0],
                s_sems.at[step, 1],
                group,
                r,
            ).start()

        each_peer(send)
        s_recv[step, g] = s_send[step, chunk]

    def fold(step):
        wait_blocks(s_recv.at[step], s_sems.at[step, 1])
        for h in range(n):
            turn_s[h * rows : (h + 1) * rows] = s_recv[step, h].astype(F32)
        lane = lax.broadcasted_iota(jnp.int32, (n, 2 * waves), 1)
        for i in range(rows):
            slab = turn_s[pl.ds(i, n, stride=rows), :]
            wide = jnp.concatenate(
                [jnp.where(lane < waves, slab, 0.0), jnp.where(lane < waves, 0.0, slab)], axis=0
            ).astype(BF16)
            both = jnp.dot(w_both[i], wide, preferred_element_type=F32)
            turn_f[i * chunks : (i + 1) * chunks] = both[:chunks] + both[chunks:]
        for k in range(chunks):
            f_send[step, k] = turn_f[pl.ds(k, rows, stride=chunks), :].astype(BF16)
        place = r * chunks + chunk

        def send(k, ray):
            remote(
                f_send.at[step, k],
                f_recv.at[step, place],
                f_sems.at[step, 0],
                f_sems.at[step, 1 + r],
                first_target + k,
                ray,
            ).start()

        if step:
            for d in ray_order:
                each_target(lambda k, ray=other_ray(d): send(k, ray), True)
        each_target(lambda k: send(k, r), False)
        f_recv[step, place] = f_send[step, chunk]

    def send_partial(step, part):
        p_send[step] = part
        copies = [
            remote(
                p_send.at[step],
                p_recv.at[step, r],
                p_sems.at[step, 0, d - 1],
                p_sems.at[step, 1, d - 1],
                g,
                other_ray(d),
            )
            for d in ray_order
        ]
        for copy in copies:
            copy.start()
        p_copies.append(copies)
        p_recv[step, r] = part

    for copy in slab_copies:
        copy.wait_recv()
    first_slab = rs_recv[0].astype(F32)
    for k in range(1, m):
        first_slab = first_slab + rs_recv[k].astype(F32)
    send_slab(0, first_slab)
    for copy in cycle_copies + inv_copies + rad_copies:
        copy.start()

    wait_blocks(w_recv, w_sems.at[1])
    for i in range(rows):
        w_all = w_recv[:, i, :]
        w_high = w_all.astype(BF16)
        w_both[i, :chunks] = w_high
        w_both[i, chunks:] = (w_all - w_high.astype(F32)).astype(BF16)
    fold(0)
    for copy in inv_copies:
        copy.wait_recv()
    for copy in inv_passed:
        copy.start()

    load_self.wait()
    load_blocks.wait()
    load_exc.wait()
    for copy in cycle_copies:
        copy.wait_recv()
    base[...] = jnp.zeros_like(base)
    for step in range(steps):
        base[step, :, mine] = exc[step].astype(F32)

    def add_cycle(b, first, last):
        shift = list_ref[0, b]
        source = g + shift - REACH
        valid = (b < count_ref[0]) & (source >= 0) & (source < n)
        past = [
            nearby[shift, lax.rem(start_slot - i + slots, slots)] for i in range(slots - first)
        ]
        past = [jnp.where(valid, x, jnp.zeros_like(x)) for x in past]
        blank = jnp.zeros_like(past[0])
        lagged = jnp.concatenate(
            [
                jnp.concatenate([blank] * k + past[: len(past) - k], axis=1)
                for k in range(last - first)
            ],
            axis=0,
        )
        near = jnp.dot(
            lagged,
            blocks[b, first:].reshape((slots - first) * width, size),
            preferred_element_type=F32,
        )
        for k in range(last - first):
            base[first + k] = base[first + k] - near[k * waves : (k + 1) * waves]

    def add_first(b, carry):
        add_cycle(b, 0, 1)
        return carry

    def add_later(b, carry):
        add_cycle(b, 1, steps)
        return carry

    lax.fori_loop(0, entries, add_first, 0)

    def gathered_sum(step):
        for copy in p_copies[step]:
            copy.wait_recv()
        total = p_recv[step, 0].astype(F32)
        for d in range(1, m):
            total = total + p_recv[step, d].astype(F32)
        return total

    def turn_field(pieces):
        turned = jnp.concatenate([x.astype(F32) for x in pieces], axis=0).T.astype(BF16)
        span = rays // 2
        return jnp.concatenate(
            [
                turned[p * waves : (p + 1) * waves, k * span : (k + 1) * span]
                for k in range(len(pieces) // chunks)
                for p in range(2)
            ],
            axis=1,
        )

    for step in range(steps):
        if step == 0:
            load_rec.wait()
            wait_blocks(f_recv.at[0], f_sems.at[0, 1 + r], chunks - 1)
            field = turn_field([f_recv[0, r * chunks + k] for k in range(chunks)])
            far = jnp.dot(field, rec_full[rows_here, :], preferred_element_type=F32)
            send_partial(0, (base[0] - far).astype(BF16))
            for copy in rec_copies[0]:
                copy.start()
            load_rad.wait()
            load_inv.wait()
            load_own_inv.wait()
            for copy in rad_copies + inv_passed:
                copy.wait_recv()
            slab_of_drive[...] = lax.dot_general(
                rad_full[...], inv_full[...], dims, preferred_element_type=F32
            ).astype(BF16)
            lax.fori_loop(0, entries, add_later, 0)
            drive = gathered_sum(0).astype(BF16)
        else:
            total = gathered_sum(step)
            if step == 1:
                for copy in rec_copies[1] + rec_passed:
                    copy.wait_recv()
            for d in ray_order + [0]:
                plane_ray = other_ray(d)
                wait_blocks(
                    f_recv.at[step], f_sems.at[step, 1 + plane_ray], chunks if d else chunks - 1
                )
                field = turn_field([f_recv[step, plane_ray * chunks + k] for k in range(chunks)])
                start = pl.multiple_of(plane_ray * rays, rays)
                total = total - jnp.dot(
                    field, rec_full[pl.ds(start, rays), :], preferred_element_type=F32
                )
            drive = total.astype(BF16)
        current = jnp.dot(drive, inv[...], preferred_element_type=F32).astype(BF16)
        if step + 1 < steps:
            slab = lax.dot_general(slab_of_drive[...], drive, dims, preferred_element_type=F32)
            wide = jnp.concatenate([slab[: rays // 2], slab[rays // 2 :]], axis=1)
        own[step] = current
        if step + 1 < steps:
            fresh = fresh_of[step]
            copies = near_copies(own.at[step], fresh, step + 1)
            for copy in copies:
                copy.start()
            near_all.extend(copies)
            send_slab(step + 1, wide)
            if step == 0:
                for copy in rec_copies[0]:
                    copy.wait_recv()
                for copy in rec_passed + rec_copies[1]:
                    copy.start()
            fresh[REACH] = current
        out_ref[step] = current
        if step + 1 < steps:
            for copy in copies:
                copy.wait_recv()

            def add_near(later):
                latest = [fresh[near_shift[b]] for b in range(entries)]
                latest = [
                    jnp.where(near_valid[b], x, jnp.zeros_like(x)) for b, x in enumerate(latest)
                ]
                base[later] = base[later] - jnp.dot(
                    jnp.concatenate(latest, axis=1),
                    blocks[:, later - step - 1].reshape(entries * width, size),
                    preferred_element_type=F32,
                )

            add_near(step + 1)
            send_partial(step + 1, base[step + 1].astype(BF16))
            fold(step + 1)
            for later in range(step + 2, steps):
                add_near(later)

    ringed = inv_copies + inv_passed + sum(rec_copies, rec_passed)
    for copy in slab_copies + rad_copies + ringed + near_all + sum(p_copies, []):
        copy.wait_send()
    wait_blocks(w_send, w_sems.at[0])
    for step in range(steps):
        wait_blocks(s_recv.at[step], s_sems.at[step, 0])
        wait_blocks(f_recv.at[step], f_sems.at[step, 0], None if step else chunks - 1)


def layout_of(n):
    inner = 1
    while inner * inner < n:
        inner *= 2
    return inner, max(n // (2 * inner), 1)


def solution(mesh):
    n = mesh.shape["groups"]
    m = mesh.shape["rays"]
    inner, copies_of_fold = layout_of(n)
    chunks = n // copies_of_fold

    def local(
        excitation,
        cycle,
        near_blocks,
        near_list,
        near_count,
        newest,
        inverse,
        radiate,
        translate,
        receive,
    ):
        steps, waves, width = excitation.shape
        slots = cycle.shape[0]
        entries = near_list.shape[1]
        size = m * width
        rays = receive.shape[0]
        rows = rays // (2 * chunks)
        spread = 2 * REACH + 1
        anywhere = pl.BlockSpec(memory_space=pl.ANY)
        dma = pltpu.SemaphoreType.DMA
        vmem = pltpu.VMEM
        smem = pltpu.SMEM
        return pl.pallas_call(
            functools.partial(kernel, n, inner, copies_of_fold, m),
            out_shape=pltpu.VMEM(excitation.shape, BF16),
            in_specs=[anywhere] * 10,
            out_specs=pl.BlockSpec(memory_space=vmem),
            scratch_shapes=[
                smem(near_list.shape, jnp.int32),
                smem(near_count.shape, jnp.int32),
                smem(newest.shape, jnp.int32),
                vmem(excitation.shape, BF16),
                vmem(cycle.shape, BF16),
                vmem((entries, slots, width, size), BF16),
                vmem((n, rays), F32),
                vmem(radiate.shape, BF16),
                vmem(inverse.shape, BF16),
                vmem((m, rays // 2, 2 * waves), BF16),
                vmem((m, rays // 2, 2 * waves), BF16),
                vmem((rays, size), BF16),
                vmem((size, size), BF16),
                vmem((rays, size), BF16),
                vmem((m * rays, size), BF16),
                vmem((spread, slots, waves, width), BF16),
                vmem((spread, waves, width), BF16),
                vmem((spread, waves, width), BF16),
                vmem((chunks, rows, 2 * n), F32),
                vmem((chunks, rows, 2 * n), F32),
                vmem((rows, 2 * chunks, 2 * n), BF16),
                vmem((n * rows, 2 * waves), F32),
                vmem((chunks * rows, 2 * waves), F32),
                vmem((steps, chunks, rows, 2 * waves), BF16),
                vmem((steps, n, rows, 2 * waves), BF16),
                vmem((steps, chunks, rows, 2 * waves), BF16),
                vmem((steps, m * chunks, rows, 2 * waves), BF16),
                vmem((steps, waves, size), F32),
                vmem((steps, waves, size), BF16),
                vmem((steps, m, waves, size), BF16),
                vmem((steps, waves, width), BF16),
                pltpu.SemaphoreType.REGULAR,
                dma((13,)),
                dma((7, m - 1)),
                dma((7, m - 1)),
                dma((2,)),
                dma((steps, 2)),
                dma((steps, 1 + m)),
                dma((steps, 4)),
                dma((steps, 4)),
                dma((steps, 2, m - 1)),
            ],
            compiler_params=pltpu.CompilerParams(
                collective_id=0, has_side_effects=True, vmem_limit_bytes=56 * 1024 * 1024
            ),
        )(
            excitation,
            cycle,
            near_blocks,
            near_list,
            near_count,
            newest,
            inverse,
            radiate,
            translate,
            receive,
        )

    placed = (
        P(None, None, ("groups", "rays")),
        P(None, None, ("groups", "rays")),
        P("groups", None, None, "rays", None),
        P("groups", None),
        P("groups"),
        P(),
        P(None, ("groups", "rays")),
        P(None, ("groups", "rays")),
        P("groups", None, "rays"),
        P("rays", "groups"),
    )
    return jax.shard_map(
        local,
        mesh=mesh,
        in_specs=placed,
        out_specs=P(None, None, ("groups", "rays")),
        check_vma=False,
    )
```

```python
import functools

import jax
import jax.numpy as jnp
from jax import lax
from jax.experimental import pallas as pl
from jax.experimental.pallas import tpu as pltpu
from jax.sharding import PartitionSpec as P

REACH = 2
NEAR_SHIFTS = (-2, -1, 1, 2)
MESH = pl.DeviceIdType.MESH
F32 = jnp.float32
BF16 = jnp.bfloat16


def kernel(
    n,
    inner,
    copies_of_fold,
    m,
    exc_hbm,
    cyc_hbm,
    blocks_hbm,
    list_hbm,
    count_hbm,
    newest_hbm,
    inv_hbm,
    rad_hbm,
    tr_hbm,
    rec_hbm,
    out_ref,
    list_ref,
    count_ref,
    newest_ref,
    exc,
    cyc,
    blocks,
    tr,
    rad,
    inv,
    rs_send,
    rs_recv,
    rad_full,
    inv_full,
    slab_of_drive,
    rec_full,
    slab_of_field,
    current_of_field,
    nearby,
    fresh_first,
    fresh_second,
    w_send,
    w_recv,
    w_both,
    turn_s,
    turn_f,
    s_send,
    s_recv,
    f_send,
    f_recv,
    base,
    p_send,
    p_recv,
    own,
    row_sem,
    load_sems,
    x_send,
    x_recv,
    w_sems,
    s_sems,
    f_sems,
    near_send,
    near_recv,
    p_sems,
):
    steps, waves, width = exc.shape
    slots = cyc.shape[0]
    entries = list_ref.shape[1]
    size = m * width
    rays = tr.shape[1]
    outer = n // inner
    chunks = n // copies_of_fold
    rows = rays // (2 * chunks)
    g = lax.axis_index("groups")
    r = lax.axis_index("rays")
    go = g // inner
    gi = g - go * inner
    pair = go // 2
    plane = go - 2 * pair
    chunk = plane * inner + gi
    first_target = g - chunk
    mine = pl.ds(pl.multiple_of(r * width, width), width)
    dims = (((1,), (1,)), ((), ()))
    fresh_of = (fresh_first, fresh_second)
    ray_order = sorted(range(1, m), key=lambda d: -min(d, m - d))
    inner_order = sorted(range(inner), key=lambda d: -min(d, inner - d))

    def wrap(x, limit):
        return jnp.where(x >= limit, x - limit, x)

    inner_place = [wrap(gi + d, inner) for d in range(inner)]
    ray_place = [wrap(r + d, m) for d in range(m)]

    def near_group(d):
        return wrap(g + d + n, n) if d < 0 else wrap(g + d, n)

    def other_ray(d):
        return ray_place[d]

    def remote(src, dst, send_sem, recv_sem, group, ray):
        return pltpu.make_async_remote_copy(
            src_ref=src,
            dst_ref=dst,
            send_sem=send_sem,
            recv_sem=recv_sem,
            device_id=(group, ray),
            device_id_type=MESH,
        )

    def each_peer(act):
        def body(k, carry):
            shift, change = carry
            place = wrap(go + shift, outer)
            other = place * inner
            bit = place - 2 * (place // 2)
            for d in inner_order:
                act(other + inner_place[d], bit * inner + inner_place[d])
            return shift + change, jnp.where(change < 0, 1 - change, -1 - change)

        lax.fori_loop(0, outer - 1, body, (jnp.int32(outer // 2), jnp.int32(-1)))
        for d in inner_order:
            if d:
                act(go * inner + inner_place[d], plane * inner + inner_place[d])

    def each_target(act, with_self):
        for d in inner_order:
            act((1 - plane) * inner + inner_place[d])
        for d in inner_order:
            if d or with_self:
                act(plane * inner + inner_place[d])

    def wait_blocks(like, sem, count=None):
        part = like.at[pl.ds(0, like.shape[0] - 1 if count is None else count)]
        pltpu.make_async_copy(part, part, sem).wait()

    def near_copies(src, dst, index):
        return [
            remote(
                src,
                dst.at[REACH - shift],
                near_send.at[index, k],
                near_recv.at[index, k],
                near_group(shift),
                r,
            )
            for k, shift in enumerate(NEAR_SHIFTS)
        ]

    def ray_copies(src_of, dst, index):
        return [
            remote(
                src_of(d), dst, x_send.at[index, d - 1], x_recv.at[index, d - 1], g, other_ray(d)
            )
            for d in ray_order
        ]

    rows_here = pl.ds(pl.multiple_of(r * rays, rays), rays)
    pairs = (
        (newest_hbm, newest_ref),
        (cyc_hbm, cyc),
        (rad_hbm, rad),
        (list_hbm, list_ref),
        (count_hbm, count_ref),
        (tr_hbm.at[0], tr),
        (rad_hbm.at[rows_here, :], rad_full.at[:, mine]),
        (blocks_hbm.at[0], blocks),
        (inv_hbm, inv_full.at[:, mine]),
        (inv_hbm, inv),
        (cyc_hbm, nearby.at[REACH]),
        (rec_hbm, rec_full.at[rows_here, :]),
        (exc_hbm, exc),
    )
    loads = [
        pltpu.make_async_copy(src, dst, load_sems.at[i]) for i, (src, dst) in enumerate(pairs)
    ]
    for load in loads[:3]:
        load.start()

    barrier = pltpu.get_barrier_semaphore()
    greeted = [(g, other_ray(d)) for d in ray_order]
    greeted += [(go * inner + inner_place[d], r) for d in inner_order if d]
    row_peers = [(wrap(go + d, outer) * inner + gi, r) for d in range(1, outer)]
    greeted += row_peers
    greeted += [(near_group(d), r) for d in NEAR_SHIFTS]
    for device in greeted:
        pl.semaphore_signal(barrier, inc=1, device_id=device, device_id_type=MESH)

    for load in loads[3:]:
        load.start(priority=1)
    (
        load_newest,
        load_cyc,
        load_all_rad,
        load_list,
        load_count,
        load_tr,
        load_rad,
        load_blocks,
        load_inv,
        load_own_inv,
        load_self,
        load_rec,
        load_exc,
    ) = loads

    pl.semaphore_wait(barrier, len(greeted))

    for device in row_peers:
        pl.semaphore_signal(row_sem, inc=1, device_id=device, device_id_type=MESH)
    load_newest.wait()
    load_cyc.wait()
    start_slot = newest_ref[0]
    newest_value = cyc[start_slot]
    load_all_rad.wait()
    slab_copies = ray_copies(lambda d: rs_send.at[other_ray(d)], rs_recv.at[r], 0)
    for d, copy in zip(ray_order + [0], slab_copies + [None]):
        ray = other_ray(d)
        block = rad[pl.ds(pl.multiple_of(ray * rays, rays), rays), :]
        block = lax.dot_general(block, newest_value, dims, preferred_element_type=F32)
        block = jnp.concatenate([block[: rays // 2], block[rays // 2 :]], axis=1).astype(BF16)
        if copy is None:
            rs_recv[r] = block
        else:
            rs_send[ray] = block
            copy.start()
    cycle_copies = near_copies(cyc_hbm, nearby, 0)
    near_all = list(cycle_copies)

    load_list.wait()
    load_count.wait()
    near_shift = []
    near_valid = []
    for b in range(entries):
        shift = list_ref[0, b]
        source = g + shift - REACH
        near_shift.append(shift)
        near_valid.append((b < count_ref[0]) & (source >= 0) & (source < n))
    load_tr.wait()
    every = lax.broadcasted_iota(jnp.int32, (n, rays), 0)
    weights = tr[...]
    for b in range(entries):
        hit = near_valid[b] & (every == g + near_shift[b] - REACH)
        weights = jnp.where(hit, 0.0, weights)
    turned = weights.T
    w_rows = jnp.concatenate([turned[: rays // 2], turned[rays // 2 :]], axis=1)
    w_send[...] = w_rows.reshape(w_send.shape)

    pl.semaphore_wait(row_sem, len(row_peers))

    def send_weights(k):
        remote(
            w_send.at[k], w_recv.at[chunk], w_sems.at[0], w_sems.at[1], first_target + k, r
        ).start()

    each_target(send_weights, False)
    w_recv[chunk] = w_send[chunk]
    rad_copies = ray_copies(
        lambda d: rad_hbm.at[pl.ds(pl.multiple_of(other_ray(d) * rays, rays), rays), :],
        rad_full.at[:, mine],
        1,
    )
    near_rays = sorted({1 % m, m - 1} - {0})
    half = rays // 2

    def columns_of(ray):
        return pl.ds(pl.multiple_of(ray * width, width), width)

    def rows_of(ray, k):
        return pl.ds(pl.multiple_of(ray * rays + k * half, half), half)

    def ring_copies(part_of, index):
        copies = []
        for k, d in enumerate(near_rays):
            src, dst = part_of(d, k)
            copies.append(
                remote(src, dst, x_send.at[index, d - 1], x_recv.at[index, d - 1], g, other_ray(d))
            )
        return copies

    def inv_part(d, k):
        part = inv_full.at[pl.ds(k * (size // 2), size // 2), columns_of(other_ray(m - d))]
        return part, part

    def rec_part(d, k):
        part = rec_full.at[rows_of(other_ray(m - d), k), :]
        return part, part

    inv_copies = ring_copies(lambda d, k: (inv_hbm, inv_full.at[:, mine]), 2)
    inv_passed = ring_copies(inv_part, 3) if m == 4 else []
    rec_copies = [
        ring_copies(
            lambda d, k: (rec_hbm.at[pl.ds(k * half, half), :], rec_full.at[rows_of(r, k), :]), 4
        ),
        ring_copies(
            lambda d, k: (
                rec_hbm.at[pl.ds((1 - k) * half, half), :],
                rec_full.at[rows_of(r, 1 - k), :],
            ),
            5,
        ),
    ]
    rec_passed = ring_copies(rec_part, 6) if m == 4 else []
    p_copies = []

    def send_slab(step, wide):
        for k in range(chunks):
            s_send[step, k] = wide[k * rows : (k + 1) * rows].astype(BF16)

        def send(group, k):
            remote(
                s_send.at[step, k],
                s_recv.at[step, g],
                s_sems.at[step, 0],
                s_sems.at[step, 1],
                group,
                r,
            ).start()

        each_peer(send)
        s_recv[step, g] = s_send[step, chunk]

    def fold(step):
        wait_blocks(s_recv.at[step], s_sems.at[step, 1])
        for h in range(n):
            turn_s[h * rows : (h + 1) * rows] = s_recv[step, h].astype(F32)
        lane = lax.broadcasted_iota(jnp.int32, (n, 2 * waves), 1)
        for i in range(rows):
            slab = turn_s[pl.ds(i, n, stride=rows), :]
            wide = jnp.concatenate(
                [jnp.where(lane < waves, slab, 0.0), jnp.where(lane < waves, 0.0, slab)], axis=0
            ).astype(BF16)
            both = jnp.dot(w_both[i], wide, preferred_element_type=F32)
            turn_f[i * chunks : (i + 1) * chunks] = both[:chunks] + both[chunks:]
        for k in range(chunks):
            f_send[step, k] = turn_f[pl.ds(k, rows, stride=chunks), :].astype(BF16)
        place = r * chunks + chunk

        def send(k, ray):
            remote(
                f_send.at[step, k],
                f_recv.at[step, place],
                f_sems.at[step, 0],
                f_sems.at[step, 1],
                first_target + k,
                ray,
            ).start()

        if step and m > 1:

            def body(k, carry):
                d = jnp.where(k == 0, m // 2, jnp.where(k == 1, 1, m - 1))
                ray = wrap(r + d, m)
                each_target(lambda k: send(k, ray), True)
                return carry

            lax.fori_loop(0, m - 1, body, 0)
        each_target(lambda k: send(k, r), False)
        f_recv[step, place] = f_send[step, chunk]

    def send_partial(step, part):
        p_send[step] = part
        copies = [
            remote(
                p_send.at[step],
                p_recv.at[step, r],
                p_sems.at[step, 0, d - 1],
                p_sems.at[step, 1, d - 1],
                g,
                other_ray(d),
            )
            for d in ray_order
        ]
        for copy in copies:
            copy.start()
        p_copies.append(copies)
        p_recv[step, r] = part

    for copy in slab_copies:
        copy.wait_recv()
    first_slab = rs_recv[0].astype(F32)
    for k in range(1, m):
        first_slab = first_slab + rs_recv[k].astype(F32)
    send_slab(0, first_slab)
    for copy in cycle_copies + inv_copies + rad_copies:
        copy.start()

    wait_blocks(w_recv, w_sems.at[1])
    for i in range(rows):
        w_all = w_recv[:, i, :]
        w_high = w_all.astype(BF16)
        w_both[i, :chunks] = w_high
        w_both[i, chunks:] = (w_all - w_high.astype(F32)).astype(BF16)
    fold(0)
    for copy in inv_copies:
        copy.wait_recv()
    for copy in inv_passed:
        copy.start()

    load_self.wait()
    load_blocks.wait()
    load_exc.wait()
    for copy in cycle_copies:
        copy.wait_recv()
    base[...] = jnp.zeros_like(base)
    for step in range(steps):
        base[step, :, mine] = exc[step].astype(F32)

    def add_cycle(b, carry):
        shift = list_ref[0, b]
        source = g + shift - REACH
        valid = (b < count_ref[0]) & (source >= 0) & (source < n)
        past = [nearby[shift, lax.rem(start_slot - i + slots, slots)] for i in range(slots)]
        past = [jnp.where(valid, x, jnp.zeros_like(x)) for x in past]
        blank = jnp.zeros_like(past[0])
        lagged = jnp.concatenate(
            [
                jnp.concatenate([blank] * step + past[: slots - step], axis=1)
                for step in range(steps)
            ],
            axis=0,
        )
        near = jnp.dot(
            lagged, blocks[b].reshape(slots * width, size), preferred_element_type=F32
        )
        for step in range(steps):
            base[step] = base[step] - near[step * waves : (step + 1) * waves]
        return carry


    lax.fori_loop(0, entries, add_cycle, 0)

    def gathered_sum(step):
        for copy in p_copies[step]:
            copy.wait_recv()
        total = p_recv[step, 0].astype(F32)
        for d in range(1, m):
            total = total + p_recv[step, d].astype(F32)
        return total

    def turn_field(pieces):
        turned = jnp.concatenate([x.astype(F32) for x in pieces], axis=0).T.astype(BF16)
        span = rays // 2
        return jnp.concatenate(
            [
                turned[p * waves : (p + 1) * waves, k * span : (k + 1) * span]
                for k in range(len(pieces) // chunks)
                for p in range(2)
            ],
            axis=1,
        )

    for step in range(steps):
        more = step + 1 < steps
        if step == 0:
            load_rec.wait()
            wait_blocks(f_recv.at[0], f_sems.at[0, 1], chunks - 1)
            field = turn_field([f_recv[0, r * chunks + k] for k in range(chunks)])
            far = jnp.dot(field, rec_full[rows_here, :], preferred_element_type=F32)
            send_partial(0, (base[0] - far).astype(BF16))
            for copy in rec_copies[0]:
                copy.start()
            load_rad.wait()
            load_inv.wait()
            load_own_inv.wait()
            for copy in rad_copies + inv_passed:
                copy.wait_recv()
            slab_of_drive[...] = lax.dot_general(
                rad_full[...], inv_full[...], dims, preferred_element_type=F32
            ).astype(BF16)
            drive = gathered_sum(0).astype(BF16)
            current = jnp.dot(drive, inv[...], preferred_element_type=F32).astype(BF16)
            slab = lax.dot_general(slab_of_drive[...], drive, dims, preferred_element_type=F32)
        else:
            if step == 1:
                for copy in rec_copies[1] + rec_passed:
                    copy.wait_recv()
                current_of_field[...] = jnp.dot(
                    rec_full[...], inv[...], preferred_element_type=F32
                ).astype(BF16)
                slab_of_field[...] = lax.dot_general(
                    slab_of_drive[...], rec_full[...], dims, preferred_element_type=F32
                ).astype(BF16)
            known = gathered_sum(step).astype(BF16)
            current = jnp.dot(known, inv[...], preferred_element_type=F32)
            if more:
                slab = lax.dot_general(slab_of_drive[...], known, dims, preferred_element_type=F32)
            wait_blocks(f_recv.at[step], f_sems.at[step, 1])
            field = turn_field([f_recv[step, k] for k in range(m * chunks)])
            current = (
                current - jnp.dot(field, current_of_field[...], preferred_element_type=F32)
            ).astype(BF16)
            if more:
                slab = slab - lax.dot_general(
                    slab_of_field[...], field, dims, preferred_element_type=F32
                )
        if more:
            wide = jnp.concatenate([slab[: rays // 2], slab[rays // 2 :]], axis=1)
        own[step] = current
        if step + 1 < steps:
            fresh = fresh_of[step]
            copies = near_copies(own.at[step], fresh, step + 1)
            for copy in copies:
                copy.start()
            near_all.extend(copies)
            send_slab(step + 1, wide)
            if step == 0:
                for copy in rec_copies[0]:
                    copy.wait_recv()
                for copy in rec_passed + rec_copies[1]:
                    copy.start()
            fresh[REACH] = current
        out_ref[step] = current
        if step + 1 < steps:
            for copy in copies:
                copy.wait_recv()

            def add_near(later):
                latest = [fresh[near_shift[b]] for b in range(entries)]
                latest = [
                    jnp.where(near_valid[b], x, jnp.zeros_like(x)) for b, x in enumerate(latest)
                ]
                base[later] = base[later] - jnp.dot(
                    jnp.concatenate(latest, axis=1),
                    blocks[:, later - step - 1].reshape(entries * width, size),
                    preferred_element_type=F32,
                )

            add_near(step + 1)
            send_partial(step + 1, base[step + 1].astype(BF16))
            fold(step + 1)
            for later in range(step + 2, steps):
                add_near(later)

    ringed = inv_copies + inv_passed + sum(rec_copies, rec_passed)
    for copy in slab_copies + rad_copies + ringed + near_all + sum(p_copies, []):
        copy.wait_send()
    wait_blocks(w_send, w_sems.at[0])
    for step in range(steps):
        wait_blocks(s_recv.at[step], s_sems.at[step, 0])
        wait_blocks(f_recv.at[step], f_sems.at[step, 0], None if step else chunks - 1)


def layout_of(n):
    inner = 1
    while inner * inner < n:
        inner *= 2
    return inner, max(n // (2 * inner), 1)


def solution(mesh):
    n = mesh.shape["groups"]
    m = mesh.shape["rays"]
    inner, copies_of_fold = layout_of(n)
    chunks = n // copies_of_fold

    def local(
        excitation,
        cycle,
        near_blocks,
        near_list,
        near_count,
        newest,
        inverse,
        radiate,
        translate,
        receive,
    ):
        steps, waves, width = excitation.shape
        slots = cycle.shape[0]
        entries = near_list.shape[1]
        size = m * width
        rays = receive.shape[0]
        rows = rays // (2 * chunks)
        spread = 2 * REACH + 1
        anywhere = pl.BlockSpec(memory_space=pl.ANY)
        dma = pltpu.SemaphoreType.DMA
        vmem = pltpu.VMEM
        smem = pltpu.SMEM
        return pl.pallas_call(
            functools.partial(kernel, n, inner, copies_of_fold, m),
            out_shape=pltpu.VMEM(excitation.shape, BF16),
            in_specs=[anywhere] * 10,
            out_specs=pl.BlockSpec(memory_space=vmem),
            scratch_shapes=[
                smem(near_list.shape, jnp.int32),
                smem(near_count.shape, jnp.int32),
                smem(newest.shape, jnp.int32),
                vmem(excitation.shape, BF16),
                vmem(cycle.shape, BF16),
                vmem((entries, slots, width, size), BF16),
                vmem((n, rays), F32),
                vmem(radiate.shape, BF16),
                vmem(inverse.shape, BF16),
                vmem((m, rays // 2, 2 * waves), BF16),
                vmem((m, rays // 2, 2 * waves), BF16),
                vmem((rays, size), BF16),
                vmem((size, size), BF16),
                vmem((rays, size), BF16),
                vmem((m * rays, size), BF16),
                vmem((rays, m * rays), BF16),
                vmem((m * rays, width), BF16),
                vmem((spread, slots, waves, width), BF16),
                vmem((spread, waves, width), BF16),
                vmem((spread, waves, width), BF16),
                vmem((chunks, rows, 2 * n), F32),
                vmem((chunks, rows, 2 * n), F32),
                vmem((rows, 2 * chunks, 2 * n), BF16),
                vmem((n * rows, 2 * waves), F32),
                vmem((chunks * rows, 2 * waves), F32),
                vmem((steps, chunks, rows, 2 * waves), BF16),
                vmem((steps, n, rows, 2 * waves), BF16),
                vmem((steps, chunks, rows, 2 * waves), BF16),
                vmem((steps, m * chunks, rows, 2 * waves), BF16),
                vmem((steps, waves, size), F32),
                vmem((steps, waves, size), BF16),
                vmem((steps, m, waves, size), BF16),
                vmem((steps, waves, width), BF16),
                pltpu.SemaphoreType.REGULAR,
                dma((13,)),
                dma((7, m - 1)),
                dma((7, m - 1)),
                dma((2,)),
                dma((steps, 2)),
                dma((steps, 2)),
                dma((steps, 4)),
                dma((steps, 4)),
                dma((steps, 2, m - 1)),
            ],
            compiler_params=pltpu.CompilerParams(
                collective_id=0, has_side_effects=True, vmem_limit_bytes=56 * 1024 * 1024
            ),
        )(
            excitation,
            cycle,
            near_blocks,
            near_list,
            near_count,
            newest,
            inverse,
            radiate,
            translate,
            receive,
        )

    placed = (
        P(None, None, ("groups", "rays")),
        P(None, None, ("groups", "rays")),
        P("groups", None, None, "rays", None),
        P("groups", None),
        P("groups"),
        P(),
        P(None, ("groups", "rays")),
        P(None, ("groups", "rays")),
        P("groups", None, "rays"),
        P("rays", "groups"),
    )
    return jax.shard_map(
        local,
        mesh=mesh,
        in_specs=placed,
        out_specs=P(None, None, ("groups", "rays")),
        check_vma=False,
    )
```

```python
import functools

import jax
import jax.numpy as jnp
from jax import lax
from jax.experimental import pallas as pl
from jax.experimental.pallas import tpu as pltpu
from jax.sharding import PartitionSpec as P

REACH = 2
NEAR_SHIFTS = (-2, -1, 1, 2)
MESH = pl.DeviceIdType.MESH
F32 = jnp.float32
BF16 = jnp.bfloat16


def kernel(
    n,
    inner,
    copies_of_fold,
    m,
    exc_hbm,
    cyc_hbm,
    blocks_hbm,
    list_hbm,
    count_hbm,
    newest_hbm,
    inv_hbm,
    rad_hbm,
    tr_hbm,
    rec_hbm,
    out_ref,
    list_ref,
    count_ref,
    newest_ref,
    exc,
    cyc,
    blocks,
    tr,
    rad,
    inv,
    rs_send,
    rs_recv,
    rad_full,
    inv_full,
    slab_of_drive,
    rec_full,
    slab_of_field,
    current_of_field,
    nearby,
    fresh_first,
    fresh_second,
    w_send,
    w_recv,
    w_both,
    turn_s,
    turn_f,
    s_send,
    s_recv,
    f_send,
    f_recv,
    base,
    p_send,
    p_recv,
    own,
    row_sem,
    load_sems,
    x_send,
    x_recv,
    w_sems,
    s_sems,
    f_sems,
    near_send,
    near_recv,
    p_sems,
):
    steps, waves, width = exc.shape
    slots = cyc.shape[0]
    entries = list_ref.shape[1]
    size = m * width
    rays = tr.shape[1]
    outer = n // inner
    chunks = n // copies_of_fold
    rows = rays // (2 * chunks)
    g = lax.axis_index("groups")
    r = lax.axis_index("rays")
    go = g // inner
    gi = g - go * inner
    pair = go // 2
    plane = go - 2 * pair
    chunk = plane * inner + gi
    first_target = g - chunk
    mine = pl.ds(pl.multiple_of(r * width, width), width)
    dims = (((1,), (1,)), ((), ()))
    fresh_of = (fresh_first, fresh_second)
    ray_order = sorted(range(1, m), key=lambda d: -min(d, m - d))
    inner_order = sorted(range(inner), key=lambda d: -min(d, inner - d))

    def wrap(x, limit):
        return jnp.where(x >= limit, x - limit, x)

    inner_place = [wrap(gi + d, inner) for d in range(inner)]
    ray_place = [wrap(r + d, m) for d in range(m)]

    def near_group(d):
        return wrap(g + d + n, n) if d < 0 else wrap(g + d, n)

    def other_ray(d):
        return ray_place[d]

    def remote(src, dst, send_sem, recv_sem, group, ray):
        return pltpu.make_async_remote_copy(
            src_ref=src,
            dst_ref=dst,
            send_sem=send_sem,
            recv_sem=recv_sem,
            device_id=(group, ray),
            device_id_type=MESH,
        )

    def each_peer(act):
        def body(k, carry):
            shift, change = carry
            place = wrap(go + shift, outer)
            other = place * inner
            bit = place - 2 * (place // 2)
            for d in inner_order:
                act(other + inner_place[d], bit * inner + inner_place[d])
            return shift + change, jnp.where(change < 0, 1 - change, -1 - change)

        lax.fori_loop(0, outer - 1, body, (jnp.int32(outer // 2), jnp.int32(-1)))
        for d in inner_order:
            if d:
                act(go * inner + inner_place[d], plane * inner + inner_place[d])

    def each_target(act, with_self):
        for d in inner_order:
            act((1 - plane) * inner + inner_place[d])
        for d in inner_order:
            if d or with_self:
                act(plane * inner + inner_place[d])

    def wait_blocks(like, sem, count=None):
        part = like.at[pl.ds(0, like.shape[0] - 1 if count is None else count)]
        pltpu.make_async_copy(part, part, sem).wait()

    def near_copies(src, dst, index):
        return [
            remote(
                src,
                dst.at[REACH - shift],
                near_send.at[index, k],
                near_recv.at[index, k],
                near_group(shift),
                r,
            )
            for k, shift in enumerate(NEAR_SHIFTS)
        ]

    def ray_copies(src_of, dst, index):
        return [
            remote(
                src_of(d), dst, x_send.at[index, d - 1], x_recv.at[index, d - 1], g, other_ray(d)
            )
            for d in ray_order
        ]

    rows_here = pl.ds(pl.multiple_of(r * rays, rays), rays)
    pairs = (
        (newest_hbm, newest_ref),
        (cyc_hbm, cyc),
        (rad_hbm, rad),
        (list_hbm, list_ref),
        (count_hbm, count_ref),
        (tr_hbm.at[0], tr),
        (rad_hbm.at[rows_here, :], rad_full.at[:, mine]),
        (blocks_hbm.at[0], blocks),
        (inv_hbm, inv_full.at[:, mine]),
        (inv_hbm, inv),
        (cyc_hbm, nearby.at[REACH]),
        (rec_hbm, rec_full.at[rows_here, :]),
        (exc_hbm, exc),
    )
    loads = [
        pltpu.make_async_copy(src, dst, load_sems.at[i]) for i, (src, dst) in enumerate(pairs)
    ]
    for load in loads[:3]:
        load.start()

    barrier = pltpu.get_barrier_semaphore()
    greeted = [(g, other_ray(d)) for d in ray_order]
    greeted += [(go * inner + inner_place[d], r) for d in inner_order if d]
    row_peers = [(wrap(go + d, outer) * inner + gi, r) for d in range(1, outer)]
    greeted += row_peers
    greeted += [(near_group(d), r) for d in NEAR_SHIFTS]
    for device in greeted:
        pl.semaphore_signal(barrier, inc=1, device_id=device, device_id_type=MESH)

    for load in loads[3:]:
        load.start(priority=1)
    (
        load_newest,
        load_cyc,
        load_all_rad,
        load_list,
        load_count,
        load_tr,
        load_rad,
        load_blocks,
        load_inv,
        load_own_inv,
        load_self,
        load_rec,
        load_exc,
    ) = loads

    pl.semaphore_wait(barrier, len(greeted))

    for device in row_peers:
        pl.semaphore_signal(row_sem, inc=1, device_id=device, device_id_type=MESH)
    load_newest.wait()
    load_cyc.wait()
    start_slot = newest_ref[0]
    newest_value = cyc[start_slot]
    load_all_rad.wait()
    slab_copies = ray_copies(lambda d: rs_send.at[other_ray(d)], rs_recv.at[r], 0)
    for d, copy in zip(ray_order + [0], slab_copies + [None]):
        ray = other_ray(d)
        block = rad[pl.ds(pl.multiple_of(ray * rays, rays), rays), :]
        block = lax.dot_general(block, newest_value, dims, preferred_element_type=F32)
        block = jnp.concatenate([block[: rays // 2], block[rays // 2 :]], axis=1).astype(BF16)
        if copy is None:
            rs_recv[r] = block
        else:
            rs_send[ray] = block
            copy.start()
    cycle_copies = near_copies(cyc_hbm, nearby, 0)
    near_all = list(cycle_copies)

    load_list.wait()
    load_count.wait()
    near_shift = []
    near_valid = []
    for b in range(entries):
        shift = list_ref[0, b]
        source = g + shift - REACH
        near_shift.append(shift)
        near_valid.append((b < count_ref[0]) & (source >= 0) & (source < n))
    load_tr.wait()
    every = lax.broadcasted_iota(jnp.int32, (n, rays), 0)
    weights = tr[...]
    for b in range(entries):
        hit = near_valid[b] & (every == g + near_shift[b] - REACH)
        weights = jnp.where(hit, 0.0, weights)
    turned = weights.T
    w_rows = jnp.concatenate([turned[: rays // 2], turned[rays // 2 :]], axis=1)
    w_send[...] = w_rows.reshape(w_send.shape)

    pl.semaphore_wait(row_sem, len(row_peers))

    def send_weights(k):
        remote(
            w_send.at[k], w_recv.at[chunk], w_sems.at[0], w_sems.at[1], first_target + k, r
        ).start()

    each_target(send_weights, False)
    w_recv[chunk] = w_send[chunk]
    rad_copies = ray_copies(
        lambda d: rad_hbm.at[pl.ds(pl.multiple_of(other_ray(d) * rays, rays), rays), :],
        rad_full.at[:, mine],
        1,
    )
    near_rays = sorted({1 % m, m - 1} - {0})
    half = rays // 2

    def columns_of(ray):
        return pl.ds(pl.multiple_of(ray * width, width), width)

    def rows_of(ray, k):
        return pl.ds(pl.multiple_of(ray * rays + k * half, half), half)

    def ring_copies(part_of, index):
        copies = []
        for k, d in enumerate(near_rays):
            src, dst = part_of(d, k)
            copies.append(
                remote(src, dst, x_send.at[index, d - 1], x_recv.at[index, d - 1], g, other_ray(d))
            )
        return copies

    def inv_part(d, k):
        part = inv_full.at[pl.ds(k * (size // 2), size // 2), columns_of(other_ray(m - d))]
        return part, part

    def rec_part(d, k):
        part = rec_full.at[rows_of(other_ray(m - d), k), :]
        return part, part

    inv_copies = ring_copies(lambda d, k: (inv_hbm, inv_full.at[:, mine]), 2)
    inv_passed = ring_copies(inv_part, 3) if m == 4 else []
    rec_copies = [
        ring_copies(
            lambda d, k: (rec_hbm.at[pl.ds(k * half, half), :], rec_full.at[rows_of(r, k), :]), 4
        ),
        ring_copies(
            lambda d, k: (
                rec_hbm.at[pl.ds((1 - k) * half, half), :],
                rec_full.at[rows_of(r, 1 - k), :],
            ),
            5,
        ),
    ]
    rec_passed = ring_copies(rec_part, 6) if m == 4 else []

    def waves_of(k):
        return pl.ds(k * (waves // 2), waves // 2)

    def first_part(d, k):
        part = p_recv.at[0, other_ray(m - d), waves_of(k), :]
        return part, part

    first_copies = [
        ring_copies(
            lambda d, k: (p_send.at[0, waves_of(k), :], p_recv.at[0, r, waves_of(k), :]), 7
        ),
        ring_copies(
            lambda d, k: (p_send.at[0, waves_of(1 - k), :], p_recv.at[0, r, waves_of(1 - k), :]),
            8,
        ),
    ]
    first_passed = ring_copies(first_part, 9) if m == 4 else []
    p_copies = [first_copies[1] + first_passed]

    def send_slab(step, wide):
        for k in range(chunks):
            s_send[step, k] = wide[k * rows : (k + 1) * rows].astype(BF16)

        def send(group, k):
            remote(
                s_send.at[step, k],
                s_recv.at[step, g],
                s_sems.at[step, 0],
                s_sems.at[step, 1],
                group,
                r,
            ).start()

        each_peer(send)
        s_recv[step, g] = s_send[step, chunk]

    def fold(step):
        wait_blocks(s_recv.at[step], s_sems.at[step, 1])
        for h in range(n):
            turn_s[h * rows : (h + 1) * rows] = s_recv[step, h].astype(F32)
        lane = lax.broadcasted_iota(jnp.int32, (n, 2 * waves), 1)
        for i in range(rows):
            slab = turn_s[pl.ds(i, n, stride=rows), :]
            wide = jnp.concatenate(
                [jnp.where(lane < waves, slab, 0.0), jnp.where(lane < waves, 0.0, slab)], axis=0
            ).astype(BF16)
            both = jnp.dot(w_both[i], wide, preferred_element_type=F32)
            turn_f[i * chunks : (i + 1) * chunks] = both[:chunks] + both[chunks:]
        for k in range(chunks):
            f_send[step, k] = turn_f[pl.ds(k, rows, stride=chunks), :].astype(BF16)
        place = r * chunks + chunk

        def send(k, ray):
            remote(
                f_send.at[step, k],
                f_recv.at[step, place],
                f_sems.at[step, 0],
                f_sems.at[step, 1],
                first_target + k,
                ray,
            ).start()

        if step and m > 1:

            def body(k, carry):
                d = jnp.where(k == 0, m // 2, jnp.where(k == 1, 1, m - 1))
                ray = wrap(r + d, m)
                each_target(lambda k: send(k, ray), True)
                return carry

            lax.fori_loop(0, m - 1, body, 0)
        each_target(lambda k: send(k, r), False)
        f_recv[step, place] = f_send[step, chunk]

    def send_partial(step, part):
        p_send[step] = part
        copies = [
            remote(
                p_send.at[step],
                p_recv.at[step, r],
                p_sems.at[step, 0, d - 1],
                p_sems.at[step, 1, d - 1],
                g,
                other_ray(d),
            )
            for d in ray_order
        ]
        for copy in copies:
            copy.start()
        p_copies.append(copies)
        p_recv[step, r] = part

    for copy in slab_copies:
        copy.wait_recv()
    first_slab = rs_recv[0].astype(F32)
    for k in range(1, m):
        first_slab = first_slab + rs_recv[k].astype(F32)
    send_slab(0, first_slab)
    for copy in cycle_copies + inv_copies + rad_copies:
        copy.start()

    wait_blocks(w_recv, w_sems.at[1])
    for i in range(rows):
        w_all = w_recv[:, i, :]
        w_high = w_all.astype(BF16)
        w_both[i, :chunks] = w_high
        w_both[i, chunks:] = (w_all - w_high.astype(F32)).astype(BF16)
    fold(0)
    for copy in inv_copies:
        copy.wait_recv()
    for copy in inv_passed:
        copy.start()

    load_self.wait()
    load_blocks.wait()
    load_exc.wait()
    for copy in cycle_copies:
        copy.wait_recv()
    base[...] = jnp.zeros_like(base)
    for step in range(steps):
        base[step, :, mine] = exc[step].astype(F32)

    def add_cycle(b, carry):
        shift = list_ref[0, b]
        source = g + shift - REACH
        valid = (b < count_ref[0]) & (source >= 0) & (source < n)
        past = [nearby[shift, lax.rem(start_slot - i + slots, slots)] for i in range(slots)]
        past = [jnp.where(valid, x, jnp.zeros_like(x)) for x in past]
        blank = jnp.zeros_like(past[0])
        lagged = jnp.concatenate(
            [
                jnp.concatenate([blank] * step + past[: slots - step], axis=1)
                for step in range(steps)
            ],
            axis=0,
        )
        near = jnp.dot(
            lagged, blocks[b].reshape(slots * width, size), preferred_element_type=F32
        )
        for step in range(steps):
            base[step] = base[step] - near[step * waves : (step + 1) * waves]
        return carry


    lax.fori_loop(0, entries, add_cycle, 0)

    def gathered_sum(step):
        for copy in p_copies[step]:
            copy.wait_recv()
        total = p_recv[step, 0].astype(F32)
        for d in range(1, m):
            total = total + p_recv[step, d].astype(F32)
        return total

    def turn_field(pieces):
        turned = jnp.concatenate([x.astype(F32) for x in pieces], axis=0).T.astype(BF16)
        span = rays // 2
        return jnp.concatenate(
            [
                turned[p * waves : (p + 1) * waves, k * span : (k + 1) * span]
                for k in range(len(pieces) // chunks)
                for p in range(2)
            ],
            axis=1,
        )

    for step in range(steps):
        more = step + 1 < steps
        if step == 0:
            load_rec.wait()
            wait_blocks(f_recv.at[0], f_sems.at[0, 1], chunks - 1)
            field = turn_field([f_recv[0, r * chunks + k] for k in range(chunks)])
            far = jnp.dot(field, rec_full[rows_here, :], preferred_element_type=F32)
            term = (base[0] - far).astype(BF16)
            p_send[0] = term
            for copy in first_copies[0] + first_copies[1]:
                copy.start()
            p_recv[0, r] = term
            for copy in first_copies[0]:
                copy.wait_recv()
            for copy in first_passed + rec_copies[0]:
                copy.start()
            load_rad.wait()
            load_inv.wait()
            load_own_inv.wait()
            for copy in rad_copies + inv_passed:
                copy.wait_recv()
            slab_of_drive[...] = lax.dot_general(
                rad_full[...], inv_full[...], dims, preferred_element_type=F32
            ).astype(BF16)
            drive = gathered_sum(0).astype(BF16)
            current = jnp.dot(drive, inv[...], preferred_element_type=F32).astype(BF16)
            slab = lax.dot_general(slab_of_drive[...], drive, dims, preferred_element_type=F32)
        else:
            if step == 1:
                for copy in rec_copies[1] + rec_passed:
                    copy.wait_recv()
                current_of_field[...] = jnp.dot(
                    rec_full[...], inv[...], preferred_element_type=F32
                ).astype(BF16)
                slab_of_field[...] = lax.dot_general(
                    slab_of_drive[...], rec_full[...], dims, preferred_element_type=F32
                ).astype(BF16)
            known = gathered_sum(step).astype(BF16)
            current = jnp.dot(known, inv[...], preferred_element_type=F32)
            if more:
                slab = lax.dot_general(slab_of_drive[...], known, dims, preferred_element_type=F32)
            wait_blocks(f_recv.at[step], f_sems.at[step, 1])
            field = turn_field([f_recv[step, k] for k in range(m * chunks)])
            current = (
                current - jnp.dot(field, current_of_field[...], preferred_element_type=F32)
            ).astype(BF16)
            if more:
                slab = slab - lax.dot_general(
                    slab_of_field[...], field, dims, preferred_element_type=F32
                )
        if more:
            wide = jnp.concatenate([slab[: rays // 2], slab[rays // 2 :]], axis=1)
        own[step] = current
        if step + 1 < steps:
            fresh = fresh_of[step]
            copies = near_copies(own.at[step], fresh, step + 1)
            for copy in copies:
                copy.start()
            near_all.extend(copies)
            send_slab(step + 1, wide)
            if step == 0:
                for copy in rec_copies[0]:
                    copy.wait_recv()
                for copy in rec_passed + rec_copies[1]:
                    copy.start()
            fresh[REACH] = current
        out_ref[step] = current
        if step + 1 < steps:
            for copy in copies:
                copy.wait_recv()

            def add_near(later):
                latest = [fresh[near_shift[b]] for b in range(entries)]
                latest = [
                    jnp.where(near_valid[b], x, jnp.zeros_like(x)) for b, x in enumerate(latest)
                ]
                base[later] = base[later] - jnp.dot(
                    jnp.concatenate(latest, axis=1),
                    blocks[:, later - step - 1].reshape(entries * width, size),
                    preferred_element_type=F32,
                )

            add_near(step + 1)
            send_partial(step + 1, base[step + 1].astype(BF16))
            fold(step + 1)
            for later in range(step + 2, steps):
                add_near(later)

    ringed = inv_copies + inv_passed + sum(rec_copies, rec_passed) + first_copies[0]
    for copy in slab_copies + rad_copies + ringed + near_all + sum(p_copies, []):
        copy.wait_send()
    wait_blocks(w_send, w_sems.at[0])
    for step in range(steps):
        wait_blocks(s_recv.at[step], s_sems.at[step, 0])
        wait_blocks(f_recv.at[step], f_sems.at[step, 0], None if step else chunks - 1)


def layout_of(n):
    inner = 1
    while inner * inner < n:
        inner *= 2
    return inner, max(n // (2 * inner), 1)


def solution(mesh):
    n = mesh.shape["groups"]
    m = mesh.shape["rays"]
    inner, copies_of_fold = layout_of(n)
    chunks = n // copies_of_fold

    def local(
        excitation,
        cycle,
        near_blocks,
        near_list,
        near_count,
        newest,
        inverse,
        radiate,
        translate,
        receive,
    ):
        steps, waves, width = excitation.shape
        slots = cycle.shape[0]
        entries = near_list.shape[1]
        size = m * width
        rays = receive.shape[0]
        rows = rays // (2 * chunks)
        spread = 2 * REACH + 1
        anywhere = pl.BlockSpec(memory_space=pl.ANY)
        dma = pltpu.SemaphoreType.DMA
        vmem = pltpu.VMEM
        smem = pltpu.SMEM
        return pl.pallas_call(
            functools.partial(kernel, n, inner, copies_of_fold, m),
            out_shape=pltpu.VMEM(excitation.shape, BF16),
            in_specs=[anywhere] * 10,
            out_specs=pl.BlockSpec(memory_space=vmem),
            scratch_shapes=[
                smem(near_list.shape, jnp.int32),
                smem(near_count.shape, jnp.int32),
                smem(newest.shape, jnp.int32),
                vmem(excitation.shape, BF16),
                vmem(cycle.shape, BF16),
                vmem((entries, slots, width, size), BF16),
                vmem((n, rays), F32),
                vmem(radiate.shape, BF16),
                vmem(inverse.shape, BF16),
                vmem((m, rays // 2, 2 * waves), BF16),
                vmem((m, rays // 2, 2 * waves), BF16),
                vmem((rays, size), BF16),
                vmem((size, size), BF16),
                vmem((rays, size), BF16),
                vmem((m * rays, size), BF16),
                vmem((rays, m * rays), BF16),
                vmem((m * rays, width), BF16),
                vmem((spread, slots, waves, width), BF16),
                vmem((spread, waves, width), BF16),
                vmem((spread, waves, width), BF16),
                vmem((chunks, rows, 2 * n), F32),
                vmem((chunks, rows, 2 * n), F32),
                vmem((rows, 2 * chunks, 2 * n), BF16),
                vmem((n * rows, 2 * waves), F32),
                vmem((chunks * rows, 2 * waves), F32),
                vmem((steps, chunks, rows, 2 * waves), BF16),
                vmem((steps, n, rows, 2 * waves), BF16),
                vmem((steps, chunks, rows, 2 * waves), BF16),
                vmem((steps, m * chunks, rows, 2 * waves), BF16),
                vmem((steps, waves, size), F32),
                vmem((steps, waves, size), BF16),
                vmem((steps, m, waves, size), BF16),
                vmem((steps, waves, width), BF16),
                pltpu.SemaphoreType.REGULAR,
                dma((13,)),
                dma((10, m - 1)),
                dma((10, m - 1)),
                dma((2,)),
                dma((steps, 2)),
                dma((steps, 2)),
                dma((steps, 4)),
                dma((steps, 4)),
                dma((steps, 2, m - 1)),
            ],
            compiler_params=pltpu.CompilerParams(
                collective_id=0, has_side_effects=True, vmem_limit_bytes=56 * 1024 * 1024
            ),
        )(
            excitation,
            cycle,
            near_blocks,
            near_list,
            near_count,
            newest,
            inverse,
            radiate,
            translate,
            receive,
        )

    placed = (
        P(None, None, ("groups", "rays")),
        P(None, None, ("groups", "rays")),
        P("groups", None, None, "rays", None),
        P("groups", None),
        P("groups"),
        P(),
        P(None, ("groups", "rays")),
        P(None, ("groups", "rays")),
        P("groups", None, "rays"),
        P("rays", "groups"),
    )
    return jax.shard_map(
        local,
        mesh=mesh,
        in_specs=placed,
        out_specs=P(None, None, ("groups", "rays")),
        check_vma=False,
    )
```

```python
import functools

import jax
import jax.numpy as jnp
from jax import lax
from jax.experimental import pallas as pl
from jax.experimental.pallas import tpu as pltpu
from jax.sharding import PartitionSpec as P

REACH = 2
NEAR_SHIFTS = (-2, -1, 1, 2)
MESH = pl.DeviceIdType.MESH
F32 = jnp.float32
BF16 = jnp.bfloat16


def kernel(
    n,
    inner,
    copies_of_fold,
    m,
    exc_hbm,
    cyc_hbm,
    blocks_hbm,
    list_hbm,
    count_hbm,
    newest_hbm,
    inv_hbm,
    rad_hbm,
    tr_hbm,
    rec_hbm,
    out_ref,
    list_ref,
    count_ref,
    newest_ref,
    exc,
    cyc,
    blocks,
    tr,
    rad,
    inv,
    rs_send,
    rs_recv,
    rad_full,
    inv_full,
    slab_of_drive,
    rec_full,
    slab_of_field,
    current_of_field,
    nearby,
    fresh_first,
    fresh_second,
    w_send,
    w_recv,
    w_both,
    turn_s,
    turn_f,
    s_send,
    s_recv,
    f_send,
    f_recv,
    base,
    p_send,
    p_recv,
    own,
    row_sem,
    load_sems,
    x_send,
    x_recv,
    w_sems,
    s_sems,
    f_sems,
    near_send,
    near_recv,
    p_sems,
):
    steps, waves, width = exc.shape
    slots = cyc.shape[0]
    entries = list_ref.shape[1]
    size = m * width
    rays = tr.shape[1]
    outer = n // inner
    chunks = n // copies_of_fold
    rows = rays // (2 * chunks)
    g = lax.axis_index("groups")
    r = lax.axis_index("rays")
    go = g // inner
    gi = g - go * inner
    pair = go // 2
    plane = go - 2 * pair
    chunk = plane * inner + gi
    first_target = g - chunk
    mine = pl.ds(pl.multiple_of(r * width, width), width)
    dims = (((1,), (1,)), ((), ()))
    fresh_of = (fresh_first, fresh_second)
    ray_order = sorted(range(1, m), key=lambda d: -min(d, m - d))
    inner_order = sorted(range(inner), key=lambda d: -min(d, inner - d))

    def wrap(x, limit):
        return jnp.where(x >= limit, x - limit, x)

    inner_place = [wrap(gi + d, inner) for d in range(inner)]
    ray_place = [wrap(r + d, m) for d in range(m)]

    def near_group(d):
        return wrap(g + d + n, n) if d < 0 else wrap(g + d, n)

    def other_ray(d):
        return ray_place[d]

    def remote(src, dst, send_sem, recv_sem, group, ray):
        return pltpu.make_async_remote_copy(
            src_ref=src,
            dst_ref=dst,
            send_sem=send_sem,
            recv_sem=recv_sem,
            device_id=(group, ray),
            device_id_type=MESH,
        )

    def each_peer(act):
        def body(k, carry):
            shift, change = carry
            place = wrap(go + shift, outer)
            other = place * inner
            bit = place - 2 * (place // 2)
            for d in inner_order:
                act(other + inner_place[d], bit * inner + inner_place[d])
            return shift + change, jnp.where(change < 0, 1 - change, -1 - change)

        lax.fori_loop(0, outer - 1, body, (jnp.int32(outer // 2), jnp.int32(-1)))
        for d in inner_order:
            if d:
                act(go * inner + inner_place[d], plane * inner + inner_place[d])

    def each_target(act, with_self):
        for d in inner_order:
            act((1 - plane) * inner + inner_place[d])
        for d in inner_order:
            if d or with_self:
                act(plane * inner + inner_place[d])

    def wait_blocks(like, sem, count=None):
        part = like.at[pl.ds(0, like.shape[0] - 1 if count is None else count)]
        pltpu.make_async_copy(part, part, sem).wait()

    def near_copies(src, dst, index):
        return [
            remote(
                src,
                dst.at[REACH - shift],
                near_send.at[index, k],
                near_recv.at[index, k],
                near_group(shift),
                r,
            )
            for k, shift in enumerate(NEAR_SHIFTS)
        ]

    def ray_copies(src_of, dst, index):
        return [
            remote(
                src_of(d), dst, x_send.at[index, d - 1], x_recv.at[index, d - 1], g, other_ray(d)
            )
            for d in ray_order
        ]

    rows_here = pl.ds(pl.multiple_of(r * rays, rays), rays)
    pairs = (
        (newest_hbm, newest_ref),
        (cyc_hbm, cyc),
        (rad_hbm, rad),
        (list_hbm, list_ref),
        (count_hbm, count_ref),
        (tr_hbm.at[0], tr),
        (rad_hbm.at[rows_here, :], rad_full.at[:, mine]),
        (blocks_hbm.at[0], blocks),
        (inv_hbm, inv_full.at[:, mine]),
        (inv_hbm, inv),
        (cyc_hbm, nearby.at[REACH]),
        (rec_hbm, rec_full.at[rows_here, :]),
        (exc_hbm, exc),
    )
    loads = [
        pltpu.make_async_copy(src, dst, load_sems.at[i]) for i, (src, dst) in enumerate(pairs)
    ]
    for load in loads[:3]:
        load.start()

    barrier = pltpu.get_barrier_semaphore()
    greeted = [(g, other_ray(d)) for d in ray_order]
    greeted += [(go * inner + inner_place[d], r) for d in inner_order if d]
    row_peers = [(wrap(go + d, outer) * inner + gi, r) for d in range(1, outer)]
    greeted += row_peers
    greeted += [(near_group(d), r) for d in NEAR_SHIFTS]
    for device in greeted:
        pl.semaphore_signal(barrier, inc=1, device_id=device, device_id_type=MESH)

    for load in loads[3:]:
        load.start(priority=1)
    (
        load_newest,
        load_cyc,
        load_all_rad,
        load_list,
        load_count,
        load_tr,
        load_rad,
        load_blocks,
        load_inv,
        load_own_inv,
        load_self,
        load_rec,
        load_exc,
    ) = loads

    pl.semaphore_wait(barrier, len(greeted))

    for device in row_peers:
        pl.semaphore_signal(row_sem, inc=1, device_id=device, device_id_type=MESH)
    load_newest.wait()
    load_cyc.wait()
    start_slot = newest_ref[0]
    newest_value = cyc[start_slot]
    load_all_rad.wait()
    slab_copies = ray_copies(lambda d: rs_send.at[other_ray(d)], rs_recv.at[r], 0)
    for d, copy in zip(ray_order + [0], slab_copies + [None]):
        ray = other_ray(d)
        block = rad[pl.ds(pl.multiple_of(ray * rays, rays), rays), :]
        block = lax.dot_general(block, newest_value, dims, preferred_element_type=F32)
        block = jnp.concatenate([block[: rays // 2], block[rays // 2 :]], axis=1).astype(BF16)
        if copy is None:
            rs_recv[r] = block
        else:
            rs_send[ray] = block
            copy.start()
    cycle_copies = near_copies(cyc_hbm, nearby, 0)
    for copy in cycle_copies:
        copy.start()
    near_all = list(cycle_copies)

    load_list.wait()
    load_count.wait()
    near_shift = []
    near_valid = []
    for b in range(entries):
        shift = list_ref[0, b]
        source = g + shift - REACH
        near_shift.append(shift)
        near_valid.append((b < count_ref[0]) & (source >= 0) & (source < n))
    load_tr.wait()
    every = lax.broadcasted_iota(jnp.int32, (n, rays), 0)
    weights = tr[...]
    for b in range(entries):
        hit = near_valid[b] & (every == g + near_shift[b] - REACH)
        weights = jnp.where(hit, 0.0, weights)
    turned = weights.T
    w_rows = jnp.concatenate([turned[: rays // 2], turned[rays // 2 :]], axis=1)
    w_send[...] = w_rows.reshape(w_send.shape)

    pl.semaphore_wait(row_sem, len(row_peers))

    def send_weights(k):
        remote(
            w_send.at[k], w_recv.at[chunk], w_sems.at[0], w_sems.at[1], first_target + k, r
        ).start()

    each_target(send_weights, False)
    w_recv[chunk] = w_send[chunk]
    rad_copies = ray_copies(
        lambda d: rad_hbm.at[pl.ds(pl.multiple_of(other_ray(d) * rays, rays), rays), :],
        rad_full.at[:, mine],
        1,
    )
    near_rays = sorted({1 % m, m - 1} - {0})
    half = rays // 2

    def columns_of(ray):
        return pl.ds(pl.multiple_of(ray * width, width), width)

    def rows_of(ray, k):
        return pl.ds(pl.multiple_of(ray * rays + k * half, half), half)

    def ring_copies(part_of, index):
        copies = []
        for k, d in enumerate(near_rays):
            src, dst = part_of(d, k)
            copies.append(
                remote(src, dst, x_send.at[index, d - 1], x_recv.at[index, d - 1], g, other_ray(d))
            )
        return copies

    def inv_part(d, k):
        part = inv_full.at[pl.ds(k * (size // 2), size // 2), columns_of(other_ray(m - d))]
        return part, part

    def rec_part(d, k):
        part = rec_full.at[rows_of(other_ray(m - d), k), :]
        return part, part

    inv_copies = ring_copies(lambda d, k: (inv_hbm, inv_full.at[:, mine]), 2)
    inv_passed = ring_copies(inv_part, 3) if m == 4 else []
    rec_copies = [
        ring_copies(
            lambda d, k: (rec_hbm.at[pl.ds(k * half, half), :], rec_full.at[rows_of(r, k), :]), 4
        ),
        ring_copies(
            lambda d, k: (
                rec_hbm.at[pl.ds((1 - k) * half, half), :],
                rec_full.at[rows_of(r, 1 - k), :],
            ),
            5,
        ),
    ]
    rec_passed = ring_copies(rec_part, 6) if m == 4 else []
    p_copies = []

    def send_slab(step, wide):
        for k in range(chunks):
            s_send[step, k] = wide[k * rows : (k + 1) * rows].astype(BF16)

        def send(group, k):
            remote(
                s_send.at[step, k],
                s_recv.at[step, g],
                s_sems.at[step, 0],
                s_sems.at[step, 1],
                group,
                r,
            ).start()

        each_peer(send)
        s_recv[step, g] = s_send[step, chunk]

    def fold(step):
        wait_blocks(s_recv.at[step], s_sems.at[step, 1])
        for h in range(n):
            turn_s[h * rows : (h + 1) * rows] = s_recv[step, h].astype(F32)
        lane = lax.broadcasted_iota(jnp.int32, (n, 2 * waves), 1)
        for i in range(rows):
            slab = turn_s[pl.ds(i, n, stride=rows), :]
            wide = jnp.concatenate(
                [jnp.where(lane < waves, slab, 0.0), jnp.where(lane < waves, 0.0, slab)], axis=0
            ).astype(BF16)
            both = jnp.dot(w_both[i], wide, preferred_element_type=F32)
            turn_f[i * chunks : (i + 1) * chunks] = both[:chunks] + both[chunks:]
        for k in range(chunks):
            f_send[step, k] = turn_f[pl.ds(k, rows, stride=chunks), :].astype(BF16)
        place = r * chunks + chunk

        def send(k, ray):
            remote(
                f_send.at[step, k],
                f_recv.at[step, place],
                f_sems.at[step, 0],
                f_sems.at[step, 1],
                first_target + k,
                ray,
            ).start()

        if step and m > 1:

            def body(k, carry):
                d = jnp.where(k == 0, m // 2, jnp.where(k == 1, 1, m - 1))
                ray = wrap(r + d, m)
                each_target(lambda k: send(k, ray), True)
                return carry

            lax.fori_loop(0, m - 1, body, 0)
        each_target(lambda k: send(k, r), False)
        f_recv[step, place] = f_send[step, chunk]

    def send_partial(step, part):
        p_send[step] = part
        copies = [
            remote(
                p_send.at[step],
                p_recv.at[step, r],
                p_sems.at[step, 0, d - 1],
                p_sems.at[step, 1, d - 1],
                g,
                other_ray(d),
            )
            for d in ray_order
        ]
        for copy in copies:
            copy.start()
        p_copies.append(copies)
        p_recv[step, r] = part

    for copy in slab_copies:
        copy.wait_recv()
    first_slab = rs_recv[0].astype(F32)
    for k in range(1, m):
        first_slab = first_slab + rs_recv[k].astype(F32)
    send_slab(0, first_slab)
    for copy in inv_copies:
        copy.start()

    load_self.wait()
    load_blocks.wait()
    load_exc.wait()
    for copy in cycle_copies:
        copy.wait_recv()
    base[...] = jnp.zeros_like(base)
    for step in range(steps):
        base[step, :, mine] = exc[step].astype(F32)

    def add_cycle(b, carry):
        shift = list_ref[0, b]
        source = g + shift - REACH
        valid = (b < count_ref[0]) & (source >= 0) & (source < n)
        past = [nearby[shift, lax.rem(start_slot - i + slots, slots)] for i in range(slots)]
        past = [jnp.where(valid, x, jnp.zeros_like(x)) for x in past]
        blank = jnp.zeros_like(past[0])
        lagged = jnp.concatenate(
            [
                jnp.concatenate([blank] * step + past[: slots - step], axis=1)
                for step in range(steps)
            ],
            axis=0,
        )
        near = jnp.dot(
            lagged, blocks[b].reshape(slots * width, size), preferred_element_type=F32
        )
        for step in range(steps):
            base[step] = base[step] - near[step * waves : (step + 1) * waves]
        return carry


    lax.fori_loop(0, entries, add_cycle, 0)

    wait_blocks(w_recv, w_sems.at[1])
    for i in range(rows):
        w_all = w_recv[:, i, :]
        w_high = w_all.astype(BF16)
        w_both[i, :chunks] = w_high
        w_both[i, chunks:] = (w_all - w_high.astype(F32)).astype(BF16)
    fold(0)
    for copy in inv_copies:
        copy.wait_recv()
    for copy in inv_passed + rad_copies:
        copy.start()

    def gathered_sum(step):
        for copy in p_copies[step]:
            copy.wait_recv()
        total = p_recv[step, 0].astype(F32)
        for d in range(1, m):
            total = total + p_recv[step, d].astype(F32)
        return total

    def turn_field(pieces):
        turned = jnp.concatenate([x.astype(F32) for x in pieces], axis=0).T.astype(BF16)
        span = rays // 2
        return jnp.concatenate(
            [
                turned[p * waves : (p + 1) * waves, k * span : (k + 1) * span]
                for k in range(len(pieces) // chunks)
                for p in range(2)
            ],
            axis=1,
        )

    for step in range(steps):
        more = step + 1 < steps
        if step == 0:
            load_rec.wait()
            wait_blocks(f_recv.at[0], f_sems.at[0, 1], chunks - 1)
            field = turn_field([f_recv[0, r * chunks + k] for k in range(chunks)])
            far = jnp.dot(field, rec_full[rows_here, :], preferred_element_type=F32)
            send_partial(0, (base[0] - far).astype(BF16))
            for copy in rec_copies[0]:
                copy.start()
            load_rad.wait()
            load_inv.wait()
            load_own_inv.wait()
            for copy in rad_copies + inv_passed:
                copy.wait_recv()
            slab_of_drive[...] = lax.dot_general(
                rad_full[...], inv_full[...], dims, preferred_element_type=F32
            ).astype(BF16)
            drive = gathered_sum(0).astype(BF16)
            current = jnp.dot(drive, inv[...], preferred_element_type=F32).astype(BF16)
            slab = lax.dot_general(slab_of_drive[...], drive, dims, preferred_element_type=F32)
        else:
            if step == 1:
                for copy in rec_copies[1] + rec_passed:
                    copy.wait_recv()
                current_of_field[...] = jnp.dot(
                    rec_full[...], inv[...], preferred_element_type=F32
                ).astype(BF16)
                slab_of_field[...] = lax.dot_general(
                    slab_of_drive[...], rec_full[...], dims, preferred_element_type=F32
                ).astype(BF16)
            known = gathered_sum(step).astype(BF16)
            current = jnp.dot(known, inv[...], preferred_element_type=F32)
            if more:
                slab = lax.dot_general(slab_of_drive[...], known, dims, preferred_element_type=F32)
            wait_blocks(f_recv.at[step], f_sems.at[step, 1])
            field = turn_field([f_recv[step, k] for k in range(m * chunks)])
            current = (
                current - jnp.dot(field, current_of_field[...], preferred_element_type=F32)
            ).astype(BF16)
            if more:
                slab = slab - lax.dot_general(
                    slab_of_field[...], field, dims, preferred_element_type=F32
                )
        if more:
            wide = jnp.concatenate([slab[: rays // 2], slab[rays // 2 :]], axis=1)
        own[step] = current
        if step + 1 < steps:
            fresh = fresh_of[step]
            copies = near_copies(own.at[step], fresh, step + 1)
            for copy in copies:
                copy.start()
            near_all.extend(copies)
            send_slab(step + 1, wide)
            if step == 0:
                for copy in rec_copies[0]:
                    copy.wait_recv()
                for copy in rec_passed + rec_copies[1]:
                    copy.start()
            fresh[REACH] = current
        out_ref[step] = current
        if step + 1 < steps:
            for copy in copies:
                copy.wait_recv()

            def add_near(later):
                latest = [fresh[near_shift[b]] for b in range(entries)]
                latest = [
                    jnp.where(near_valid[b], x, jnp.zeros_like(x)) for b, x in enumerate(latest)
                ]
                base[later] = base[later] - jnp.dot(
                    jnp.concatenate(latest, axis=1),
                    blocks[:, later - step - 1].reshape(entries * width, size),
                    preferred_element_type=F32,
                )

            add_near(step + 1)
            send_partial(step + 1, base[step + 1].astype(BF16))
            fold(step + 1)
            for later in range(step + 2, steps):
                add_near(later)

    ringed = inv_copies + inv_passed + sum(rec_copies, rec_passed)
    for copy in slab_copies + rad_copies + ringed + near_all + sum(p_copies, []):
        copy.wait_send()
    wait_blocks(w_send, w_sems.at[0])
    for step in range(steps):
        wait_blocks(s_recv.at[step], s_sems.at[step, 0])
        wait_blocks(f_recv.at[step], f_sems.at[step, 0], None if step else chunks - 1)


def layout_of(n):
    inner = 1
    while inner * inner < n:
        inner *= 2
    return inner, max(n // (2 * inner), 1)


def solution(mesh):
    n = mesh.shape["groups"]
    m = mesh.shape["rays"]
    inner, copies_of_fold = layout_of(n)
    chunks = n // copies_of_fold

    def local(
        excitation,
        cycle,
        near_blocks,
        near_list,
        near_count,
        newest,
        inverse,
        radiate,
        translate,
        receive,
    ):
        steps, waves, width = excitation.shape
        slots = cycle.shape[0]
        entries = near_list.shape[1]
        size = m * width
        rays = receive.shape[0]
        rows = rays // (2 * chunks)
        spread = 2 * REACH + 1
        anywhere = pl.BlockSpec(memory_space=pl.ANY)
        dma = pltpu.SemaphoreType.DMA
        vmem = pltpu.VMEM
        smem = pltpu.SMEM
        return pl.pallas_call(
            functools.partial(kernel, n, inner, copies_of_fold, m),
            out_shape=pltpu.VMEM(excitation.shape, BF16),
            in_specs=[anywhere] * 10,
            out_specs=pl.BlockSpec(memory_space=vmem),
            scratch_shapes=[
                smem(near_list.shape, jnp.int32),
                smem(near_count.shape, jnp.int32),
                smem(newest.shape, jnp.int32),
                vmem(excitation.shape, BF16),
                vmem(cycle.shape, BF16),
                vmem((entries, slots, width, size), BF16),
                vmem((n, rays), F32),
                vmem(radiate.shape, BF16),
                vmem(inverse.shape, BF16),
                vmem((m, rays // 2, 2 * waves), BF16),
                vmem((m, rays // 2, 2 * waves), BF16),
                vmem((rays, size), BF16),
                vmem((size, size), BF16),
                vmem((rays, size), BF16),
                vmem((m * rays, size), BF16),
                vmem((rays, m * rays), BF16),
                vmem((m * rays, width), BF16),
                vmem((spread, slots, waves, width), BF16),
                vmem((spread, waves, width), BF16),
                vmem((spread, waves, width), BF16),
                vmem((chunks, rows, 2 * n), F32),
                vmem((chunks, rows, 2 * n), F32),
                vmem((rows, 2 * chunks, 2 * n), BF16),
                vmem((n * rows, 2 * waves), F32),
                vmem((chunks * rows, 2 * waves), F32),
                vmem((steps, chunks, rows, 2 * waves), BF16),
                vmem((steps, n, rows, 2 * waves), BF16),
                vmem((steps, chunks, rows, 2 * waves), BF16),
                vmem((steps, m * chunks, rows, 2 * waves), BF16),
                vmem((steps, waves, size), F32),
                vmem((steps, waves, size), BF16),
                vmem((steps, m, waves, size), BF16),
                vmem((steps, waves, width), BF16),
                pltpu.SemaphoreType.REGULAR,
                dma((13,)),
                dma((7, m - 1)),
                dma((7, m - 1)),
                dma((2,)),
                dma((steps, 2)),
                dma((steps, 2)),
                dma((steps, 4)),
                dma((steps, 4)),
                dma((steps, 2, m - 1)),
            ],
            compiler_params=pltpu.CompilerParams(
                collective_id=0, has_side_effects=True, vmem_limit_bytes=56 * 1024 * 1024
            ),
        )(
            excitation,
            cycle,
            near_blocks,
            near_list,
            near_count,
            newest,
            inverse,
            radiate,
            translate,
            receive,
        )

    placed = (
        P(None, None, ("groups", "rays")),
        P(None, None, ("groups", "rays")),
        P("groups", None, None, "rays", None),
        P("groups", None),
        P("groups"),
        P(),
        P(None, ("groups", "rays")),
        P(None, ("groups", "rays")),
        P("groups", None, "rays"),
        P("rays", "groups"),
    )
    return jax.shard_map(
        local,
        mesh=mesh,
        in_specs=placed,
        out_specs=P(None, None, ("groups", "rays")),
        check_vma=False,
    )
```

```python
import functools

import jax
import jax.numpy as jnp
from jax import lax
from jax.experimental import pallas as pl
from jax.experimental.pallas import tpu as pltpu
from jax.sharding import PartitionSpec as P

REACH = 2
NEAR_SHIFTS = (-2, -1, 1, 2)
MESH = pl.DeviceIdType.MESH
F32 = jnp.float32
BF16 = jnp.bfloat16


def kernel(
    n,
    inner,
    copies_of_fold,
    m,
    exc_hbm,
    cyc_hbm,
    blocks_hbm,
    list_hbm,
    count_hbm,
    newest_hbm,
    inv_hbm,
    rad_hbm,
    tr_hbm,
    rec_hbm,
    out_ref,
    list_ref,
    count_ref,
    newest_ref,
    exc,
    cyc,
    blocks,
    tr,
    rad,
    inv,
    rs_send,
    rs_recv,
    rad_full,
    inv_full,
    slab_of_drive,
    rec_full,
    slab_of_field,
    current_of_field,
    nearby,
    fresh_first,
    fresh_second,
    w_send,
    w_recv,
    w_both,
    turn_s,
    turn_f,
    s_send,
    s_recv,
    f_send,
    f_recv,
    base,
    p_send,
    p_recv,
    own,
    row_sem,
    load_sems,
    x_send,
    x_recv,
    w_sems,
    s_sems,
    f_sems,
    near_send,
    near_recv,
    p_sems,
):
    steps, waves, width = exc.shape
    slots = cyc.shape[0]
    entries = list_ref.shape[1]
    size = m * width
    rays = tr.shape[1]
    outer = n // inner
    chunks = n // copies_of_fold
    rows = rays // (2 * chunks)
    g = lax.axis_index("groups")
    r = lax.axis_index("rays")
    go = g // inner
    gi = g - go * inner
    pair = go // 2
    plane = go - 2 * pair
    chunk = plane * inner + gi
    first_target = g - chunk
    mine = pl.ds(pl.multiple_of(r * width, width), width)
    dims = (((1,), (1,)), ((), ()))
    fresh_of = (fresh_first, fresh_second)
    ray_order = sorted(range(1, m), key=lambda d: -min(d, m - d))
    inner_order = sorted(range(inner), key=lambda d: -min(d, inner - d))

    def wrap(x, limit):
        return jnp.where(x >= limit, x - limit, x)

    inner_place = [wrap(gi + d, inner) for d in range(inner)]
    ray_place = [wrap(r + d, m) for d in range(m)]

    def near_group(d):
        return wrap(g + d + n, n) if d < 0 else wrap(g + d, n)

    def other_ray(d):
        return ray_place[d]

    def remote(src, dst, send_sem, recv_sem, group, ray):
        return pltpu.make_async_remote_copy(
            src_ref=src,
            dst_ref=dst,
            send_sem=send_sem,
            recv_sem=recv_sem,
            device_id=(group, ray),
            device_id_type=MESH,
        )

    def each_peer(act):
        def body(k, carry):
            shift, change = carry
            place = wrap(go + shift, outer)
            other = place * inner
            bit = place - 2 * (place // 2)
            for d in inner_order:
                act(other + inner_place[d], bit * inner + inner_place[d])
            return shift + change, jnp.where(change < 0, 1 - change, -1 - change)

        lax.fori_loop(0, outer - 1, body, (jnp.int32(outer // 2), jnp.int32(-1)))
        for d in inner_order:
            if d:
                act(go * inner + inner_place[d], plane * inner + inner_place[d])

    def each_target(act, with_self):
        for d in inner_order:
            act((1 - plane) * inner + inner_place[d])
        for d in inner_order:
            if d or with_self:
                act(plane * inner + inner_place[d])

    def wait_blocks(like, sem, count=None):
        part = like.at[pl.ds(0, like.shape[0] - 1 if count is None else count)]
        pltpu.make_async_copy(part, part, sem).wait()

    def near_copies(src, dst, index):
        return [
            remote(
                src,
                dst.at[REACH - shift],
                near_send.at[index, k],
                near_recv.at[index, k],
                near_group(shift),
                r,
            )
            for k, shift in enumerate(NEAR_SHIFTS)
        ]

    def ray_copies(src_of, dst, index):
        return [
            remote(
                src_of(d), dst, x_send.at[index, d - 1], x_recv.at[index, d - 1], g, other_ray(d)
            )
            for d in ray_order
        ]

    rows_here = pl.ds(pl.multiple_of(r * rays, rays), rays)
    pairs = (
        (newest_hbm, newest_ref),
        (cyc_hbm, cyc),
        (rad_hbm, rad),
        (list_hbm, list_ref),
        (count_hbm, count_ref),
        (tr_hbm.at[0], tr),
        (rad_hbm.at[rows_here, :], rad_full.at[:, mine]),
        (blocks_hbm.at[0], blocks),
        (inv_hbm, inv_full.at[:, mine]),
        (inv_hbm, inv),
        (cyc_hbm, nearby.at[REACH]),
        (rec_hbm, rec_full.at[rows_here, :]),
        (exc_hbm, exc),
    )
    loads = [
        pltpu.make_async_copy(src, dst, load_sems.at[i]) for i, (src, dst) in enumerate(pairs)
    ]
    for load in loads[:3]:
        load.start()

    barrier = pltpu.get_barrier_semaphore()
    greeted = [(g, other_ray(d)) for d in ray_order]
    greeted += [(go * inner + inner_place[d], r) for d in inner_order if d]
    row_peers = [(wrap(go + d, outer) * inner + gi, r) for d in range(1, outer)]
    greeted += row_peers
    greeted += [(near_group(d), r) for d in NEAR_SHIFTS]
    for device in greeted:
        pl.semaphore_signal(barrier, inc=1, device_id=device, device_id_type=MESH)

    for load in loads[3:]:
        load.start(priority=1)
    (
        load_newest,
        load_cyc,
        load_all_rad,
        load_list,
        load_count,
        load_tr,
        load_rad,
        load_blocks,
        load_inv,
        load_own_inv,
        load_self,
        load_rec,
        load_exc,
    ) = loads

    pl.semaphore_wait(barrier, len(greeted))

    for device in row_peers:
        pl.semaphore_signal(row_sem, inc=1, device_id=device, device_id_type=MESH)
    load_newest.wait()
    load_cyc.wait()
    start_slot = newest_ref[0]
    newest_value = cyc[start_slot]
    load_all_rad.wait()
    slab_copies = ray_copies(lambda d: rs_send.at[other_ray(d)], rs_recv.at[r], 0)
    for d, copy in zip(ray_order + [0], slab_copies + [None]):
        ray = other_ray(d)
        block = rad[pl.ds(pl.multiple_of(ray * rays, rays), rays), :]
        block = lax.dot_general(block, newest_value, dims, preferred_element_type=F32)
        block = jnp.concatenate([block[: rays // 2], block[rays // 2 :]], axis=1).astype(BF16)
        if copy is None:
            rs_recv[r] = block
        else:
            rs_send[ray] = block
            copy.start()
    cycle_copies = near_copies(cyc_hbm, nearby, 0)
    near_all = list(cycle_copies)

    load_list.wait()
    load_count.wait()
    near_shift = []
    near_valid = []
    for b in range(entries):
        shift = list_ref[0, b]
        source = g + shift - REACH
        near_shift.append(shift)
        near_valid.append((b < count_ref[0]) & (source >= 0) & (source < n))
    load_tr.wait()
    every = lax.broadcasted_iota(jnp.int32, (n, rays), 0)
    weights = tr[...]
    for b in range(entries):
        hit = near_valid[b] & (every == g + near_shift[b] - REACH)
        weights = jnp.where(hit, 0.0, weights)
    turned = weights.T
    w_rows = jnp.concatenate([turned[: rays // 2], turned[rays // 2 :]], axis=1)
    w_send[...] = w_rows.reshape(w_send.shape)

    pl.semaphore_wait(row_sem, len(row_peers))

    def send_weights(k):
        remote(
            w_send.at[k], w_recv.at[chunk], w_sems.at[0], w_sems.at[1], first_target + k, r
        ).start()

    each_target(send_weights, False)
    w_recv[chunk] = w_send[chunk]
    rad_copies = ray_copies(
        lambda d: rad_hbm.at[pl.ds(pl.multiple_of(other_ray(d) * rays, rays), rays), :],
        rad_full.at[:, mine],
        1,
    )
    near_rays = sorted({1 % m, m - 1} - {0})
    half = rays // 2

    def columns_of(ray):
        return pl.ds(pl.multiple_of(ray * width, width), width)

    def rows_of(ray, k):
        return pl.ds(pl.multiple_of(ray * rays + k * half, half), half)

    def ring_copies(part_of, index):
        copies = []
        for k, d in enumerate(near_rays):
            src, dst = part_of(d, k)
            copies.append(
                remote(src, dst, x_send.at[index, d - 1], x_recv.at[index, d - 1], g, other_ray(d))
            )
        return copies

    def inv_part(d, k):
        part = inv_full.at[pl.ds(k * (size // 2), size // 2), columns_of(other_ray(m - d))]
        return part, part

    def rec_part(d, k):
        part = rec_full.at[rows_of(other_ray(m - d), k), :]
        return part, part

    inv_copies = ring_copies(lambda d, k: (inv_hbm, inv_full.at[:, mine]), 2)
    inv_passed = ring_copies(inv_part, 3) if m == 4 else []
    rec_copies = [
        ring_copies(
            lambda d, k: (rec_hbm.at[pl.ds(k * half, half), :], rec_full.at[rows_of(r, k), :]), 4
        ),
        ring_copies(
            lambda d, k: (
                rec_hbm.at[pl.ds((1 - k) * half, half), :],
                rec_full.at[rows_of(r, 1 - k), :],
            ),
            5,
        ),
    ]
    rec_passed = ring_copies(rec_part, 6) if m == 4 else []
    p_copies = []

    def send_slab(step, wide):
        for k in range(chunks):
            s_send[step, k] = wide[k * rows : (k + 1) * rows].astype(BF16)

        def send(group, k):
            remote(
                s_send.at[step, k],
                s_recv.at[step, g],
                s_sems.at[step, 0],
                s_sems.at[step, 1],
                group,
                r,
            ).start()

        each_peer(send)
        s_recv[step, g] = s_send[step, chunk]

    def fold(step):
        wait_blocks(s_recv.at[step], s_sems.at[step, 1])
        for h in range(n):
            turn_s[h * rows : (h + 1) * rows] = s_recv[step, h].astype(F32)
        lane = lax.broadcasted_iota(jnp.int32, (n, 2 * waves), 1)
        for i in range(rows):
            slab = turn_s[pl.ds(i, n, stride=rows), :]
            wide = jnp.concatenate(
                [jnp.where(lane < waves, slab, 0.0), jnp.where(lane < waves, 0.0, slab)], axis=0
            ).astype(BF16)
            both = jnp.dot(w_both[i], wide, preferred_element_type=F32)
            turn_f[i * chunks : (i + 1) * chunks] = both[:chunks] + both[chunks:]
        for k in range(chunks):
            f_send[step, k] = turn_f[pl.ds(k, rows, stride=chunks), :].astype(BF16)
        place = r * chunks + chunk

        def send(k, ray):
            remote(
                f_send.at[step, k],
                f_recv.at[step, place],
                f_sems.at[step, 0],
                f_sems.at[step, 1],
                first_target + k,
                ray,
            ).start()

        if step and m > 1:

            def body(k, carry):
                d = jnp.where(k == 0, m // 2, jnp.where(k == 1, 1, m - 1))
                ray = wrap(r + d, m)
                each_target(lambda k: send(k, ray), True)
                return carry

            lax.fori_loop(0, m - 1, body, 0)
        each_target(lambda k: send(k, r), False)
        f_recv[step, place] = f_send[step, chunk]

    def send_partial(step, part):
        p_send[step] = part
        copies = [
            remote(
                p_send.at[step],
                p_recv.at[step, r],
                p_sems.at[step, 0, d - 1],
                p_sems.at[step, 1, d - 1],
                g,
                other_ray(d),
            )
            for d in ray_order
        ]
        for copy in copies:
            copy.start()
        p_copies.append(copies)
        p_recv[step, r] = part

    for copy in slab_copies:
        copy.wait_recv()
    first_slab = rs_recv[0].astype(F32)
    for k in range(1, m):
        first_slab = first_slab + rs_recv[k].astype(F32)
    send_slab(0, first_slab)
    for copy in cycle_copies + inv_copies + rad_copies:
        copy.start()

    wait_blocks(w_recv, w_sems.at[1])
    for i in range(rows):
        w_all = w_recv[:, i, :]
        w_high = w_all.astype(BF16)
        w_both[i, :chunks] = w_high
        w_both[i, chunks:] = (w_all - w_high.astype(F32)).astype(BF16)
    fold(0)

    load_self.wait()
    load_blocks.wait()
    load_exc.wait()
    for copy in cycle_copies:
        copy.wait_recv()
    base[...] = jnp.zeros_like(base)
    for step in range(steps):
        base[step, :, mine] = exc[step].astype(F32)

    def add_cycle(b, first, last):
        shift = list_ref[0, b]
        source = g + shift - REACH
        valid = (b < count_ref[0]) & (source >= 0) & (source < n)
        past = [
            nearby[shift, lax.rem(start_slot - i + slots, slots)] for i in range(slots - first)
        ]
        past = [jnp.where(valid, x, jnp.zeros_like(x)) for x in past]
        blank = jnp.zeros_like(past[0])
        lagged = jnp.concatenate(
            [
                jnp.concatenate([blank] * k + past[: len(past) - k], axis=1)
                for k in range(last - first)
            ],
            axis=0,
        )
        near = jnp.dot(
            lagged,
            blocks[b, first:].reshape((slots - first) * width, size),
            preferred_element_type=F32,
        )
        for k in range(last - first):
            base[first + k] = base[first + k] - near[k * waves : (k + 1) * waves]

    def add_first(b, carry):
        add_cycle(b, 0, 1)
        return carry

    def add_later(b, carry):
        add_cycle(b, 1, steps)
        return carry

    lax.fori_loop(0, entries, add_first, 0)
    for copy in inv_copies:
        copy.wait_recv()
    for copy in inv_passed:
        copy.start()

    def gathered_sum(step):
        for copy in p_copies[step]:
            copy.wait_recv()
        total = p_recv[step, 0].astype(F32)
        for d in range(1, m):
            total = total + p_recv[step, d].astype(F32)
        return total

    def turn_field(pieces):
        turned = jnp.concatenate([x.astype(F32) for x in pieces], axis=0).T.astype(BF16)
        span = rays // 2
        return jnp.concatenate(
            [
                turned[p * waves : (p + 1) * waves, k * span : (k + 1) * span]
                for k in range(len(pieces) // chunks)
                for p in range(2)
            ],
            axis=1,
        )

    for step in range(steps):
        more = step + 1 < steps
        if step == 0:
            load_rec.wait()
            wait_blocks(f_recv.at[0], f_sems.at[0, 1], chunks - 1)
            field = turn_field([f_recv[0, r * chunks + k] for k in range(chunks)])
            far = jnp.dot(field, rec_full[rows_here, :], preferred_element_type=F32)
            send_partial(0, (base[0] - far).astype(BF16))
            for copy in rec_copies[0]:
                copy.start()
            load_rad.wait()
            load_inv.wait()
            load_own_inv.wait()
            for copy in rad_copies + inv_passed:
                copy.wait_recv()
            slab_of_drive[...] = lax.dot_general(
                rad_full[...], inv_full[...], dims, preferred_element_type=F32
            ).astype(BF16)
            lax.fori_loop(0, entries, add_later, 0)
            drive = gathered_sum(0).astype(BF16)
            current = jnp.dot(drive, inv[...], preferred_element_type=F32).astype(BF16)
            slab = lax.dot_general(slab_of_drive[...], drive, dims, preferred_element_type=F32)
        else:
            if step == 1:
                for copy in rec_copies[1] + rec_passed:
                    copy.wait_recv()
                current_of_field[...] = jnp.dot(
                    rec_full[...], inv[...], preferred_element_type=F32
                ).astype(BF16)
                slab_of_field[...] = lax.dot_general(
                    slab_of_drive[...], rec_full[...], dims, preferred_element_type=F32
                ).astype(BF16)
            known = gathered_sum(step).astype(BF16)
            current = jnp.dot(known, inv[...], preferred_element_type=F32)
            if more:
                slab = lax.dot_general(slab_of_drive[...], known, dims, preferred_element_type=F32)
            wait_blocks(f_recv.at[step], f_sems.at[step, 1])
            field = turn_field([f_recv[step, k] for k in range(m * chunks)])
            current = (
                current - jnp.dot(field, current_of_field[...], preferred_element_type=F32)
            ).astype(BF16)
            if more:
                slab = slab - lax.dot_general(
                    slab_of_field[...], field, dims, preferred_element_type=F32
                )
        if more:
            wide = jnp.concatenate([slab[: rays // 2], slab[rays // 2 :]], axis=1)
        own[step] = current
        if step + 1 < steps:
            fresh = fresh_of[step]
            copies = near_copies(own.at[step], fresh, step + 1)
            for copy in copies:
                copy.start()
            near_all.extend(copies)
            send_slab(step + 1, wide)
            if step == 0:
                for copy in rec_copies[0]:
                    copy.wait_recv()
                for copy in rec_passed + rec_copies[1]:
                    copy.start()
            fresh[REACH] = current
        out_ref[step] = current
        if step + 1 < steps:
            for copy in copies:
                copy.wait_recv()

            def add_near(later):
                latest = [fresh[near_shift[b]] for b in range(entries)]
                latest = [
                    jnp.where(near_valid[b], x, jnp.zeros_like(x)) for b, x in enumerate(latest)
                ]
                base[later] = base[later] - jnp.dot(
                    jnp.concatenate(latest, axis=1),
                    blocks[:, later - step - 1].reshape(entries * width, size),
                    preferred_element_type=F32,
                )

            add_near(step + 1)
            send_partial(step + 1, base[step + 1].astype(BF16))
            fold(step + 1)
            for later in range(step + 2, steps):
                add_near(later)

    ringed = inv_copies + inv_passed + sum(rec_copies, rec_passed)
    for copy in slab_copies + rad_copies + ringed + near_all + sum(p_copies, []):
        copy.wait_send()
    wait_blocks(w_send, w_sems.at[0])
    for step in range(steps):
        wait_blocks(s_recv.at[step], s_sems.at[step, 0])
        wait_blocks(f_recv.at[step], f_sems.at[step, 0], None if step else chunks - 1)


def layout_of(n):
    inner = 1
    while inner * inner < n:
        inner *= 2
    return inner, max(n // (2 * inner), 1)


def solution(mesh):
    n = mesh.shape["groups"]
    m = mesh.shape["rays"]
    inner, copies_of_fold = layout_of(n)
    chunks = n // copies_of_fold

    def local(
        excitation,
        cycle,
        near_blocks,
        near_list,
        near_count,
        newest,
        inverse,
        radiate,
        translate,
        receive,
    ):
        steps, waves, width = excitation.shape
        slots = cycle.shape[0]
        entries = near_list.shape[1]
        size = m * width
        rays = receive.shape[0]
        rows = rays // (2 * chunks)
        spread = 2 * REACH + 1
        anywhere = pl.BlockSpec(memory_space=pl.ANY)
        dma = pltpu.SemaphoreType.DMA
        vmem = pltpu.VMEM
        smem = pltpu.SMEM
        return pl.pallas_call(
            functools.partial(kernel, n, inner, copies_of_fold, m),
            out_shape=pltpu.VMEM(excitation.shape, BF16),
            in_specs=[anywhere] * 10,
            out_specs=pl.BlockSpec(memory_space=vmem),
            scratch_shapes=[
                smem(near_list.shape, jnp.int32),
                smem(near_count.shape, jnp.int32),
                smem(newest.shape, jnp.int32),
                vmem(excitation.shape, BF16),
                vmem(cycle.shape, BF16),
                vmem((entries, slots, width, size), BF16),
                vmem((n, rays), F32),
                vmem(radiate.shape, BF16),
                vmem(inverse.shape, BF16),
                vmem((m, rays // 2, 2 * waves), BF16),
                vmem((m, rays // 2, 2 * waves), BF16),
                vmem((rays, size), BF16),
                vmem((size, size), BF16),
                vmem((rays, size), BF16),
                vmem((m * rays, size), BF16),
                vmem((rays, m * rays), BF16),
                vmem((m * rays, width), BF16),
                vmem((spread, slots, waves, width), BF16),
                vmem((spread, waves, width), BF16),
                vmem((spread, waves, width), BF16),
                vmem((chunks, rows, 2 * n), F32),
                vmem((chunks, rows, 2 * n), F32),
                vmem((rows, 2 * chunks, 2 * n), BF16),
                vmem((n * rows, 2 * waves), F32),
                vmem((chunks * rows, 2 * waves), F32),
                vmem((steps, chunks, rows, 2 * waves), BF16),
                vmem((steps, n, rows, 2 * waves), BF16),
                vmem((steps, chunks, rows, 2 * waves), BF16),
                vmem((steps, m * chunks, rows, 2 * waves), BF16),
                vmem((steps, waves, size), F32),
                vmem((steps, waves, size), BF16),
                vmem((steps, m, waves, size), BF16),
                vmem((steps, waves, width), BF16),
                pltpu.SemaphoreType.REGULAR,
                dma((13,)),
                dma((7, m - 1)),
                dma((7, m - 1)),
                dma((2,)),
                dma((steps, 2)),
                dma((steps, 2)),
                dma((steps, 4)),
                dma((steps, 4)),
                dma((steps, 2, m - 1)),
            ],
            compiler_params=pltpu.CompilerParams(
                collective_id=0, has_side_effects=True, vmem_limit_bytes=56 * 1024 * 1024
            ),
        )(
            excitation,
            cycle,
            near_blocks,
            near_list,
            near_count,
            newest,
            inverse,
            radiate,
            translate,
            receive,
        )

    placed = (
        P(None, None, ("groups", "rays")),
        P(None, None, ("groups", "rays")),
        P("groups", None, None, "rays", None),
        P("groups", None),
        P("groups"),
        P(),
        P(None, ("groups", "rays")),
        P(None, ("groups", "rays")),
        P("groups", None, "rays"),
        P("rays", "groups"),
    )
    return jax.shard_map(
        local,
        mesh=mesh,
        in_specs=placed,
        out_specs=P(None, None, ("groups", "rays")),
        check_vma=False,
    )
```

```python
import functools

import jax
import jax.numpy as jnp
from jax import lax
from jax.experimental import pallas as pl
from jax.experimental.pallas import tpu as pltpu
from jax.sharding import PartitionSpec as P

REACH = 2
NEAR_SHIFTS = (-2, -1, 1, 2)
MESH = pl.DeviceIdType.MESH
F32 = jnp.float32
BF16 = jnp.bfloat16


def kernel(
    n,
    inner,
    copies_of_fold,
    m,
    exc_hbm,
    cyc_hbm,
    blocks_hbm,
    list_hbm,
    count_hbm,
    newest_hbm,
    inv_hbm,
    rad_hbm,
    tr_hbm,
    rec_hbm,
    out_ref,
    list_ref,
    count_ref,
    newest_ref,
    exc,
    cyc,
    blocks,
    tr,
    rad,
    inv,
    rs_send,
    rs_recv,
    rad_full,
    inv_full,
    slab_of_drive,
    rec_full,
    slab_of_field,
    current_of_field,
    nearby,
    fresh_first,
    fresh_second,
    w_send,
    w_recv,
    w_both,
    turn_s,
    turn_f,
    s_send,
    s_recv,
    f_send,
    f_recv,
    base,
    p_send,
    p_recv,
    own,
    row_sem,
    load_sems,
    x_send,
    x_recv,
    w_sems,
    s_sems,
    f_sems,
    near_send,
    near_recv,
    p_sems,
):
    steps, waves, width = exc.shape
    slots = cyc.shape[0]
    entries = list_ref.shape[1]
    size = m * width
    rays = tr.shape[1]
    outer = n // inner
    chunks = n // copies_of_fold
    rows = rays // (2 * chunks)
    g = lax.axis_index("groups")
    r = lax.axis_index("rays")
    go = g // inner
    gi = g - go * inner
    pair = go // 2
    plane = go - 2 * pair
    chunk = plane * inner + gi
    first_target = g - chunk
    mine = pl.ds(pl.multiple_of(r * width, width), width)
    dims = (((1,), (1,)), ((), ()))
    fresh_of = (fresh_first, fresh_second)
    ray_order = sorted(range(1, m), key=lambda d: -min(d, m - d))
    inner_order = sorted(range(inner), key=lambda d: -min(d, inner - d))

    def wrap(x, limit):
        return jnp.where(x >= limit, x - limit, x)

    inner_place = [wrap(gi + d, inner) for d in range(inner)]
    ray_place = [wrap(r + d, m) for d in range(m)]

    def near_group(d):
        return wrap(g + d + n, n) if d < 0 else wrap(g + d, n)

    def other_ray(d):
        return ray_place[d]

    def remote(src, dst, send_sem, recv_sem, group, ray):
        return pltpu.make_async_remote_copy(
            src_ref=src,
            dst_ref=dst,
            send_sem=send_sem,
            recv_sem=recv_sem,
            device_id=(group, ray),
            device_id_type=MESH,
        )

    def each_peer(act):
        def body(k, carry):
            shift, change = carry
            place = wrap(go + shift, outer)
            other = place * inner
            bit = place - 2 * (place // 2)
            for d in inner_order:
                act(other + inner_place[d], bit * inner + inner_place[d])
            return shift + change, jnp.where(change < 0, 1 - change, -1 - change)

        lax.fori_loop(0, outer - 1, body, (jnp.int32(outer // 2), jnp.int32(-1)))
        for d in inner_order:
            if d:
                act(go * inner + inner_place[d], plane * inner + inner_place[d])

    def each_target(act, with_self):
        for d in inner_order:
            act((1 - plane) * inner + inner_place[d])
        for d in inner_order:
            if d or with_self:
                act(plane * inner + inner_place[d])

    def wait_blocks(like, sem, count=None):
        part = like.at[pl.ds(0, like.shape[0] - 1 if count is None else count)]
        pltpu.make_async_copy(part, part, sem).wait()

    def near_copies(src, dst, index):
        return [
            remote(
                src,
                dst.at[REACH - shift],
                near_send.at[index, k],
                near_recv.at[index, k],
                near_group(shift),
                r,
            )
            for k, shift in enumerate(NEAR_SHIFTS)
        ]

    def ray_copies(src_of, dst, index):
        return [
            remote(
                src_of(d), dst, x_send.at[index, d - 1], x_recv.at[index, d - 1], g, other_ray(d)
            )
            for d in ray_order
        ]

    rows_here = pl.ds(pl.multiple_of(r * rays, rays), rays)
    pairs = (
        (newest_hbm, newest_ref),
        (cyc_hbm, cyc),
        (rad_hbm, rad),
        (list_hbm, list_ref),
        (count_hbm, count_ref),
        (tr_hbm.at[0], tr),
        (rad_hbm.at[rows_here, :], rad_full.at[:, mine]),
        (blocks_hbm.at[0], blocks),
        (inv_hbm, inv_full.at[:, mine]),
        (inv_hbm, inv),
        (cyc_hbm, nearby.at[REACH]),
        (rec_hbm, rec_full.at[rows_here, :]),
        (exc_hbm, exc),
    )
    loads = [
        pltpu.make_async_copy(src, dst, load_sems.at[i]) for i, (src, dst) in enumerate(pairs)
    ]
    for load in loads[:3]:
        load.start()

    barrier = pltpu.get_barrier_semaphore()
    greeted = [(g, other_ray(d)) for d in ray_order]
    greeted += [(go * inner + inner_place[d], r) for d in inner_order if d]
    row_peers = [(wrap(go + d, outer) * inner + gi, r) for d in range(1, outer)]
    greeted += row_peers
    greeted += [(near_group(d), r) for d in NEAR_SHIFTS]
    for device in greeted:
        pl.semaphore_signal(barrier, inc=1, device_id=device, device_id_type=MESH)

    for load in loads[3:]:
        load.start(priority=1)
    (
        load_newest,
        load_cyc,
        load_all_rad,
        load_list,
        load_count,
        load_tr,
        load_rad,
        load_blocks,
        load_inv,
        load_own_inv,
        load_self,
        load_rec,
        load_exc,
    ) = loads

    load_newest.wait()
    load_cyc.wait()
    start_slot = newest_ref[0]
    newest_value = cyc[start_slot]
    load_all_rad.wait()
    for d in ray_order + [0]:
        ray = other_ray(d)
        block = rad[pl.ds(pl.multiple_of(ray * rays, rays), rays), :]
        block = lax.dot_general(block, newest_value, dims, preferred_element_type=F32)
        block = jnp.concatenate([block[: rays // 2], block[rays // 2 :]], axis=1).astype(BF16)
        if d:
            rs_send[ray] = block
        else:
            rs_recv[r] = block

    pl.semaphore_wait(barrier, len(greeted))

    slab_copies = ray_copies(lambda d: rs_send.at[other_ray(d)], rs_recv.at[r], 0)
    for copy in slab_copies:
        copy.start()
    for device in row_peers:
        pl.semaphore_signal(row_sem, inc=1, device_id=device, device_id_type=MESH)
    cycle_copies = near_copies(cyc_hbm, nearby, 0)
    near_all = list(cycle_copies)

    load_list.wait()
    load_count.wait()
    near_shift = []
    near_valid = []
    for b in range(entries):
        shift = list_ref[0, b]
        source = g + shift - REACH
        near_shift.append(shift)
        near_valid.append((b < count_ref[0]) & (source >= 0) & (source < n))
    load_tr.wait()
    every = lax.broadcasted_iota(jnp.int32, (n, rays), 0)
    weights = tr[...]
    for b in range(entries):
        hit = near_valid[b] & (every == g + near_shift[b] - REACH)
        weights = jnp.where(hit, 0.0, weights)
    turned = weights.T
    w_rows = jnp.concatenate([turned[: rays // 2], turned[rays // 2 :]], axis=1)
    w_send[...] = w_rows.reshape(w_send.shape)

    pl.semaphore_wait(row_sem, len(row_peers))

    def send_weights(k):
        remote(
            w_send.at[k], w_recv.at[chunk], w_sems.at[0], w_sems.at[1], first_target + k, r
        ).start()

    each_target(send_weights, False)
    w_recv[chunk] = w_send[chunk]
    rad_copies = ray_copies(
        lambda d: rad_hbm.at[pl.ds(pl.multiple_of(other_ray(d) * rays, rays), rays), :],
        rad_full.at[:, mine],
        1,
    )
    near_rays = sorted({1 % m, m - 1} - {0})
    half = rays // 2

    def columns_of(ray):
        return pl.ds(pl.multiple_of(ray * width, width), width)

    def rows_of(ray, k):
        return pl.ds(pl.multiple_of(ray * rays + k * half, half), half)

    def ring_copies(part_of, index):
        copies = []
        for k, d in enumerate(near_rays):
            src, dst = part_of(d, k)
            copies.append(
                remote(src, dst, x_send.at[index, d - 1], x_recv.at[index, d - 1], g, other_ray(d))
            )
        return copies

    def inv_part(d, k):
        part = inv_full.at[pl.ds(k * (size // 2), size // 2), columns_of(other_ray(m - d))]
        return part, part

    def rec_part(d, k):
        part = rec_full.at[rows_of(other_ray(m - d), k), :]
        return part, part

    inv_copies = ring_copies(lambda d, k: (inv_hbm, inv_full.at[:, mine]), 2)
    inv_passed = ring_copies(inv_part, 3) if m == 4 else []
    rec_copies = [
        ring_copies(
            lambda d, k: (rec_hbm.at[pl.ds(k * half, half), :], rec_full.at[rows_of(r, k), :]), 4
        ),
        ring_copies(
            lambda d, k: (
                rec_hbm.at[pl.ds((1 - k) * half, half), :],
                rec_full.at[rows_of(r, 1 - k), :],
            ),
            5,
        ),
    ]
    rec_passed = ring_copies(rec_part, 6) if m == 4 else []
    p_copies = []

    def send_slab(step, wide):
        for k in range(chunks):
            s_send[step, k] = wide[k * rows : (k + 1) * rows].astype(BF16)

        def send(group, k):
            remote(
                s_send.at[step, k],
                s_recv.at[step, g],
                s_sems.at[step, 0],
                s_sems.at[step, 1],
                group,
                r,
            ).start()

        each_peer(send)
        s_recv[step, g] = s_send[step, chunk]

    def fold(step):
        wait_blocks(s_recv.at[step], s_sems.at[step, 1])
        for h in range(n):
            turn_s[h * rows : (h + 1) * rows] = s_recv[step, h].astype(F32)
        lane = lax.broadcasted_iota(jnp.int32, (n, 2 * waves), 1)
        for i in range(rows):
            slab = turn_s[pl.ds(i, n, stride=rows), :]
            wide = jnp.concatenate(
                [jnp.where(lane < waves, slab, 0.0), jnp.where(lane < waves, 0.0, slab)], axis=0
            ).astype(BF16)
            both = jnp.dot(w_both[i], wide, preferred_element_type=F32)
            turn_f[i * chunks : (i + 1) * chunks] = both[:chunks] + both[chunks:]
        for k in range(chunks):
            f_send[step, k] = turn_f[pl.ds(k, rows, stride=chunks), :].astype(BF16)
        place = r * chunks + chunk

        def send(k, ray):
            remote(
                f_send.at[step, k],
                f_recv.at[step, place],
                f_sems.at[step, 0],
                f_sems.at[step, 1],
                first_target + k,
                ray,
            ).start()

        if step and m > 1:

            def body(k, carry):
                d = jnp.where(k == 0, m // 2, jnp.where(k == 1, 1, m - 1))
                ray = wrap(r + d, m)
                each_target(lambda k: send(k, ray), True)
                return carry

            lax.fori_loop(0, m - 1, body, 0)
        each_target(lambda k: send(k, r), False)
        f_recv[step, place] = f_send[step, chunk]

    def send_partial(step, part):
        p_send[step] = part
        copies = [
            remote(
                p_send.at[step],
                p_recv.at[step, r],
                p_sems.at[step, 0, d - 1],
                p_sems.at[step, 1, d - 1],
                g,
                other_ray(d),
            )
            for d in ray_order
        ]
        for copy in copies:
            copy.start()
        p_copies.append(copies)
        p_recv[step, r] = part

    for copy in slab_copies:
        copy.wait_recv()
    first_slab = rs_recv[0].astype(F32)
    for k in range(1, m):
        first_slab = first_slab + rs_recv[k].astype(F32)
    send_slab(0, first_slab)
    for copy in cycle_copies + inv_copies + rad_copies:
        copy.start()

    wait_blocks(w_recv, w_sems.at[1])
    for i in range(rows):
        w_all = w_recv[:, i, :]
        w_high = w_all.astype(BF16)
        w_both[i, :chunks] = w_high
        w_both[i, chunks:] = (w_all - w_high.astype(F32)).astype(BF16)
    fold(0)
    for copy in inv_copies:
        copy.wait_recv()
    for copy in inv_passed:
        copy.start()

    load_self.wait()
    load_blocks.wait()
    load_exc.wait()
    for copy in cycle_copies:
        copy.wait_recv()
    base[...] = jnp.zeros_like(base)
    for step in range(steps):
        base[step, :, mine] = exc[step].astype(F32)

    def add_cycle(b, carry):
        shift = list_ref[0, b]
        source = g + shift - REACH
        valid = (b < count_ref[0]) & (source >= 0) & (source < n)
        past = [nearby[shift, lax.rem(start_slot - i + slots, slots)] for i in range(slots)]
        past = [jnp.where(valid, x, jnp.zeros_like(x)) for x in past]
        blank = jnp.zeros_like(past[0])
        lagged = jnp.concatenate(
            [
                jnp.concatenate([blank] * step + past[: slots - step], axis=1)
                for step in range(steps)
            ],
            axis=0,
        )
        near = jnp.dot(
            lagged, blocks[b].reshape(slots * width, size), preferred_element_type=F32
        )
        for step in range(steps):
            base[step] = base[step] - near[step * waves : (step + 1) * waves]
        return carry


    lax.fori_loop(0, entries, add_cycle, 0)

    def gathered_sum(step):
        for copy in p_copies[step]:
            copy.wait_recv()
        total = p_recv[step, 0].astype(F32)
        for d in range(1, m):
            total = total + p_recv[step, d].astype(F32)
        return total

    def turn_field(pieces):
        turned = jnp.concatenate([x.astype(F32) for x in pieces], axis=0).T.astype(BF16)
        span = rays // 2
        return jnp.concatenate(
            [
                turned[p * waves : (p + 1) * waves, k * span : (k + 1) * span]
                for k in range(len(pieces) // chunks)
                for p in range(2)
            ],
            axis=1,
        )

    for step in range(steps):
        more = step + 1 < steps
        if step == 0:
            load_rec.wait()
            wait_blocks(f_recv.at[0], f_sems.at[0, 1], chunks - 1)
            field = turn_field([f_recv[0, r * chunks + k] for k in range(chunks)])
            far = jnp.dot(field, rec_full[rows_here, :], preferred_element_type=F32)
            send_partial(0, (base[0] - far).astype(BF16))
            for copy in rec_copies[0]:
                copy.start()
            load_rad.wait()
            load_inv.wait()
            load_own_inv.wait()
            for copy in rad_copies + inv_passed:
                copy.wait_recv()
            slab_of_drive[...] = lax.dot_general(
                rad_full[...], inv_full[...], dims, preferred_element_type=F32
            ).astype(BF16)
            drive = gathered_sum(0).astype(BF16)
            current = jnp.dot(drive, inv[...], preferred_element_type=F32).astype(BF16)
            slab = lax.dot_general(slab_of_drive[...], drive, dims, preferred_element_type=F32)
        else:
            if step == 1:
                for copy in rec_copies[1] + rec_passed:
                    copy.wait_recv()
                current_of_field[...] = jnp.dot(
                    rec_full[...], inv[...], preferred_element_type=F32
                ).astype(BF16)
                slab_of_field[...] = lax.dot_general(
                    slab_of_drive[...], rec_full[...], dims, preferred_element_type=F32
                ).astype(BF16)
            known = gathered_sum(step).astype(BF16)
            current = jnp.dot(known, inv[...], preferred_element_type=F32)
            if more:
                slab = lax.dot_general(slab_of_drive[...], known, dims, preferred_element_type=F32)
            wait_blocks(f_recv.at[step], f_sems.at[step, 1])
            field = turn_field([f_recv[step, k] for k in range(m * chunks)])
            current = (
                current - jnp.dot(field, current_of_field[...], preferred_element_type=F32)
            ).astype(BF16)
            if more:
                slab = slab - lax.dot_general(
                    slab_of_field[...], field, dims, preferred_element_type=F32
                )
        if more:
            wide = jnp.concatenate([slab[: rays // 2], slab[rays // 2 :]], axis=1)
        own[step] = current
        if step + 1 < steps:
            fresh = fresh_of[step]
            copies = near_copies(own.at[step], fresh, step + 1)
            for copy in copies:
                copy.start()
            near_all.extend(copies)
            send_slab(step + 1, wide)
            if step == 0:
                for copy in rec_copies[0]:
                    copy.wait_recv()
                for copy in rec_passed + rec_copies[1]:
                    copy.start()
            fresh[REACH] = current
        out_ref[step] = current
        if step + 1 < steps:
            for copy in copies:
                copy.wait_recv()

            def add_near(later):
                latest = [fresh[near_shift[b]] for b in range(entries)]
                latest = [
                    jnp.where(near_valid[b], x, jnp.zeros_like(x)) for b, x in enumerate(latest)
                ]
                base[later] = base[later] - jnp.dot(
                    jnp.concatenate(latest, axis=1),
                    blocks[:, later - step - 1].reshape(entries * width, size),
                    preferred_element_type=F32,
                )

            add_near(step + 1)
            send_partial(step + 1, base[step + 1].astype(BF16))
            fold(step + 1)
            for later in range(step + 2, steps):
                add_near(later)

    ringed = inv_copies + inv_passed + sum(rec_copies, rec_passed)
    for copy in slab_copies + rad_copies + ringed + near_all + sum(p_copies, []):
        copy.wait_send()
    wait_blocks(w_send, w_sems.at[0])
    for step in range(steps):
        wait_blocks(s_recv.at[step], s_sems.at[step, 0])
        wait_blocks(f_recv.at[step], f_sems.at[step, 0], None if step else chunks - 1)


def layout_of(n):
    inner = 1
    while inner * inner < n:
        inner *= 2
    return inner, max(n // (2 * inner), 1)


def solution(mesh):
    n = mesh.shape["groups"]
    m = mesh.shape["rays"]
    inner, copies_of_fold = layout_of(n)
    chunks = n // copies_of_fold

    def local(
        excitation,
        cycle,
        near_blocks,
        near_list,
        near_count,
        newest,
        inverse,
        radiate,
        translate,
        receive,
    ):
        steps, waves, width = excitation.shape
        slots = cycle.shape[0]
        entries = near_list.shape[1]
        size = m * width
        rays = receive.shape[0]
        rows = rays // (2 * chunks)
        spread = 2 * REACH + 1
        anywhere = pl.BlockSpec(memory_space=pl.ANY)
        dma = pltpu.SemaphoreType.DMA
        vmem = pltpu.VMEM
        smem = pltpu.SMEM
        return pl.pallas_call(
            functools.partial(kernel, n, inner, copies_of_fold, m),
            out_shape=pltpu.VMEM(excitation.shape, BF16),
            in_specs=[anywhere] * 10,
            out_specs=pl.BlockSpec(memory_space=vmem),
            scratch_shapes=[
                smem(near_list.shape, jnp.int32),
                smem(near_count.shape, jnp.int32),
                smem(newest.shape, jnp.int32),
                vmem(excitation.shape, BF16),
                vmem(cycle.shape, BF16),
                vmem((entries, slots, width, size), BF16),
                vmem((n, rays), F32),
                vmem(radiate.shape, BF16),
                vmem(inverse.shape, BF16),
                vmem((m, rays // 2, 2 * waves), BF16),
                vmem((m, rays // 2, 2 * waves), BF16),
                vmem((rays, size), BF16),
                vmem((size, size), BF16),
                vmem((rays, size), BF16),
                vmem((m * rays, size), BF16),
                vmem((rays, m * rays), BF16),
                vmem((m * rays, width), BF16),
                vmem((spread, slots, waves, width), BF16),
                vmem((spread, waves, width), BF16),
                vmem((spread, waves, width), BF16),
                vmem((chunks, rows, 2 * n), F32),
                vmem((chunks, rows, 2 * n), F32),
                vmem((rows, 2 * chunks, 2 * n), BF16),
                vmem((n * rows, 2 * waves), F32),
                vmem((chunks * rows, 2 * waves), F32),
                vmem((steps, chunks, rows, 2 * waves), BF16),
                vmem((steps, n, rows, 2 * waves), BF16),
                vmem((steps, chunks, rows, 2 * waves), BF16),
                vmem((steps, m * chunks, rows, 2 * waves), BF16),
                vmem((steps, waves, size), F32),
                vmem((steps, waves, size), BF16),
                vmem((steps, m, waves, size), BF16),
                vmem((steps, waves, width), BF16),
                pltpu.SemaphoreType.REGULAR,
                dma((13,)),
                dma((7, m - 1)),
                dma((7, m - 1)),
                dma((2,)),
                dma((steps, 2)),
                dma((steps, 2)),
                dma((steps, 4)),
                dma((steps, 4)),
                dma((steps, 2, m - 1)),
            ],
            compiler_params=pltpu.CompilerParams(
                collective_id=0, has_side_effects=True, vmem_limit_bytes=56 * 1024 * 1024
            ),
        )(
            excitation,
            cycle,
            near_blocks,
            near_list,
            near_count,
            newest,
            inverse,
            radiate,
            translate,
            receive,
        )

    placed = (
        P(None, None, ("groups", "rays")),
        P(None, None, ("groups", "rays")),
        P("groups", None, None, "rays", None),
        P("groups", None),
        P("groups"),
        P(),
        P(None, ("groups", "rays")),
        P(None, ("groups", "rays")),
        P("groups", None, "rays"),
        P("rays", "groups"),
    )
    return jax.shard_map(
        local,
        mesh=mesh,
        in_specs=placed,
        out_specs=P(None, None, ("groups", "rays")),
        check_vma=False,
    )
```
